32 devices in a mesh: dp: 4 (over x, core), space: 8 (over z, y).
Axes of the slice: x: 2, y: 2, z: 4, core: 2. Of those that a mesh axis runs over, the one named last changes fastest.
Arguments:
- layer_input: bfloat16 [4, 64, 16, 1024], P('dp', None, 'space'), may hold values from -6 to 6
- hidden_pre: bfloat16 [4, 128, 16, 1024], P('dp', None, 'space'), may hold values from -6 to 6
- output_pre: bfloat16 [4, 256, 8, 256], P('dp', None, 'space'), may hold values from -6 to 6
- output_grad: bfloat16 [4, 256, 8, 256], P('dp', None, 'space'), may hold values from -48 to 48
- weight_a: bfloat16 [27, 64, 128], replicated, may hold values from -0.15625 to 0.15625
- weight_b: bfloat16 [27, 128, 256], replicated, may hold values from -0.109375 to 0.109375
Outputs:
- input_grad: bfloat16 [4, 64, 16, 1024], P('dp', None, 'space')
- weight_grad_a: float32 [27, 64, 128], replicated
- weight_grad_b: float32 [27, 128, 256], replicated
The draws below stay inside these ranges and needn't reach their ends.
All inputs are finite; a program needn't handle non-finite values.
Results may differ from the reference program's by a relative error of at most 0.013.
Values may be sent and summed in bfloat16 or wider, within the bound.
No kernel may reach another device: no remote copies, remote signals or barrier semaphores. Data moves between devices by JAX's collectives and lax.ppermute only.
A program may use at most 64 MiB of HBM per device.

```python
import jax
import jax.numpy as jnp
from jax import lax

CA = 64
KA = 128
KB = 256
GRID = 32
SAMPLES = 4
NZA = 16
NZB = 8


def steps_of(rng, dims, split, low, high):
    level, own = 1.0, jax.random.fold_in(rng, 6)
    for dim, shards_of in split:
        heights = jnp.exp(jax.random.uniform(jax.random.fold_in(own, dim), (shards_of,), jnp.float32, low / len(split), high / len(split)))
        level = level * jnp.repeat(heights, dims[dim] // shards_of).reshape([-1 if axis == dim else 1 for axis in range(len(dims))])
    return level


def noise(key, shape, scale, reach, shards=(), held_as=jnp.bfloat16):
    drawn = jax.random.normal(key, shape, jnp.float32) * scale
    if len(shards) > 0:
        drawn = steps_of(key, shape, shards, -0.22, 0.18) * drawn
    return jnp.clip(drawn, min=-reach, max=reach).astype(held_as)


def setup_inputs(seed: int = 0) -> dict:
    seeds = jax.random.split(jax.random.key(seed), 7)
    return {
        "layer_input": noise(seeds[0], (SAMPLES, CA, NZA, GRID * GRID), 1.0, 6.0, ((0, 4), (2, 8))),
        "hidden_pre": noise(seeds[1], (SAMPLES, KA, NZA, GRID * GRID), 1.0, 6.0, ((0, 4), (2, 8))),
        "output_pre": noise(seeds[2], (SAMPLES, KB, NZB, GRID * GRID // 4), 1.0, 6.0, ((0, 4), (2, 8))),
        "output_grad": noise(seeds[3], (SAMPLES, KB, NZB, GRID * GRID // 4), 8.0, 48.0, ((0, 4), (2, 8))),
        "weight_a": noise(seeds[4], (27, CA, KA), (27 * CA) ** -0.5, 0.15625),
        "weight_b": noise(seeds[5], (27, KA, KB), (27 * KA) ** -0.5, 0.109375),
    }


negative_slope = 0.3

def conv_layer(field, kernel):
    shaped = kernel.reshape(3, 3, 3, kernel.shape[1], kernel.shape[2])
    result = lax.conv_general_dilated(field[None], shaped, (1, 1, 1), ((1, 1), (1, 1), (1, 1)), dimension_numbers=('NCDHW', 'DHWIO', 'NCDHW'), precision=lax.Precision.HIGHEST)
    return result[0]

def slopes(values):
    return jnp.where(values > 0, jnp.ones_like(values), negative_slope * jnp.ones_like(values))

def reference(layer_input, hidden_pre, output_pre, output_grad, weight_a, weight_b):
    half = GRID // 2
    kernel_a = weight_a.astype(jnp.float32)
    kernel_b = weight_b.astype(jnp.float32)

    def one_sample(carry, items):
        source, hidden, outer, upstream = items
        outer_f = outer.astype(jnp.float32)
        grad_outer = (upstream.astype(jnp.float32) * slopes(outer_f)).astype(jnp.bfloat16)
        hidden_f = hidden.astype(jnp.float32)
        active = jnp.where(hidden_f > 0, hidden_f, negative_slope * hidden_f)
        pooled = active.reshape(KA, NZB, 2, half, 2, half, 2).mean(axis=(2, 4, 6)).astype(jnp.bfloat16)
        unused_b, pull_b = jax.vjp(conv_layer, pooled.astype(jnp.float32), kernel_b)
        back_b, term_b = pull_b(grad_outer.astype(jnp.float32).reshape(KB, NZB, half, half))
        spread = jnp.repeat(jnp.repeat(jnp.repeat(back_b, 2, 1), 2, 2), 2, 3) * 0.125
        grad_hidden = (spread * slopes(hidden_f.reshape(KA, NZA, GRID, GRID))).astype(jnp.bfloat16)
        field = source.astype(jnp.float32).reshape(CA, NZA, GRID, GRID)
        unused_a, pull_a = jax.vjp(conv_layer, field, kernel_a)
        back_a, term_a = pull_a(grad_hidden.astype(jnp.float32))
        carry = (carry[0] + term_a.reshape(27, CA, KA), carry[1] + term_b.reshape(27, KA, KB))
        return (carry, back_a.astype(jnp.bfloat16).reshape(CA, NZA, GRID * GRID))
    start = (jnp.zeros((27, CA, KA), jnp.float32), jnp.zeros((27, KA, KB), jnp.float32))
    totals, input_grad = lax.scan(one_sample, start, (layer_input, hidden_pre, output_pre, output_grad))
    scale_a = 1.0 / jnp.sqrt(jnp.float32(SAMPLES * NZA * GRID * GRID))
    scale_b = 1.0 / jnp.sqrt(jnp.float32(SAMPLES * NZB * half * half))
    return (input_grad, totals[0] * scale_a, totals[1] * scale_b)
```

```python
import math

import jax
import jax.numpy as jnp
from jax import lax
from jax.sharding import PartitionSpec as P

negative_slope = 0.3


def padded_2(cells, sides, width):
    for axis, dim in sides:
        count = lax.axis_size(axis)
        ends = count - 1
        head = lax.slice_in_dim(cells, 0, width, axis=dim)
        tail = lax.slice_in_dim(cells, cells.shape[dim] - width, cells.shape[dim], axis=dim)
        cells = jnp.concatenate(
            [
                lax.ppermute(tail, axis, [(i, (i + 1) % count) for i in range(ends)]),
                cells,
                lax.ppermute(head, axis, [((i + 1) % count, i) for i in range(ends)]),
            ],
            axis=dim,
        )
    return cells


def slopes(values):
    return jnp.where(values > 0, jnp.ones_like(values), negative_slope * jnp.ones_like(values))


def window(padded, tap_z, tap_y, tap_x, depth, side):
    planes = padded[:, tap_z : tap_z + depth, :]
    margin = side + 1
    wider = jnp.pad(planes, ((0, 0), (0, 0), (margin, margin)))
    offset = (tap_y - 1) * side + (tap_x - 1)
    piece = wider[:, :, margin + offset : margin + offset + side * side]
    column = jnp.arange(side * side, dtype=jnp.int32) % side + (tap_x - 1)
    inside = (column >= 0) & (column < side)
    piece = jnp.where(inside, piece, jnp.zeros_like(piece))
    return piece.reshape(padded.shape[0], depth * side * side)


def outer_product(left, right):
    return lax.dot_general(
        left, right, (((1,), (1,)), ((), ())), preferred_element_type=jnp.float32
    )


def per_device(layer_input, hidden_pre, output_pre, output_grad, weight_a, weight_b):
    side = math.isqrt(layer_input.shape[3])
    half = side // 2
    depth_a = layer_input.shape[2]
    depth_b = depth_a // 2
    source = layer_input[0]
    hidden = hidden_pre[0]
    outer = output_pre[0]
    upstream = output_grad[0]
    chan_in = source.shape[0]
    width_a = hidden.shape[0]
    width_b = outer.shape[0]
    grad_outer = (upstream.astype(jnp.float32) * slopes(outer.astype(jnp.float32))).astype(
        jnp.bfloat16
    )
    hidden_f = hidden.astype(jnp.float32)
    active = jnp.where(hidden_f > 0, hidden_f, negative_slope * hidden_f)
    pooled = (
        active.reshape(width_a, depth_b, 2, half, 2, half, 2)
        .mean(axis=(2, 4, 6))
        .astype(jnp.bfloat16)
    )
    pooled = pooled.reshape(width_a, depth_b, half * half)
    outer_pad = padded_2(grad_outer, (("space", 1),), 1)
    pooled_pad = padded_2(pooled, (("space", 1),), 1)
    grad_flat = grad_outer.reshape(width_b, depth_b * half * half)
    back_b = jnp.zeros((width_a, depth_b * half * half), jnp.float32)
    terms_b = []
    for tap in range(27):
        tap_z, tap_y, tap_x = (tap // 9, tap // 3 % 3, tap % 3)
        mirror = window(outer_pad, 2 - tap_z, 2 - tap_y, 2 - tap_x, depth_b, half)
        back_b = back_b + jnp.dot(weight_b[tap], mirror, preferred_element_type=jnp.float32)
        terms_b.append(
            outer_product(window(pooled_pad, tap_z, tap_y, tap_x, depth_b, half), grad_flat)
        )
    sums_b = jnp.stack(terms_b)
    total_b = lax.psum(sums_b.astype(jnp.bfloat16), ("dp", "space")).astype(jnp.float32)
    coarse = back_b.reshape(width_a, depth_b, half, half)
    upward = jnp.repeat(jnp.repeat(jnp.repeat(coarse, 2, 1), 2, 2), 2, 3) * 0.125
    upward = upward.reshape(width_a, depth_a * side * side)
    grad_hidden = (upward * slopes(hidden_f.reshape(width_a, depth_a * side * side))).astype(
        jnp.bfloat16
    )
    grad_hidden = grad_hidden.reshape(width_a, depth_a, side * side)
    hidden_pad = padded_2(grad_hidden, (("space", 1),), 1)
    source_pad = padded_2(source, (("space", 1),), 1)
    hidden_flat = grad_hidden.reshape(width_a, depth_a * side * side)
    back_a = jnp.zeros((chan_in, depth_a * side * side), jnp.float32)
    terms_a = []
    for tap in range(27):
        tap_z, tap_y, tap_x = (tap // 9, tap // 3 % 3, tap % 3)
        mirror = window(hidden_pad, 2 - tap_z, 2 - tap_y, 2 - tap_x, depth_a, side)
        back_a = back_a + jnp.dot(weight_a[tap], mirror, preferred_element_type=jnp.float32)
        terms_a.append(
            outer_product(window(source_pad, tap_z, tap_y, tap_x, depth_a, side), hidden_flat)
        )
    sums_a = jnp.stack(terms_a)
    input_grad = back_a.astype(jnp.bfloat16).reshape(1, chan_in, depth_a, side * side)
    total_a = lax.psum(sums_a.astype(jnp.bfloat16), ("dp", "space")).astype(jnp.float32)
    samples = lax.axis_size("dp")
    planes_a = depth_a * lax.axis_size("space")
    scale_a = 1.0 / math.sqrt(samples * planes_a * side * side)
    scale_b = 1.0 / math.sqrt(samples * (planes_a // 2) * half * half)
    return (input_grad, total_a * scale_a, total_b * scale_b)


def solution(mesh):
    in_specs = (
        P("dp", None, "space", None),
        P("dp", None, "space", None),
        P("dp", None, "space", None),
        P("dp", None, "space", None),
        P(),
        P(),
    )
    out_specs = (P("dp", None, "space", None), P(), P())
    return jax.shard_map(
        per_device, mesh=mesh, in_specs=in_specs, out_specs=out_specs, check_vma=False
    )
```

```python
import math

import jax
import jax.numpy as jnp
from jax import lax
from jax.experimental import pallas as pl
from jax.experimental.pallas import tpu as pltpu
from jax.sharding import PartitionSpec as P

negative_slope = 0.3
f32 = jnp.float32
bf16 = jnp.bfloat16
vmem = pl.BlockSpec(memory_space=pltpu.VMEM)
transposed = (((1,), (1,)), ((), ()))


def shifted(cells, rows, columns, side):
    size = side * side
    offset = rows * side + columns
    if offset:
        cells = pltpu.roll(cells, (-offset) % size, 1)
    place = lax.broadcasted_iota(jnp.int32, cells.shape, 1)
    if rows:
        y = place // side + rows
        cells = jnp.where((y >= 0) & (y < side), cells, 0.0)
    if columns:
        x = place % side + columns
        cells = jnp.where((x >= 0) & (x < side), cells, 0.0)
    return cells


def gathered(parts, side):
    total = None
    for c in range(3):
        line = parts(1, c) + shifted(parts(0, c), 1, 0, side) + shifted(parts(2, c), -1, 0, side)
        line = shifted(line, 0, 1 - c, side)
        total = line if total is None else total + line
    return total


def pool_matrix(side):
    half = side // 2
    fine = lax.broadcasted_iota(jnp.int32, (side * side, half * half), 0)
    coarse = lax.broadcasted_iota(jnp.int32, (side * side, half * half), 1)
    parent = (fine // (2 * side)) * half + (fine % side) // 2
    return jnp.where(parent == coarse, 0.125, 0.0).astype(bf16)


def call(kernel, out_shape, scratch, flops, *args):
    return pl.pallas_call(
        kernel,
        out_shape=out_shape,
        in_specs=[vmem] * len(args),
        out_specs=jax.tree.map(lambda _: vmem, out_shape),
        scratch_shapes=scratch,
        compiler_params=pltpu.CompilerParams(vmem_limit_bytes=48 * 1024 * 1024),
        cost_estimate=pl.CostEstimate(flops=flops, bytes_accessed=2 << 20, transcendentals=0),
    )(*args)


def first_kernel(side, hidden, grad, source, pooled, up, down):
    width = hidden.shape[1]
    pool = pool_matrix(side)
    total = None
    for plane in range(2):
        cells = hidden[plane].astype(f32)
        stacked = jnp.concatenate([jnp.maximum(cells, 0.0), jnp.minimum(cells, 0.0)], 0).astype(bf16)
        part = jnp.dot(stacked, pool, preferred_element_type=f32)
        total = part if total is None else total + part
    pooled[...] = (total[:width] + negative_slope * total[width:]).astype(bf16)
    rows, cols = grad.shape
    for out, plane in ((up, 1), (down, 0)):
        out[:rows] = grad[...]
        chan = source.shape[1]
        for piece in range(source.shape[2] // cols):
            out[rows + piece * chan : rows + (piece + 1) * chan] = source[
                plane, :, piece * cols : (piece + 1) * cols
            ]


def sums_b_kernel(half, pooled, grad, before, after, sums, moved):
    width = pooled.shape[0]
    rows = grad.shape[0]
    cells = pooled[...].astype(f32)
    for tap in range(9):
        moved[tap * width : (tap + 1) * width] = shifted(cells, tap // 3 - 1, tap % 3 - 1, half).astype(bf16)
    planes = (after[:rows], grad[...], before[:rows])
    for a in range(3):
        sums[a * 9 * width : (a + 1) * 9 * width] = lax.dot_general(
            moved[...], planes[a], transposed, preferred_element_type=f32
        ).astype(bf16)


def middle_kernel(side, weight, grad, before, after, hidden, source, sums, grad_hidden, products, moved):
    half = side // 2
    width = hidden.shape[1]
    rows = grad.shape[0]
    cols = grad.shape[1]
    chan = source.shape[1]
    size = side * side
    block = 9 * width
    products[...] = jnp.dot(weight[:block], after[:rows], preferred_element_type=f32)
    products[...] += jnp.dot(weight[block : 2 * block], grad[...], preferred_element_type=f32)
    products[...] += jnp.dot(weight[2 * block :], before[:rows], preferred_element_type=f32)

    def part(b, c):
        tap = 3 * b + c
        return products[tap * width : (tap + 1) * width]

    back = gathered(part, half)
    high = back.astype(bf16)
    low = (back - high.astype(f32)).astype(bf16)
    pool = pool_matrix(side)
    spread = lax.dot_general(high, pool, transposed, preferred_element_type=f32)
    spread += lax.dot_general(low, pool, transposed, preferred_element_type=f32)
    for plane in range(2):
        slope = jnp.where(hidden[plane].astype(f32) > 0, 1.0, negative_slope)
        grad_hidden[plane * width : (plane + 1) * width] = (spread * slope).astype(bf16)

    def plane_of(index):
        if index in (0, 1):
            return source[index]
        edge = before if index < 0 else after
        pieces = [edge[rows + k * chan : rows + (k + 1) * chan] for k in range(size // cols)]
        return jnp.concatenate(pieces, 1)

    for index in range(-1, 3):
        cells = plane_of(index).astype(f32)
        for tap in range(9):
            moved[index + 1, tap * chan : (tap + 1) * chan] = shifted(
                cells, tap // 3 - 1, tap % 3 - 1, side
            ).astype(bf16)
    both = grad_hidden[...]
    outer0 = lax.dot_general(moved[0], both[:width], transposed, preferred_element_type=f32)
    inner0 = lax.dot_general(moved[1], both, transposed, preferred_element_type=f32)
    inner1 = lax.dot_general(moved[2], both, transposed, preferred_element_type=f32)
    outer1 = lax.dot_general(moved[3], both[width:], transposed, preferred_element_type=f32)
    tall = 9 * chan
    sums[:tall] = (outer0 + inner0[:, width:]).astype(bf16)
    sums[tall : 2 * tall] = (inner0[:, :width] + inner1[:, width:]).astype(bf16)
    sums[2 * tall :] = (inner1[:, :width] + outer1).astype(bf16)


def input_kernel(side, weight, grad_hidden, own, to_before, to_after, products):
    width = weight.shape[1]
    tall = weight.shape[0] // 3
    chan = tall // 9
    both = grad_hidden[...]

    def part(b, c):
        tap = 3 * b + c
        return products[tap * chan : (tap + 1) * chan]

    products[...] = jnp.dot(weight[:tall], both[:width], preferred_element_type=f32)
    to_before[...] = gathered(part, side).astype(bf16)
    products[...] = jnp.dot(weight[2 * tall :], both[width:], preferred_element_type=f32)
    to_after[...] = gathered(part, side).astype(bf16)
    for plane in range(2):
        mixed = jnp.concatenate(
            [weight[(plane + 1) * tall : (plane + 2) * tall], weight[plane * tall : (plane + 1) * tall]], 1
        )
        products[...] = jnp.dot(mixed, both, preferred_element_type=f32)
        own[plane] = gathered(part, side)


def per_device(layer_input, hidden_pre, output_pre, output_grad, weight_a, weight_b):
    side = math.isqrt(layer_input.shape[3])
    half = side // 2
    size, small = side * side, half * half
    depth_a = layer_input.shape[2]
    source = layer_input[0].transpose(1, 0, 2)
    hidden = hidden_pre[0].transpose(1, 0, 2)
    chan = source.shape[1]
    width_a = hidden.shape[1]
    width_b = output_pre.shape[1]
    outer = output_pre[0, :, 0].astype(f32)
    grad = (output_grad[0, :, 0].astype(f32) * jnp.where(outer > 0, 1.0, negative_slope)).astype(bf16)
    shape = jax.ShapeDtypeStruct
    tall = width_b + chan * size // small
    pooled, up, down = call(
        lambda *refs: first_kernel(side, *refs),
        [shape((width_a, small), bf16), shape((tall, small), bf16), shape((tall, small), bf16)],
        [],
        1 << 28,
        hidden,
        grad,
        source,
    )
    slabs = lax.axis_size("space")
    upward = [(i, i + 1) for i in range(slabs - 1)]
    downward = [(i + 1, i) for i in range(slabs - 1)]
    before = lax.ppermute(up, "space", upward)
    after = lax.ppermute(down, "space", downward)
    sums_b = call(
        lambda *refs: sums_b_kernel(half, *refs),
        shape((27 * width_a, width_b), bf16),
        [pltpu.VMEM((9 * width_a, small), bf16)],
        1 << 29,
        pooled,
        grad,
        before,
        after,
    )
    sums_a, grad_hidden = call(
        lambda *refs: middle_kernel(side, *refs),
        [shape((27 * chan, width_a), bf16), shape((2 * width_a, size), bf16)],
        [pltpu.VMEM((9 * width_a, small), f32), pltpu.VMEM((4, 9 * chan, size), bf16)],
        1 << 30,
        weight_b.reshape(27 * width_a, width_b),
        grad,
        before,
        after,
        hidden,
        source,
    )
    own, to_before, to_after = call(
        lambda *refs: input_kernel(side, *refs),
        [shape((2, chan, size), f32), shape((chan, size), bf16), shape((chan, size), bf16)],
        [pltpu.VMEM((9 * chan, size), f32)],
        1 << 29,
        weight_a.reshape(27 * chan, width_a),
        grad_hidden,
    )
    from_before = lax.ppermute(to_after, "space", upward)
    from_after = lax.ppermute(to_before, "space", downward)
    input_grad = own + jnp.stack([from_before, from_after]).astype(f32)
    input_grad = input_grad.astype(bf16).transpose(1, 0, 2)[None]
    samples = lax.axis_size("dp")

    def summed(part, count):
        part = lax.psum_scatter(part, "dp", scatter_dimension=0, tiled=True)
        part = lax.psum(part, "space")
        part = lax.all_gather(part, "dp", axis=0, tiled=True)
        return part.astype(f32) * (1.0 / math.sqrt(count))

    planes_a = depth_a * slabs
    total_b = summed(sums_b, samples * (planes_a // 2) * small)
    total_a = summed(sums_a, samples * planes_a * size)
    return (input_grad, total_a.reshape(weight_a.shape), total_b.reshape(weight_b.shape))


def solution(mesh):
    in_specs = (
        P("dp", None, "space", None),
        P("dp", None, "space", None),
        P("dp", None, "space", None),
        P("dp", None, "space", None),
        P(),
        P(),
    )
    out_specs = (P("dp", None, "space", None), P(), P())
    return jax.shard_map(
        per_device, mesh=mesh, in_specs=in_specs, out_specs=out_specs, check_vma=False
    )
```

```python
import math

import jax
import jax.numpy as jnp
from jax import lax
from jax.experimental import pallas as pl
from jax.experimental.pallas import tpu as pltpu
from jax.sharding import PartitionSpec as P

negative_slope = 0.3
f32 = jnp.float32
bf16 = jnp.bfloat16
vmem = pl.BlockSpec(memory_space=pltpu.VMEM)
transposed = (((1,), (1,)), ((), ()))


def shifted(cells, rows, columns, side):
    size = side * side
    offset = rows * side + columns
    if offset:
        cells = pltpu.roll(cells, (-offset) % size, 1)
    place = lax.broadcasted_iota(jnp.int32, cells.shape, 1)
    if rows:
        y = place // side + rows
        cells = jnp.where((y >= 0) & (y < side), cells, 0.0)
    if columns:
        x = place % side + columns
        cells = jnp.where((x >= 0) & (x < side), cells, 0.0)
    return cells


def gathered(parts, side):
    total = None
    for c in range(3):
        line = parts(1, c) + shifted(parts(0, c), 1, 0, side) + shifted(parts(2, c), -1, 0, side)
        line = shifted(line, 0, 1 - c, side)
        total = line if total is None else total + line
    return total


def pool_matrix(side):
    half = side // 2
    fine = lax.broadcasted_iota(jnp.int32, (side * side, half * half), 0)
    coarse = lax.broadcasted_iota(jnp.int32, (side * side, half * half), 1)
    parent = (fine // (2 * side)) * half + (fine % side) // 2
    return jnp.where(parent == coarse, 0.125, 0.0).astype(bf16)


def call(kernel, out_shape, scratch, flops, *args):
    return pl.pallas_call(
        kernel,
        out_shape=out_shape,
        in_specs=[vmem] * len(args),
        out_specs=jax.tree.map(lambda _: vmem, out_shape),
        scratch_shapes=scratch,
        compiler_params=pltpu.CompilerParams(vmem_limit_bytes=48 * 1024 * 1024),
        cost_estimate=pl.CostEstimate(flops=flops, bytes_accessed=2 << 20, transcendentals=0),
    )(*args)


def first_kernel(side, hidden, grad, source, pooled, up, down):
    width = hidden.shape[1]
    pool = pool_matrix(side)
    total = None
    for plane in range(2):
        cells = hidden[plane].astype(f32)
        stacked = jnp.concatenate([jnp.maximum(cells, 0.0), jnp.minimum(cells, 0.0)], 0).astype(bf16)
        part = jnp.dot(stacked, pool, preferred_element_type=f32)
        total = part if total is None else total + part
    pooled[...] = (total[:width] + negative_slope * total[width:]).astype(bf16)
    rows, cols = grad.shape
    for out, plane in ((up, 1), (down, 0)):
        out[:rows] = grad[...]
        chan = source.shape[1]
        for piece in range(source.shape[2] // cols):
            out[rows + piece * chan : rows + (piece + 1) * chan] = source[
                plane, :, piece * cols : (piece + 1) * cols
            ]


def share_kernel(plan, got, out, moved, totals):
    size = got.shape[2]
    half = math.isqrt(size)
    width, share, samples, slabs = plan.width, plan.share, plan.samples, plan.slabs
    for sample in range(samples):
        cells = got[sample, :width].astype(f32)
        for tap in range(9):
            moved[tap * width : (tap + 1) * width, sample * size : (sample + 1) * size] = shifted(
                cells, tap // 3 - 1, tap % 3 - 1, half
            ).astype(bf16)
    right = jnp.concatenate([got[k, width : width + 3 * share] for k in range(samples)], 1)
    result = lax.dot_general(moved[...], right, transposed, preferred_element_type=f32)
    for a in range(3):
        pieces = [
            result[k * plan.tall : (k + 1) * plan.tall, a * share : (a + 1) * share] for k in range(plan.pieces)
        ]
        totals[a * plan.tall : (a + 1) * plan.tall] = jnp.concatenate(pieces, 1)
    totals[3 * plan.tall :] = jnp.zeros((plan.pad_b, 128), f32)
    start = width + 3 * share
    first = got[0, start:].astype(f32)
    for sample in range(1, samples):
        first += got[sample, start:].astype(f32)
    first = first.astype(bf16)
    for slab in range(slabs):
        out[slab, : plan.pad_b] = totals[slab * plan.rows_b : slab * plan.rows_b + plan.pad_b].astype(bf16)
        row = slab * plan.rows_a
        column, row = row // plan.half_a, row % plan.half_a
        out[slab, plan.pad_b :] = first[row : row + plan.rows_a, column * 128 : (column + 1) * 128]


def sum_kernel(parts, out):
    total = parts[0].astype(f32)
    for k in range(1, parts.shape[0]):
        total += parts[k].astype(f32)
    out[...] = total.astype(bf16)


def last_kernel(plan, scale_a, scale_b, got, out_a, out_b, share_rows):
    devices = plan.samples * plan.slabs
    for device in range(devices):
        row = device * plan.rows_a
        if row < out_a.shape[0]:
            out_a[row : row + plan.rows_a] = got[device, plan.pad_b :].astype(f32) * scale_a
        sample, slab = device // plan.slabs, device % plan.slabs
        block = got[device, : plan.pad_b].astype(f32)[: plan.rows_b]
        share_rows[sample, slab * plan.rows_b : (slab + 1) * plan.rows_b] = block * scale_b
    for a in range(3):
        for k in range(plan.pieces):
            parts = [
                share_rows[sample, a * plan.tall : (a + 1) * plan.tall][:, k * plan.share : (k + 1) * plan.share]
                for sample in range(plan.samples)
            ]
            row = (a * plan.pieces + k) * plan.tall
            out_b[row : row + plan.tall] = jnp.concatenate(parts, 1)


class Plan:
    def __init__(self, samples, slabs, chan, width, width_b):
        self.samples, self.slabs, self.width = samples, slabs, width
        self.share = width_b // samples
        self.pieces = 128 // self.share
        self.tall = 9 * width // self.pieces
        self.rows_b = 3 * self.tall // slabs
        self.pad_b = -(-self.rows_b // 16) * 16
        self.rows_a = -(-27 * chan // (16 * samples * slabs)) * 16
        self.half_a = self.rows_a * slabs // 2
        self.message = width + 3 * self.share + self.half_a
        self.block = self.pad_b + self.rows_a


def middle_kernel(side, plan, weight, pooled, grad, before, after, hidden, source, message, grad_hidden, products, moved, sums):
    half = side // 2
    width = hidden.shape[1]
    rows = grad.shape[0]
    cols = grad.shape[1]
    chan = source.shape[1]
    size = side * side
    block = 9 * width
    products[...] = jnp.dot(weight[:block], after[:rows], preferred_element_type=f32)
    products[...] += jnp.dot(weight[block : 2 * block], grad[...], preferred_element_type=f32)
    products[...] += jnp.dot(weight[2 * block :], before[:rows], preferred_element_type=f32)

    def part(b, c):
        tap = 3 * b + c
        return products[tap * width : (tap + 1) * width]

    back = gathered(part, half)
    high = back.astype(bf16)
    low = (back - high.astype(f32)).astype(bf16)
    pool = pool_matrix(side)
    spread = lax.dot_general(high, pool, transposed, preferred_element_type=f32)
    spread += lax.dot_general(low, pool, transposed, preferred_element_type=f32)
    for plane in range(2):
        slope = jnp.where(hidden[plane].astype(f32) > 0, 1.0, negative_slope)
        grad_hidden[plane * width : (plane + 1) * width] = (spread * slope).astype(bf16)

    def plane_of(index):
        if index in (0, 1):
            return source[index]
        edge = before if index < 0 else after
        pieces = [edge[rows + k * chan : rows + (k + 1) * chan] for k in range(size // cols)]
        return jnp.concatenate(pieces, 1)

    for index in range(-1, 3):
        cells = plane_of(index).astype(f32)
        for tap in range(9):
            moved[index + 1, tap * chan : (tap + 1) * chan] = shifted(
                cells, tap // 3 - 1, tap % 3 - 1, side
            ).astype(bf16)
    both = grad_hidden[...]
    outer0 = lax.dot_general(moved[0], both[:width], transposed, preferred_element_type=f32)
    inner0 = lax.dot_general(moved[1], both, transposed, preferred_element_type=f32)
    inner1 = lax.dot_general(moved[2], both, transposed, preferred_element_type=f32)
    outer1 = lax.dot_general(moved[3], both[width:], transposed, preferred_element_type=f32)
    tall = 9 * chan
    sums[:tall] = outer0 + inner0[:, width:]
    sums[tall : 2 * tall] = inner0[:, :width] + inner1[:, width:]
    sums[2 * tall : 3 * tall] = inner1[:, :width] + outer1
    sums[3 * tall :] = jnp.zeros((sums.shape[0] - 3 * tall, width), f32)
    share = plan.share
    for member in range(plan.samples):
        message[member, :width] = pooled[...]
        for a, plane in enumerate((after, grad, before)):
            row = width + a * share
            message[member, row : row + share] = plane[member * share : (member + 1) * share]
        row = width + 3 * share
        for column in range(2):
            start = (2 * member + column) * plan.half_a
            message[member, row:, column * 128 : (column + 1) * 128] = sums[start : start + plan.half_a].astype(bf16)


def input_kernel(side, weight, grad_hidden, own, to_before, to_after, products):
    width = weight.shape[1]
    tall = weight.shape[0] // 3
    chan = tall // 9
    both = grad_hidden[...]

    def part(b, c):
        tap = 3 * b + c
        return products[tap * chan : (tap + 1) * chan]

    products[...] = jnp.dot(weight[:tall], both[:width], preferred_element_type=f32)
    to_before[...] = gathered(part, side).astype(bf16)
    products[...] = jnp.dot(weight[2 * tall :], both[width:], preferred_element_type=f32)
    to_after[...] = gathered(part, side).astype(bf16)
    for plane in range(2):
        mixed = jnp.concatenate(
            [weight[(plane + 1) * tall : (plane + 2) * tall], weight[plane * tall : (plane + 1) * tall]], 1
        )
        products[...] = jnp.dot(mixed, both, preferred_element_type=f32)
        own[plane] = gathered(part, side)


def per_device(layer_input, hidden_pre, output_pre, output_grad, weight_a, weight_b):
    side = math.isqrt(layer_input.shape[3])
    half = side // 2
    size, small = side * side, half * half
    depth_a = layer_input.shape[2]
    source = layer_input[0].transpose(1, 0, 2)
    hidden = hidden_pre[0].transpose(1, 0, 2)
    chan = source.shape[1]
    width_a = hidden.shape[1]
    width_b = output_pre.shape[1]
    outer = output_pre[0, :, 0].astype(f32)
    grad = (output_grad[0, :, 0].astype(f32) * jnp.where(outer > 0, 1.0, negative_slope)).astype(bf16)
    shape = jax.ShapeDtypeStruct
    tall = width_b + chan * size // small
    pooled, up, down = call(
        lambda *refs: first_kernel(side, *refs),
        [shape((width_a, small), bf16), shape((tall, small), bf16), shape((tall, small), bf16)],
        [],
        1 << 28,
        hidden,
        grad,
        source,
    )
    slabs = lax.axis_size("space")
    upward = [(i, i + 1) for i in range(slabs - 1)]
    downward = [(i + 1, i) for i in range(slabs - 1)]
    before = lax.ppermute(up, "space", upward)
    after = lax.ppermute(down, "space", downward)
    samples = lax.axis_size("dp")
    plan = Plan(samples, slabs, chan, width_a, width_b)
    message, grad_hidden = call(
        lambda *refs: middle_kernel(side, plan, *refs),
        [shape((samples, plan.message, small), bf16), shape((2 * width_a, size), bf16)],
        [
            pltpu.VMEM((9 * width_a, small), f32),
            pltpu.VMEM((4, 9 * chan, size), bf16),
            pltpu.VMEM((plan.rows_a * samples * slabs, width_a), f32),
        ],
        1 << 30,
        weight_b.reshape(27 * width_a, width_b),
        pooled,
        grad,
        before,
        after,
        hidden,
        source,
    )
    got = lax.all_to_all(message, "dp", 0, 0)
    blocks = call(
        lambda *refs: share_kernel(plan, *refs),
        shape((slabs, plan.block, 128), bf16),
        [
            pltpu.VMEM((9 * width_a, samples * small), bf16),
            pltpu.VMEM((3 * plan.tall + plan.pad_b, 128), f32),
        ],
        1 << 30,
        got,
    )
    parts = lax.all_to_all(blocks, "space", 0, 0)
    mine = call(sum_kernel, shape((plan.block, 128), bf16), [], 1 << 20, parts)
    everything = lax.all_gather(mine, ("dp", "space"))
    own, to_before, to_after = call(
        lambda *refs: input_kernel(side, *refs),
        [shape((2, chan, size), f32), shape((chan, size), bf16), shape((chan, size), bf16)],
        [pltpu.VMEM((9 * chan, size), f32)],
        1 << 29,
        weight_a.reshape(27 * chan, width_a),
        grad_hidden,
    )
    from_before = lax.ppermute(to_after, "space", upward)
    from_after = lax.ppermute(to_before, "space", downward)
    input_grad = own + jnp.stack([from_before, from_after]).astype(f32)
    input_grad = input_grad.astype(bf16).transpose(1, 0, 2)[None]
    planes_a = depth_a * slabs
    total_a, total_b = call(
        lambda *refs: last_kernel(
            plan,
            1.0 / math.sqrt(samples * planes_a * size),
            1.0 / math.sqrt(samples * (planes_a // 2) * small),
            *refs,
        ),
        [shape((27 * chan, width_a), f32), shape((27 * width_a, width_b), f32)],
        [pltpu.VMEM((samples, 3 * plan.tall, 128), f32)],
        1 << 20,
        everything,
    )
    return (input_grad, total_a.reshape(weight_a.shape), total_b.reshape(weight_b.shape))


def solution(mesh):
    in_specs = (
        P("dp", None, "space", None),
        P("dp", None, "space", None),
        P("dp", None, "space", None),
        P("dp", None, "space", None),
        P(),
        P(),
    )
    out_specs = (P("dp", None, "space", None), P(), P())
    return jax.shard_map(
        per_device, mesh=mesh, in_specs=in_specs, out_specs=out_specs, check_vma=False
    )
```

```python
import math

import jax
import jax.numpy as jnp
from jax import lax
from jax.experimental import pallas as pl
from jax.experimental.pallas import tpu as pltpu
from jax.sharding import PartitionSpec as P

negative_slope = 0.3
f32 = jnp.float32
bf16 = jnp.bfloat16
vmem = pl.BlockSpec(memory_space=pltpu.VMEM)
transposed = (((1,), (1,)), ((), ()))


def shifted(cells, rows, columns, side):
    size = side * side
    offset = rows * side + columns
    if offset:
        cells = pltpu.roll(cells, (-offset) % size, 1)
    place = lax.broadcasted_iota(jnp.int32, cells.shape, 1)
    if rows:
        y = place // side + rows
        cells = jnp.where((y >= 0) & (y < side), cells, 0.0)
    if columns:
        x = place % side + columns
        cells = jnp.where((x >= 0) & (x < side), cells, 0.0)
    return cells


def gathered(parts, side):
    total = None
    for c in range(3):
        line = parts(1, c) + shifted(parts(0, c), 1, 0, side) + shifted(parts(2, c), -1, 0, side)
        line = shifted(line, 0, 1 - c, side)
        total = line if total is None else total + line
    return total


def pool_matrix(side):
    half = side // 2
    fine = lax.broadcasted_iota(jnp.int32, (side * side, half * half), 0)
    coarse = lax.broadcasted_iota(jnp.int32, (side * side, half * half), 1)
    parent = (fine // (2 * side)) * half + (fine % side) // 2
    return jnp.where(parent == coarse, 0.125, 0.0).astype(bf16)


def call(kernel, out_shape, scratch, flops, *args):
    return pl.pallas_call(
        kernel,
        out_shape=out_shape,
        in_specs=[vmem] * len(args),
        out_specs=jax.tree.map(lambda _: vmem, out_shape),
        scratch_shapes=scratch,
        compiler_params=pltpu.CompilerParams(vmem_limit_bytes=48 * 1024 * 1024),
        cost_estimate=pl.CostEstimate(flops=flops, bytes_accessed=2 << 20, transcendentals=0),
    )(*args)


def first_kernel(side, hidden, grad, source, pooled, up, down):
    width = hidden.shape[1]
    pool = pool_matrix(side)
    total = None
    for plane in range(2):
        cells = hidden[plane].astype(f32)
        stacked = jnp.concatenate([jnp.maximum(cells, 0.0), jnp.minimum(cells, 0.0)], 0).astype(bf16)
        part = jnp.dot(stacked, pool, preferred_element_type=f32)
        total = part if total is None else total + part
    pooled[...] = (total[:width] + negative_slope * total[width:]).astype(bf16)
    rows, cols = grad.shape
    for out, plane in ((up, 1), (down, 0)):
        out[:rows] = grad[...]
        chan = source.shape[1]
        for piece in range(source.shape[2] // cols):
            out[rows + piece * chan : rows + (piece + 1) * chan] = source[
                plane, :, piece * cols : (piece + 1) * cols
            ]


def share_kernel(plan, got, out, moved, totals):
    size = got.shape[2]
    half = math.isqrt(size)
    width, share, samples, slabs = plan.width, plan.share, plan.samples, plan.slabs
    for sample in range(samples):
        cells = got[sample, :width].astype(f32)
        for tap in range(9):
            moved[tap * width : (tap + 1) * width, sample * size : (sample + 1) * size] = shifted(
                cells, tap // 3 - 1, tap % 3 - 1, half
            ).astype(bf16)
    right = jnp.concatenate([got[k, width : width + 3 * share] for k in range(samples)], 1)
    result = lax.dot_general(moved[...], right, transposed, preferred_element_type=f32)
    for a in range(3):
        pieces = [
            result[k * plan.tall : (k + 1) * plan.tall, a * share : (a + 1) * share] for k in range(plan.pieces)
        ]
        totals[a * plan.tall : (a + 1) * plan.tall] = jnp.concatenate(pieces, 1)
    totals[3 * plan.tall :] = jnp.zeros((plan.pad_b, 128), f32)
    start = width + 3 * share
    first = got[0, start:].astype(f32)
    for sample in range(1, samples):
        first += got[sample, start:].astype(f32)
    first = first.astype(bf16)
    for slab in range(slabs):
        out[slab, : plan.pad_b] = totals[slab * plan.rows_b : slab * plan.rows_b + plan.pad_b].astype(bf16)
        row = slab * plan.rows_a
        column, row = row // plan.half_a, row % plan.half_a
        out[slab, plan.pad_b :] = first[row : row + plan.rows_a, column * 128 : (column + 1) * 128]


def sum_kernel(parts, out):
    total = parts[0].astype(f32)
    for k in range(1, parts.shape[0]):
        total += parts[k].astype(f32)
    total = total.astype(bf16)
    for k in range(out.shape[0]):
        out[k] = total


def last_kernel(plan, scale_a, scale_b, *refs):
    shares, (out_a, out_b, share_rows) = refs[:-3], refs[-3:]
    me = lax.axis_index("dp")
    for distance, got in enumerate(shares):
        sample = me ^ distance
        for slab in range(plan.slabs):
            row = pl.multiple_of((sample * plan.slabs + slab) * plan.rows_a, plan.rows_a)

            @pl.when(row < out_a.shape[0])
            def _():
                out_a[pl.ds(row, plan.rows_a)] = got[slab, plan.pad_b :].astype(f32) * scale_a

            block = got[slab, : plan.pad_b].astype(f32)[: plan.rows_b]
            share_rows[sample, slab * plan.rows_b : (slab + 1) * plan.rows_b] = block * scale_b
    for a in range(3):
        for k in range(plan.pieces):
            parts = [
                share_rows[sample, a * plan.tall : (a + 1) * plan.tall][:, k * plan.share : (k + 1) * plan.share]
                for sample in range(plan.samples)
            ]
            row = (a * plan.pieces + k) * plan.tall
            out_b[row : row + plan.tall] = jnp.concatenate(parts, 1)


class Plan:
    def __init__(self, samples, slabs, chan, width, width_b):
        self.samples, self.slabs, self.width = samples, slabs, width
        self.share = width_b // samples
        self.pieces = 128 // self.share
        self.tall = 9 * width // self.pieces
        self.rows_b = 3 * self.tall // slabs
        self.pad_b = -(-self.rows_b // 16) * 16
        self.rows_a = -(-27 * chan // (16 * samples * slabs)) * 16
        self.half_a = self.rows_a * slabs // 2
        self.message = width + 3 * self.share + self.half_a
        self.block = self.pad_b + self.rows_a


def middle_kernel(side, plan, weight, pooled, grad, before, after, hidden, source, message, grad_hidden, products, moved, sums):
    half = side // 2
    width = hidden.shape[1]
    rows = grad.shape[0]
    cols = grad.shape[1]
    chan = source.shape[1]
    size = side * side
    block = 9 * width
    products[...] = jnp.dot(weight[:block], after[:rows], preferred_element_type=f32)
    products[...] += jnp.dot(weight[block : 2 * block], grad[...], preferred_element_type=f32)
    products[...] += jnp.dot(weight[2 * block :], before[:rows], preferred_element_type=f32)

    def part(b, c):
        tap = 3 * b + c
        return products[tap * width : (tap + 1) * width]

    back = gathered(part, half)
    high = back.astype(bf16)
    low = (back - high.astype(f32)).astype(bf16)
    pool = pool_matrix(side)
    spread = lax.dot_general(high, pool, transposed, preferred_element_type=f32)
    spread += lax.dot_general(low, pool, transposed, preferred_element_type=f32)
    for plane in range(2):
        slope = jnp.where(hidden[plane].astype(f32) > 0, 1.0, negative_slope)
        grad_hidden[plane * width : (plane + 1) * width] = (spread * slope).astype(bf16)

    def plane_of(index):
        if index in (0, 1):
            return source[index]
        edge = before if index < 0 else after
        pieces = [edge[rows + k * chan : rows + (k + 1) * chan] for k in range(size // cols)]
        return jnp.concatenate(pieces, 1)

    for index in range(-1, 3):
        cells = plane_of(index).astype(f32)
        for tap in range(9):
            moved[index + 1, tap * chan : (tap + 1) * chan] = shifted(
                cells, tap // 3 - 1, tap % 3 - 1, side
            ).astype(bf16)
    both = grad_hidden[...]
    outer0 = lax.dot_general(moved[0], both[:width], transposed, preferred_element_type=f32)
    inner0 = lax.dot_general(moved[1], both, transposed, preferred_element_type=f32)
    inner1 = lax.dot_general(moved[2], both, transposed, preferred_element_type=f32)
    outer1 = lax.dot_general(moved[3], both[width:], transposed, preferred_element_type=f32)
    tall = 9 * chan
    sums[:tall] = outer0 + inner0[:, width:]
    sums[tall : 2 * tall] = inner0[:, :width] + inner1[:, width:]
    sums[2 * tall : 3 * tall] = inner1[:, :width] + outer1
    sums[3 * tall :] = jnp.zeros((sums.shape[0] - 3 * tall, width), f32)
    share = plan.share
    for member in range(plan.samples):
        message[member, :width] = pooled[...]
        for a, plane in enumerate((after, grad, before)):
            row = width + a * share
            message[member, row : row + share] = plane[member * share : (member + 1) * share]
        row = width + 3 * share
        for column in range(2):
            start = (2 * member + column) * plan.half_a
            message[member, row:, column * 128 : (column + 1) * 128] = sums[start : start + plan.half_a].astype(bf16)


def input_kernel(side, weight, grad_hidden, own, to_before, to_after, products):
    width = weight.shape[1]
    tall = weight.shape[0] // 3
    chan = tall // 9
    both = grad_hidden[...]

    def part(b, c):
        tap = 3 * b + c
        return products[tap * chan : (tap + 1) * chan]

    products[...] = jnp.dot(weight[:tall], both[:width], preferred_element_type=f32)
    to_before[...] = gathered(part, side).astype(bf16)
    products[...] = jnp.dot(weight[2 * tall :], both[width:], preferred_element_type=f32)
    to_after[...] = gathered(part, side).astype(bf16)
    for plane in range(2):
        mixed = jnp.concatenate(
            [weight[(plane + 1) * tall : (plane + 2) * tall], weight[plane * tall : (plane + 1) * tall]], 1
        )
        products[...] = jnp.dot(mixed, both, preferred_element_type=f32)
        own[plane] = gathered(part, side)


def per_device(layer_input, hidden_pre, output_pre, output_grad, weight_a, weight_b):
    side = math.isqrt(layer_input.shape[3])
    half = side // 2
    size, small = side * side, half * half
    depth_a = layer_input.shape[2]
    source = layer_input[0].transpose(1, 0, 2)
    hidden = hidden_pre[0].transpose(1, 0, 2)
    chan = source.shape[1]
    width_a = hidden.shape[1]
    width_b = output_pre.shape[1]
    outer = output_pre[0, :, 0].astype(f32)
    grad = (output_grad[0, :, 0].astype(f32) * jnp.where(outer > 0, 1.0, negative_slope)).astype(bf16)
    shape = jax.ShapeDtypeStruct
    tall = width_b + chan * size // small
    pooled, up, down = call(
        lambda *refs: first_kernel(side, *refs),
        [shape((width_a, small), bf16), shape((tall, small), bf16), shape((tall, small), bf16)],
        [],
        1 << 28,
        hidden,
        grad,
        source,
    )
    slabs = lax.axis_size("space")
    upward = [(i, i + 1) for i in range(slabs - 1)]
    downward = [(i + 1, i) for i in range(slabs - 1)]
    before = lax.ppermute(up, "space", upward)
    after = lax.ppermute(down, "space", downward)
    samples = lax.axis_size("dp")
    plan = Plan(samples, slabs, chan, width_a, width_b)
    message, grad_hidden = call(
        lambda *refs: middle_kernel(side, plan, *refs),
        [shape((samples, plan.message, small), bf16), shape((2 * width_a, size), bf16)],
        [
            pltpu.VMEM((9 * width_a, small), f32),
            pltpu.VMEM((4, 9 * chan, size), bf16),
            pltpu.VMEM((plan.rows_a * samples * slabs, width_a), f32),
        ],
        1 << 30,
        weight_b.reshape(27 * width_a, width_b),
        pooled,
        grad,
        before,
        after,
        hidden,
        source,
    )
    got = lax.all_to_all(message, "dp", 0, 0)
    blocks = call(
        lambda *refs: share_kernel(plan, *refs),
        shape((slabs, plan.block, 128), bf16),
        [
            pltpu.VMEM((9 * width_a, samples * small), bf16),
            pltpu.VMEM((3 * plan.tall + plan.pad_b, 128), f32),
        ],
        1 << 30,
        got,
    )
    parts = lax.all_to_all(blocks, "space", 0, 0)
    mine = call(sum_kernel, shape((slabs, plan.block, 128), bf16), [], 1 << 20, parts)
    shares = {0: lax.all_to_all(mine, "space", 0, 0)}
    strides = [samples >> k for k in range(1, samples.bit_length())]

    def exchanged(stride, part):
        return lax.ppermute(part, "dp", [(i, i ^ stride) for i in range(samples)])

    received = {strides[0]: exchanged(strides[0], shares[0])}
    early = {stride: exchanged(stride, shares[0]) for stride in strides[1:]}
    own, to_before, to_after = call(
        lambda *refs: input_kernel(side, *refs),
        [shape((2, chan, size), f32), shape((chan, size), bf16), shape((chan, size), bf16)],
        [pltpu.VMEM((9 * chan, size), f32)],
        1 << 29,
        weight_a.reshape(27 * chan, width_a),
        grad_hidden,
    )
    from_before = lax.ppermute(to_after, "space", upward)
    from_after = lax.ppermute(to_before, "space", downward)
    input_grad = own + jnp.stack([from_before, from_after]).astype(f32)
    input_grad = input_grad.astype(bf16).transpose(1, 0, 2)[None]
    received[strides[0]], input_grad = lax.optimization_barrier((received[strides[0]], input_grad))
    shares.update(received)
    shares.update(early)
    for stride in strides[1:]:
        for k in list(shares):
            if k ^ stride not in shares:
                shares[k ^ stride] = exchanged(stride, shares[k])
    planes_a = depth_a * slabs
    total_a, total_b = call(
        lambda *refs: last_kernel(
            plan,
            1.0 / math.sqrt(samples * planes_a * size),
            1.0 / math.sqrt(samples * (planes_a // 2) * small),
            *refs,
        ),
        [shape((27 * chan, width_a), f32), shape((27 * width_a, width_b), f32)],
        [pltpu.VMEM((samples, 3 * plan.tall, 128), f32)],
        1 << 20,
        *[shares[k] for k in range(samples)],
    )
    return (input_grad, total_a.reshape(weight_a.shape), total_b.reshape(weight_b.shape))


def solution(mesh):
    in_specs = (
        P("dp", None, "space", None),
        P("dp", None, "space", None),
        P("dp", None, "space", None),
        P("dp", None, "space", None),
        P(),
        P(),
    )
    out_specs = (P("dp", None, "space", None), P(), P())
    return jax.shard_map(
        per_device, mesh=mesh, in_specs=in_specs, out_specs=out_specs, check_vma=False
    )
```

```python
import math

import jax
import jax.numpy as jnp
from jax import lax
from jax.experimental import pallas as pl
from jax.experimental.pallas import tpu as pltpu
from jax.sharding import PartitionSpec as P

negative_slope = 0.3
f32 = jnp.float32
bf16 = jnp.bfloat16
vmem = pl.BlockSpec(memory_space=pltpu.VMEM)
transposed = (((1,), (1,)), ((), ()))


def shifted(cells, rows, columns, side):
    size = side * side
    offset = rows * side + columns
    if offset:
        cells = pltpu.roll(cells, (-offset) % size, 1)
    place = lax.broadcasted_iota(jnp.int32, cells.shape, 1)
    if rows:
        y = place // side + rows
        cells = jnp.where((y >= 0) & (y < side), cells, 0.0)
    if columns:
        x = place % side + columns
        cells = jnp.where((x >= 0) & (x < side), cells, 0.0)
    return cells


def gathered(parts, side):
    total = None
    for c in range(3):
        line = parts(1, c) + shifted(parts(0, c), 1, 0, side) + shifted(parts(2, c), -1, 0, side)
        line = shifted(line, 0, 1 - c, side)
        total = line if total is None else total + line
    return total


def pool_matrix(side):
    half = side // 2
    fine = lax.broadcasted_iota(jnp.int32, (side * side, half * half), 0)
    coarse = lax.broadcasted_iota(jnp.int32, (side * side, half * half), 1)
    parent = (fine // (2 * side)) * half + (fine % side) // 2
    return jnp.where(parent == coarse, 0.125, 0.0).astype(bf16)


def call(kernel, out_shape, scratch, flops, *args):
    result = pl.pallas_call(
        kernel,
        out_shape=out_shape,
        in_specs=[vmem] * len(args),
        out_specs=jax.tree.map(lambda _: vmem, out_shape),
        scratch_shapes=scratch,
        compiler_params=pltpu.CompilerParams(vmem_limit_bytes=48 * 1024 * 1024),
        cost_estimate=pl.CostEstimate(flops=flops, bytes_accessed=2 << 20, transcendentals=0),
    )(*args)
    return list(result) if isinstance(out_shape, list) else result


def pool_kernel(side, hidden, pooled):
    width = hidden.shape[1]
    pool = pool_matrix(side)
    total = None
    for plane in range(2):
        cells = hidden[plane].astype(f32)
        stacked = jnp.concatenate([jnp.maximum(cells, 0.0), jnp.minimum(cells, 0.0)], 0).astype(bf16)
        part = jnp.dot(stacked, pool, preferred_element_type=f32)
        total = part if total is None else total + part
    pooled[...] = (total[:width] + negative_slope * total[width:]).astype(bf16)


def pack_kernel(plan, pooled, grad, before, after, *messages):
    me = lax.axis_index("dp")
    for distance, message in enumerate(messages):
        message[: plan.width] = pooled[...]
        start = pl.multiple_of((me ^ distance) * plan.share, plan.share)
        for a, plane in enumerate((after, grad, before)):
            row = plan.width + a * plan.share
            message[row : row + plan.share] = plane[pl.ds(start, plan.share)]


def share_kernel(plan, *refs):
    got, (out, moved, totals) = refs[:-3], refs[-3:]
    size = got[0].shape[1]
    half = math.isqrt(size)
    width, share = plan.width, plan.share
    for k, message in enumerate(got):
        cells = message[:width].astype(f32)
        for tap in range(9):
            moved[tap * width : (tap + 1) * width, k * size : (k + 1) * size] = shifted(
                cells, tap // 3 - 1, tap % 3 - 1, half
            ).astype(bf16)
    right = jnp.concatenate([message[width:] for message in got], 1)
    result = lax.dot_general(moved[...], right, transposed, preferred_element_type=f32)
    for a in range(3):
        pieces = [
            result[k * plan.tall : (k + 1) * plan.tall, a * share : (a + 1) * share] for k in range(plan.pieces)
        ]
        totals[a * plan.tall : (a + 1) * plan.tall] = jnp.concatenate(pieces, 1)
    totals[3 * plan.tall :] = jnp.zeros((plan.pad_b, 128), f32)
    for slab in range(plan.slabs):
        out[slab] = totals[slab * plan.rows_b : slab * plan.rows_b + plan.pad_b]


def blocks_kernel(plan, totals, *refs):
    got, blocks, first = refs[: plan.samples], refs[plan.samples : -1], refs[-1]
    total = got[0][...].astype(f32)
    for message in got[1:]:
        total += message[...].astype(f32)
    first[...] = total
    me = lax.axis_index("space")
    for distance, block in enumerate(blocks):
        slab = me ^ distance
        block[: plan.pad_b] = totals[slab].astype(bf16)
        row = pl.multiple_of(slab * plan.rows_a, plan.rows_a)
        block[plan.pad_b :] = first[pl.ds(row, plan.rows_a)].astype(bf16)


def sum_kernel(*refs):
    total = refs[0][...].astype(f32)
    for part in refs[1:-1]:
        total += part[...].astype(f32)
    refs[-1][...] = total.astype(bf16)


def stack_kernel(*refs):
    me = lax.axis_index("space")
    for distance, block in enumerate(refs[:-1]):
        refs[-1][me ^ distance] = block[...]


def last_kernel(plan, scale_a, scale_b, *refs):
    shares, (out_a, out_b, share_rows) = refs[:-3], refs[-3:]
    me = lax.axis_index("dp")
    for distance, got in enumerate(shares):
        sample = me ^ distance
        for slab in range(plan.slabs):
            row = pl.multiple_of((sample * plan.slabs + slab) * plan.rows_a, plan.rows_a)

            @pl.when(row < out_a.shape[0])
            def _():
                out_a[pl.ds(row, plan.rows_a)] = got[slab, plan.pad_b :].astype(f32) * scale_a

            block = got[slab, : plan.pad_b].astype(f32)[: plan.rows_b]
            share_rows[sample, slab * plan.rows_b : (slab + 1) * plan.rows_b] = block * scale_b
    for a in range(3):
        for k in range(plan.pieces):
            parts = [
                share_rows[sample, a * plan.tall : (a + 1) * plan.tall][:, k * plan.share : (k + 1) * plan.share]
                for sample in range(plan.samples)
            ]
            row = (a * plan.pieces + k) * plan.tall
            out_b[row : row + plan.tall] = jnp.concatenate(parts, 1)


class Plan:
    def __init__(self, samples, slabs, chan, width, width_b):
        self.samples, self.slabs, self.width = samples, slabs, width
        self.share = width_b // samples
        self.pieces = 128 // self.share
        self.tall = 9 * width // self.pieces
        self.rows_b = 3 * self.tall // slabs
        self.pad_b = -(-self.rows_b // 16) * 16
        self.rows_a = -(-27 * chan // (16 * samples * slabs)) * 16
        self.message = width + 3 * self.share
        self.block = self.pad_b + self.rows_a


def hidden_kernel(side, weight, grad, before, after, hidden, grad_hidden, products):
    half = side // 2
    width = hidden.shape[1]
    block = 9 * width
    products[...] = jnp.dot(weight[:block], after[...], preferred_element_type=f32)
    products[...] += jnp.dot(weight[block : 2 * block], grad[...], preferred_element_type=f32)
    products[...] += jnp.dot(weight[2 * block :], before[...], preferred_element_type=f32)

    def part(b, c):
        tap = 3 * b + c
        return products[tap * width : (tap + 1) * width]

    back = gathered(part, half)
    high = back.astype(bf16)
    low = (back - high.astype(f32)).astype(bf16)
    pool = pool_matrix(side)
    spread = lax.dot_general(high, pool, transposed, preferred_element_type=f32)
    spread += lax.dot_general(low, pool, transposed, preferred_element_type=f32)
    for plane in range(2):
        slope = jnp.where(hidden[plane].astype(f32) > 0, 1.0, negative_slope)
        grad_hidden[plane * width : (plane + 1) * width] = (spread * slope).astype(bf16)


def sums_a_kernel(side, plan, grad_hidden, source, before, after, *refs):
    messages, (moved, sums) = refs[:-2], refs[-2:]
    width = plan.width
    chan = source.shape[1]
    for index, plane in enumerate((before, source.at[0], source.at[1], after)):
        cells = plane[...].astype(f32)
        for tap in range(9):
            moved[index, tap * chan : (tap + 1) * chan] = shifted(
                cells, tap // 3 - 1, tap % 3 - 1, side
            ).astype(bf16)
    both = grad_hidden[...]
    outer0 = lax.dot_general(moved[0], both[:width], transposed, preferred_element_type=f32)
    inner0 = lax.dot_general(moved[1], both, transposed, preferred_element_type=f32)
    inner1 = lax.dot_general(moved[2], both, transposed, preferred_element_type=f32)
    outer1 = lax.dot_general(moved[3], both[width:], transposed, preferred_element_type=f32)
    tall = 9 * chan
    sums[:tall] = outer0 + inner0[:, width:]
    sums[tall : 2 * tall] = inner0[:, :width] + inner1[:, width:]
    sums[2 * tall : 3 * tall] = inner1[:, :width] + outer1
    sums[3 * tall :] = jnp.zeros((sums.shape[0] - 3 * tall, width), f32)
    me = lax.axis_index("dp")
    for distance, message in enumerate(messages):
        rows = message.shape[0]
        message[...] = sums[pl.ds(pl.multiple_of((me ^ distance) * rows, rows), rows)].astype(bf16)


def input_kernel(side, weight, grad_hidden, own, to_before, to_after, products):
    width = weight.shape[1]
    tall = weight.shape[0] // 3
    chan = tall // 9
    both = grad_hidden[...]

    def part(b, c):
        tap = 3 * b + c
        return products[tap * chan : (tap + 1) * chan]

    products[...] = jnp.dot(weight[:tall], both[:width], preferred_element_type=f32)
    to_before[...] = gathered(part, side).astype(bf16)
    products[...] = jnp.dot(weight[2 * tall :], both[width:], preferred_element_type=f32)
    to_after[...] = gathered(part, side).astype(bf16)
    for plane in range(2):
        mixed = jnp.concatenate(
            [weight[(plane + 1) * tall : (plane + 2) * tall], weight[plane * tall : (plane + 1) * tall]], 1
        )
        products[...] = jnp.dot(mixed, both, preferred_element_type=f32)
        own[plane] = gathered(part, side)


def swapped(part, axis, distance):
    return lax.ppermute(part, axis, [(i, i ^ distance) for i in range(lax.axis_size(axis))])


def per_device(layer_input, hidden_pre, output_pre, output_grad, weight_a, weight_b):
    side = math.isqrt(layer_input.shape[3])
    half = side // 2
    size, small = side * side, half * half
    depth_a = layer_input.shape[2]
    samples, slabs = lax.axis_size("dp"), lax.axis_size("space")
    upward = [(i, i + 1) for i in range(slabs - 1)]
    downward = [(i + 1, i) for i in range(slabs - 1)]
    shape = jax.ShapeDtypeStruct
    outer = output_pre[0, :, 0].astype(f32)
    grad = (output_grad[0, :, 0].astype(f32) * jnp.where(outer > 0, 1.0, negative_slope)).astype(bf16)
    grad, layer_input, hidden_pre = lax.optimization_barrier((grad, layer_input, hidden_pre))
    before = lax.ppermute(grad, "space", upward)
    after = lax.ppermute(grad, "space", downward)
    source = layer_input[0].transpose(1, 0, 2)
    hidden = hidden_pre[0].transpose(1, 0, 2)
    source_before = lax.ppermute(source[1], "space", upward)
    source_after = lax.ppermute(source[0], "space", downward)
    chan = source.shape[1]
    width_a = hidden.shape[1]
    width_b = grad.shape[0]
    plan = Plan(samples, slabs, chan, width_a, width_b)
    pooled = call(lambda *refs: pool_kernel(side, *refs), shape((width_a, small), bf16), [], 1 << 28, hidden)
    packed = call(
        lambda *refs: pack_kernel(plan, *refs),
        [shape((plan.message, small), bf16)] * samples,
        [],
        1 << 20,
        pooled,
        grad,
        before,
        after,
    )
    got_b = packed[:1] + [swapped(packed[k], "dp", k) for k in range(1, samples)]
    grad_hidden = call(
        lambda *refs: hidden_kernel(side, *refs),
        shape((2 * width_a, size), bf16),
        [pltpu.VMEM((9 * width_a, small), f32)],
        1 << 30,
        weight_b.reshape(27 * width_a, width_b),
        grad,
        before,
        after,
        hidden,
    )
    sums_a = call(
        lambda *refs: sums_a_kernel(side, plan, *refs),
        [shape((plan.rows_a * slabs, width_a), bf16)] * samples,
        [
            pltpu.VMEM((4, 9 * chan, size), bf16),
            pltpu.VMEM((plan.rows_a * samples * slabs, width_a), f32),
        ],
        1 << 30,
        grad_hidden,
        source,
        source_before,
        source_after,
    )
    got_a = sums_a[:1] + [swapped(sums_a[k], "dp", k) for k in range(1, samples)]
    totals = call(
        lambda *refs: share_kernel(plan, *refs),
        shape((slabs, plan.pad_b, 128), f32),
        [
            pltpu.VMEM((9 * width_a, samples * small), bf16),
            pltpu.VMEM((3 * plan.tall + plan.pad_b, 128), f32),
        ],
        1 << 30,
        *got_b,
    )
    blocks = call(
        lambda *refs: blocks_kernel(plan, *refs),
        [shape((plan.block, 128), bf16)] * slabs,
        [pltpu.VMEM((plan.rows_a * slabs, 128), f32)],
        1 << 20,
        totals,
        *got_a,
    )
    parts = blocks[:1] + [swapped(blocks[k], "space", k) for k in range(1, slabs)]
    mine = call(sum_kernel, shape((plan.block, 128), bf16), [], 1 << 20, *parts)
    gathers = [mine] + [swapped(mine, "space", k) for k in range(1, slabs)]
    stack = call(stack_kernel, shape((slabs, plan.block, 128), bf16), [], 1 << 20, *gathers)
    strides = [samples >> k for k in range(1, samples.bit_length())]
    received = {strides[0]: swapped(stack, "dp", strides[0])}
    early = {stride: swapped(stack, "dp", stride) for stride in strides[1:]}
    own, to_before, to_after = call(
        lambda *refs: input_kernel(side, *refs),
        [shape((2, chan, size), f32), shape((chan, size), bf16), shape((chan, size), bf16)],
        [pltpu.VMEM((9 * chan, size), f32)],
        1 << 29,
        weight_a.reshape(27 * chan, width_a),
        grad_hidden,
    )
    from_before = lax.ppermute(to_after, "space", upward)
    from_after = lax.ppermute(to_before, "space", downward)
    input_grad = own + jnp.stack([from_before, from_after]).astype(f32)
    input_grad = input_grad.astype(bf16).transpose(1, 0, 2)[None]
    received[strides[0]], input_grad = lax.optimization_barrier((received[strides[0]], input_grad))
    shares = {0: stack, **received, **early}
    for stride in strides[1:]:
        for k in list(shares):
            if k ^ stride not in shares:
                shares[k ^ stride] = swapped(shares[k], "dp", stride)
    planes_a = depth_a * slabs
    total_a, total_b = call(
        lambda *refs: last_kernel(
            plan,
            1.0 / math.sqrt(samples * planes_a * size),
            1.0 / math.sqrt(samples * (planes_a // 2) * small),
            *refs,
        ),
        [shape((27 * chan, width_a), f32), shape((27 * width_a, width_b), f32)],
        [pltpu.VMEM((samples, 3 * plan.tall, 128), f32)],
        1 << 20,
        *[shares[k] for k in range(samples)],
    )
    return (input_grad, total_a.reshape(weight_a.shape), total_b.reshape(weight_b.shape))


def solution(mesh):
    in_specs = (
        P("dp", None, "space", None),
        P("dp", None, "space", None),
        P("dp", None, "space", None),
        P("dp", None, "space", None),
        P(),
        P(),
    )
    out_specs = (P("dp", None, "space", None), P(), P())
    return jax.shard_map(
        per_device, mesh=mesh, in_specs=in_specs, out_specs=out_specs, check_vma=False
    )
```

```python
import math

import jax
import jax.numpy as jnp
from jax import lax
from jax.experimental import pallas as pl
from jax.experimental.pallas import tpu as pltpu
from jax.sharding import PartitionSpec as P

negative_slope = 0.3
f32 = jnp.float32
bf16 = jnp.bfloat16
vmem = pl.BlockSpec(memory_space=pltpu.VMEM)
transposed = (((1,), (1,)), ((), ()))


def shifted(cells, rows, columns, side):
    size = side * side
    offset = rows * side + columns
    if offset:
        cells = pltpu.roll(cells, (-offset) % size, 1)
    place = lax.broadcasted_iota(jnp.int32, cells.shape, 1)
    if rows:
        y = place // side + rows
        cells = jnp.where((y >= 0) & (y < side), cells, 0.0)
    if columns:
        x = place % side + columns
        cells = jnp.where((x >= 0) & (x < side), cells, 0.0)
    return cells


def gathered(parts, side):
    total = None
    for c in range(3):
        line = parts(1, c) + shifted(parts(0, c), 1, 0, side) + shifted(parts(2, c), -1, 0, side)
        line = shifted(line, 0, 1 - c, side)
        total = line if total is None else total + line
    return total


def pool_matrix(side):
    half = side // 2
    fine = lax.broadcasted_iota(jnp.int32, (side * side, half * half), 0)
    coarse = lax.broadcasted_iota(jnp.int32, (side * side, half * half), 1)
    parent = (fine // (2 * side)) * half + (fine % side) // 2
    return jnp.where(parent == coarse, 0.125, 0.0).astype(bf16)


def is_even():
    return lax.axis_index("space") % 2 == 0


def sides(even_pairs, odd_pairs):
    even = is_even()
    first, second = even_pairs[...], odd_pairs[...]
    return jnp.where(even, second, first), jnp.where(even, first, second)


def call(kernel, out_shape, scratch, flops, *args, out_specs=None):
    result = pl.pallas_call(
        kernel,
        out_shape=out_shape,
        in_specs=[vmem] * len(args),
        out_specs=out_specs or jax.tree.map(lambda _: vmem, out_shape),
        scratch_shapes=scratch,
        compiler_params=pltpu.CompilerParams(vmem_limit_bytes=48 * 1024 * 1024),
        cost_estimate=pl.CostEstimate(flops=flops, bytes_accessed=2 << 20, transcendentals=0),
    )(*args)
    return list(result) if isinstance(out_shape, list) else result


def pool_kernel(side, hidden, pooled):
    width = hidden.shape[1]
    pool = pool_matrix(side)
    total = None
    for plane in range(2):
        cells = hidden[plane].astype(f32)
        stacked = jnp.concatenate([jnp.maximum(cells, 0.0), jnp.minimum(cells, 0.0)], 0).astype(bf16)
        part = jnp.dot(stacked, pool, preferred_element_type=f32)
        total = part if total is None else total + part
    pooled[...] = (total[:width] + negative_slope * total[width:]).astype(bf16)


def pack_kernel(plan, pooled, grad, even_pairs, odd_pairs, *refs):
    me = lax.axis_index("dp")
    messages, (before, after) = refs[:-2], refs[-2:]
    before[...], after[...] = sides(even_pairs, odd_pairs)
    for distance, message in enumerate(messages):
        message[: plan.width] = pooled[...]
        start = pl.multiple_of((me ^ distance) * plan.share, plan.share)
        for a, plane in enumerate((after, grad, before)):
            row = plan.width + a * plan.share
            message[row : row + plan.share] = plane[pl.ds(start, plan.share)]


def share_kernel(plan, *refs):
    got, (out, moved, totals) = refs[:-3], refs[-3:]
    size = got[0].shape[1]
    half = math.isqrt(size)
    width, share = plan.width, plan.share
    for k, message in enumerate(got):
        cells = message[:width].astype(f32)
        for tap in range(9):
            moved[tap * width : (tap + 1) * width, k * size : (k + 1) * size] = shifted(
                cells, tap // 3 - 1, tap % 3 - 1, half
            ).astype(bf16)
    right = jnp.concatenate([message[width:] for message in got], 1)
    result = lax.dot_general(moved[...], right, transposed, preferred_element_type=f32)
    for a in range(3):
        pieces = [
            result[k * plan.tall : (k + 1) * plan.tall, a * share : (a + 1) * share] for k in range(plan.pieces)
        ]
        totals[a * plan.tall : (a + 1) * plan.tall] = jnp.concatenate(pieces, 1)
    spare = totals.shape[0] - 3 * plan.tall
    totals[3 * plan.tall :] = jnp.zeros((spare, 128), f32)
    for slab in range(plan.slabs):
        out[slab] = totals[slab * plan.rows_b : slab * plan.rows_b + plan.pad_b]


def blocks_kernel(plan, totals, *refs):
    got, blocks, first = refs[: plan.samples], refs[plan.samples : -1], refs[-1]
    total = got[0][...].astype(f32)
    for message in got[1:]:
        total += message[...].astype(f32)
    first[...] = total
    me = lax.axis_index("space")
    for distance, block in enumerate(blocks):
        for k in range(2):
            slab = me ^ distance ^ (k * plan.far)
            block[k, : plan.pad_b] = totals[slab].astype(bf16)
            row = pl.multiple_of(slab * plan.rows_a, plan.rows_a)
            block[k, plan.pad_b :] = first[pl.ds(row, plan.rows_a)].astype(bf16)


def near_kernel(*refs):
    parts, (keep, send) = refs[:-2], refs[-2:]
    total = parts[0][...].astype(f32)
    for part in parts[1:]:
        total += part[...].astype(f32)
    keep[...] = total[0]
    send[...] = total[1].astype(bf16)


def far_kernel(keep, part, out):
    out[...] = (keep[...] + part[...].astype(f32)).astype(bf16)


def stack_kernel(*refs):
    out = refs[-1]
    rank = len(out.shape)
    row = 0
    for part in refs[:-1]:
        if len(part.shape) < rank:
            out[row] = part[...]
            row += 1
        else:
            out[row : row + part.shape[0]] = part[...]
            row += part.shape[0]


def stacked(parts):
    rows = sum(part.shape[0] if part.ndim == 3 else 1 for part in parts)
    shape = jax.ShapeDtypeStruct((rows, *parts[0].shape[-2:]), bf16)
    return call(stack_kernel, shape, [], 1 << 20, *parts)


def last_kernel(plan, scale_a, scale_b, *refs):
    got, (out_a, out_b, share_rows, rows, sems) = refs[:-5], refs[-5:]
    me, here = lax.axis_index("dp"), lax.axis_index("space")
    for distance in range(plan.samples):
        sample = me ^ distance
        pair, rest = got[2 * distance : 2 * distance + 2]
        for k in range(plan.slabs):
            slab = here ^ (k // 2) ^ (k % 2 * plan.far)
            part = pair.at[k] if k < 2 else rest.at[k - 2]
            row = pl.multiple_of((sample * plan.slabs + slab) * plan.rows_a, plan.rows_a)

            @pl.when(row < out_a.shape[0])
            def _():
                out_a[pl.ds(row, plan.rows_a)] = part[plan.pad_b :].astype(f32) * scale_a

            share_rows[sample, slab] = part[: plan.pad_b].astype(f32)[: plan.rows_b] * scale_b
    columns = [share_rows[sample].reshape(-1, 128) for sample in range(plan.samples)]
    copies = []
    for a in range(3):
        for k in range(plan.pieces):
            parts = [
                column[a * plan.tall : (a + 1) * plan.tall, k * plan.share : (k + 1) * plan.share]
                for column in columns
            ]
            row = (a * plan.pieces + k) * plan.tall
            rows[row : row + plan.tall] = jnp.concatenate(parts, 1)
        height = plan.pieces * plan.tall
        place = pl.ds(a * height, height)
        copies.append(pltpu.make_async_copy(rows.at[place], out_b.at[place], sems.at[a]))
        copies[-1].start()
    for copy in copies:
        copy.wait()


class Plan:
    def __init__(self, samples, slabs, chan, width, width_b):
        self.samples, self.slabs, self.width = samples, slabs, width
        self.share = width_b // samples
        self.pieces = 128 // self.share
        self.tall = 9 * width // self.pieces
        self.rows_b = -(-3 * self.tall // (8 * slabs)) * 8
        self.pad_b = -(-self.rows_b // 16) * 16
        self.rows_a = -(-27 * chan // (16 * samples * slabs)) * 16
        self.message = width + 3 * self.share
        self.block = self.pad_b + self.rows_a
        self.far = slabs // 2


def hidden_kernel(side, weight, grad, before, after, hidden, grad_hidden, products):
    half = side // 2
    width = hidden.shape[1]
    block = 9 * width
    products[...] = jnp.dot(weight[:block], after[...], preferred_element_type=f32)
    products[...] += jnp.dot(weight[block : 2 * block], grad[...], preferred_element_type=f32)
    products[...] += jnp.dot(weight[2 * block :], before[...], preferred_element_type=f32)

    def part(b, c):
        tap = 3 * b + c
        return products[tap * width : (tap + 1) * width]

    back = gathered(part, half)
    high = back.astype(bf16)
    low = (back - high.astype(f32)).astype(bf16)
    pool = pool_matrix(side)
    spread = lax.dot_general(high, pool, transposed, preferred_element_type=f32)
    spread += lax.dot_general(low, pool, transposed, preferred_element_type=f32)
    for plane in range(2):
        slope = jnp.where(hidden[plane].astype(f32) > 0, 1.0, negative_slope)
        grad_hidden[plane * width : (plane + 1) * width] = (spread * slope).astype(bf16)


def sums_a_kernel(side, plan, grad_hidden, source, even_pairs, odd_pairs, *refs):
    messages, (moved, sums) = refs[:-2], refs[-2:]
    width = plan.width
    chan = source.shape[1]
    before, after = sides(even_pairs, odd_pairs)
    for index, plane in enumerate((before, source[0], source[1], after)):
        cells = plane.astype(f32)
        for tap in range(9):
            moved[index, tap * chan : (tap + 1) * chan] = shifted(
                cells, tap // 3 - 1, tap % 3 - 1, side
            ).astype(bf16)
    both = grad_hidden[...]
    outer0 = lax.dot_general(moved[0], both[:width], transposed, preferred_element_type=f32)
    inner0 = lax.dot_general(moved[1], both, transposed, preferred_element_type=f32)
    inner1 = lax.dot_general(moved[2], both, transposed, preferred_element_type=f32)
    outer1 = lax.dot_general(moved[3], both[width:], transposed, preferred_element_type=f32)
    tall = 9 * chan
    sums[:tall] = outer0 + inner0[:, width:]
    sums[tall : 2 * tall] = inner0[:, :width] + inner1[:, width:]
    sums[2 * tall : 3 * tall] = inner1[:, :width] + outer1
    sums[3 * tall :] = jnp.zeros((sums.shape[0] - 3 * tall, width), f32)
    me = lax.axis_index("dp")
    for distance, message in enumerate(messages):
        rows = message.shape[0]
        message[...] = sums[pl.ds(pl.multiple_of((me ^ distance) * rows, rows), rows)].astype(bf16)


def input_kernel(side, weight, grad_hidden, own, even_pairs, odd_pairs, products):
    width = weight.shape[1]
    tall = weight.shape[0] // 3
    chan = tall // 9
    both = grad_hidden[...]

    def part(b, c):
        tap = 3 * b + c
        return products[tap * chan : (tap + 1) * chan]

    products[...] = jnp.dot(weight[:tall], both[:width], preferred_element_type=f32)
    to_before = gathered(part, side).astype(bf16)
    products[...] = jnp.dot(weight[2 * tall :], both[width:], preferred_element_type=f32)
    to_after = gathered(part, side).astype(bf16)
    even_pairs[...], odd_pairs[...] = jnp.where(is_even(), to_after, to_before), jnp.where(
        is_even(), to_before, to_after
    )
    for plane in range(2):
        mixed = jnp.concatenate(
            [weight[(plane + 1) * tall : (plane + 2) * tall], weight[plane * tall : (plane + 1) * tall]], 1
        )
        products[...] = jnp.dot(mixed, both, preferred_element_type=f32)
        own[plane] = gathered(part, side)


def swapped(part, axis, distance):
    return lax.ppermute(part, axis, [(i, i ^ distance) for i in range(lax.axis_size(axis))])


def per_device(layer_input, hidden_pre, output_pre, output_grad, weight_a, weight_b):
    side = math.isqrt(layer_input.shape[3])
    half = side // 2
    size, small = side * side, half * half
    depth_a = layer_input.shape[2]
    samples, slabs = lax.axis_size("dp"), lax.axis_size("space")
    even, odd = (
        [(i + k, i + 1 - k) for i in range(start, slabs - 1, 2) for k in range(2)] for start in range(2)
    )
    shape = jax.ShapeDtypeStruct
    outer = output_pre[0, :, 0].astype(f32)
    grad = (output_grad[0, :, 0].astype(f32) * jnp.where(outer > 0, 1.0, negative_slope)).astype(bf16)
    grad, layer_input, hidden_pre = lax.optimization_barrier((grad, layer_input, hidden_pre))
    grad_sides = [lax.ppermute(grad, "space", pairs) for pairs in (even, odd)]
    source = layer_input[0].transpose(1, 0, 2)
    hidden = hidden_pre[0].transpose(1, 0, 2)
    source_sides = [
        lax.ppermute(jnp.where(is_even(), source[k], source[1 - k]), "space", pairs) for k, pairs in ((1, even), (0, odd))
    ]
    chan = source.shape[1]
    width_a = hidden.shape[1]
    width_b = grad.shape[0]
    plan = Plan(samples, slabs, chan, width_a, width_b)
    pooled = call(lambda *refs: pool_kernel(side, *refs), shape((width_a, small), bf16), [], 1 << 28, hidden)
    packed = call(
        lambda *refs: pack_kernel(plan, *refs),
        [shape((plan.message, small), bf16)] * samples + [shape(grad.shape, bf16)] * 2,
        [],
        1 << 20,
        pooled,
        grad,
        *grad_sides,
    )
    packed, (before, after) = packed[:samples], packed[samples:]
    got_b = packed[:1] + [swapped(packed[k], "dp", k) for k in range(1, samples)]
    grad_hidden = call(
        lambda *refs: hidden_kernel(side, *refs),
        shape((2 * width_a, size), bf16),
        [pltpu.VMEM((9 * width_a, small), f32)],
        1 << 30,
        weight_b.reshape(27 * width_a, width_b),
        grad,
        before,
        after,
        hidden,
    )
    sums_a = call(
        lambda *refs: sums_a_kernel(side, plan, *refs),
        [shape((plan.rows_a * slabs, width_a), bf16)] * samples,
        [
            pltpu.VMEM((4, 9 * chan, size), bf16),
            pltpu.VMEM((plan.rows_a * samples * slabs, width_a), f32),
        ],
        1 << 30,
        grad_hidden,
        source,
        *source_sides,
    )
    got_a = sums_a[:1] + [swapped(sums_a[k], "dp", k) for k in range(1, samples)]
    totals = call(
        lambda *refs: share_kernel(plan, *refs),
        shape((slabs, plan.pad_b, 128), f32),
        [
            pltpu.VMEM((9 * width_a, samples * small), bf16),
            pltpu.VMEM((slabs * plan.rows_b + plan.pad_b, 128), f32),
        ],
        1 << 30,
        *got_b,
    )
    far = plan.far
    blocks = call(
        lambda *refs: blocks_kernel(plan, *refs),
        [shape((2, plan.block, 128), bf16)] * far,
        [pltpu.VMEM((plan.rows_a * slabs, 128), f32)],
        1 << 20,
        totals,
        *got_a,
    )
    parts = blocks[:1] + [swapped(blocks[k], "space", k) for k in range(1, far)]
    own, even_part, odd_part = call(
        lambda *refs: input_kernel(side, *refs),
        [shape((2, chan, size), f32), shape((chan, size), bf16), shape((chan, size), bf16)],
        [pltpu.VMEM((9 * chan, size), f32)],
        1 << 29,
        weight_a.reshape(27 * chan, width_a),
        grad_hidden,
    )
    parts, own, even_part, odd_part = lax.optimization_barrier((parts, own, even_part, odd_part))
    keep, send = call(
        near_kernel, [shape((plan.block, 128), f32), shape((plan.block, 128), bf16)], [], 1 << 20, *parts
    )
    mine = call(far_kernel, shape((plan.block, 128), bf16), [], 1 << 20, keep, swapped(send, "space", far))
    pair = stacked([mine, swapped(mine, "space", far)])
    pair_first = swapped(pair, "dp", samples // 2)
    near = [swapped(pair, "space", k) for k in range(far - 1, 0, -1)][::-1]
    from_even, from_odd = lax.ppermute(even_part, "space", even), lax.ppermute(odd_part, "space", odd)
    near, pair_first, from_even, from_odd = lax.optimization_barrier((near, pair_first, from_even, from_odd))
    rest = stacked(near)
    rest_first = swapped(rest, "dp", samples // 2)
    from_sides = [jnp.where(is_even(), a, b) for a, b in ((from_odd, from_even), (from_even, from_odd))]
    input_grad = own + jnp.stack(from_sides).astype(f32)
    input_grad = input_grad.astype(bf16).transpose(1, 0, 2)[None]
    strides = [samples >> k for k in range(2, samples.bit_length())]
    early = {stride: [swapped(part, "dp", stride) for part in (pair, rest)] for stride in strides}
    early_pair = {stride: swapped(pair_first, "dp", stride) for stride in strides[:1]}
    rest_first, input_grad, early, early_pair = lax.optimization_barrier((rest_first, input_grad, early, early_pair))
    shares = {0: [pair, rest], samples // 2: [pair_first, rest_first], **early}
    for stride in strides:
        for k in list(shares):
            if k ^ stride not in shares:
                known = [early_pair[stride]] if k == samples // 2 and stride in early_pair else []
                shares[k ^ stride] = known + [swapped(part, "dp", stride) for part in shares[k][len(known) :]]
    planes_a = depth_a * slabs
    total_a, total_b = call(
        lambda *refs: last_kernel(
            plan,
            1.0 / math.sqrt(samples * planes_a * size),
            1.0 / math.sqrt(samples * (planes_a // 2) * small),
            *refs,
        ),
        [shape((27 * chan, width_a), f32), shape((27 * width_a, width_b), f32)],
        [
            pltpu.VMEM((samples, slabs, plan.rows_b, 128), f32),
            pltpu.VMEM((27 * width_a, width_b), f32),
            pltpu.SemaphoreType.DMA((3,)),
        ],
        1 << 20,
        *[part for k in range(samples) for part in shares[k]],
        out_specs=[vmem, pl.BlockSpec(memory_space=pl.ANY)],
    )
    return (input_grad, total_a.reshape(weight_a.shape), total_b.reshape(weight_b.shape))


def solution(mesh):
    in_specs = (
        P("dp", None, "space", None),
        P("dp", None, "space", None),
        P("dp", None, "space", None),
        P("dp", None, "space", None),
        P(),
        P(),
    )
    out_specs = (P("dp", None, "space", None), P(), P())
    return jax.shard_map(
        per_device, mesh=mesh, in_specs=in_specs, out_specs=out_specs, check_vma=False
    )
```

```python
import math

import jax
import jax.numpy as jnp
from jax import lax
from jax.experimental import pallas as pl
from jax.experimental.pallas import tpu as pltpu
from jax.sharding import PartitionSpec as P

negative_slope = 0.3
f32 = jnp.float32
bf16 = jnp.bfloat16
vmem = pl.BlockSpec(memory_space=pltpu.VMEM)
transposed = (((1,), (1,)), ((), ()))


def shifted(cells, rows, columns, side):
    size = side * side
    offset = rows * side + columns
    if offset:
        cells = pltpu.roll(cells, (-offset) % size, 1)
    place = lax.broadcasted_iota(jnp.int32, cells.shape, 1)
    if rows:
        y = place // side + rows
        cells = jnp.where((y >= 0) & (y < side), cells, 0.0)
    if columns:
        x = place % side + columns
        cells = jnp.where((x >= 0) & (x < side), cells, 0.0)
    return cells


def gathered(parts, side):
    total = None
    for c in range(3):
        line = parts(1, c) + shifted(parts(0, c), 1, 0, side) + shifted(parts(2, c), -1, 0, side)
        line = shifted(line, 0, 1 - c, side)
        total = line if total is None else total + line
    return total


def pool_matrix(side):
    half = side // 2
    fine = lax.broadcasted_iota(jnp.int32, (side * side, half * half), 0)
    coarse = lax.broadcasted_iota(jnp.int32, (side * side, half * half), 1)
    parent = (fine // (2 * side)) * half + (fine % side) // 2
    return jnp.where(parent == coarse, 0.125, 0.0).astype(bf16)


def is_even():
    return lax.axis_index("space") % 2 == 0


def sides(even_pairs, odd_pairs):
    even = is_even()
    first, second = even_pairs[...], odd_pairs[...]
    return jnp.where(even, second, first), jnp.where(even, first, second)


def call(kernel, out_shape, scratch, flops, *args, out_specs=None):
    result = pl.pallas_call(
        kernel,
        out_shape=out_shape,
        in_specs=[vmem] * len(args),
        out_specs=out_specs or jax.tree.map(lambda _: vmem, out_shape),
        scratch_shapes=scratch,
        compiler_params=pltpu.CompilerParams(vmem_limit_bytes=48 * 1024 * 1024),
        cost_estimate=pl.CostEstimate(flops=flops, bytes_accessed=2 << 20, transcendentals=0),
    )(*args)
    return list(result) if isinstance(out_shape, list) else result


def pool_kernel(side, hidden, pooled):
    width = hidden.shape[1]
    pool = pool_matrix(side)
    total = None
    for plane in range(2):
        cells = hidden[plane].astype(f32)
        stacked = jnp.concatenate([jnp.maximum(cells, 0.0), jnp.minimum(cells, 0.0)], 0).astype(bf16)
        part = jnp.dot(stacked, pool, preferred_element_type=f32)
        total = part if total is None else total + part
    pooled[...] = (total[:width] + negative_slope * total[width:]).astype(bf16)


def early_kernel(plan, pooled, grad, *messages):
    me = lax.axis_index("dp")
    for distance, message in enumerate(messages):
        message[: plan.width] = pooled[...]
        start = pl.multiple_of((me ^ distance) * plan.share, plan.share)
        message[plan.width :] = grad[pl.ds(start, plan.share)]


def late_kernel(plan, even_pairs, odd_pairs, *refs):
    me = lax.axis_index("dp")
    messages, (before, after) = refs[:-2], refs[-2:]
    before[...], after[...] = sides(even_pairs, odd_pairs)
    for distance, message in enumerate(messages):
        start = pl.multiple_of((me ^ distance) * plan.share, plan.share)
        for k, plane in enumerate((after, before)):
            message[k * plan.share : (k + 1) * plan.share] = plane[pl.ds(start, plan.share)]


def share_kernel(plan, *refs):
    early, late, (out, moved, totals) = refs[: plan.samples], refs[plan.samples : -3], refs[-3:]
    size = early[0].shape[1]
    half = math.isqrt(size)
    width, share = plan.width, plan.share
    for k, message in enumerate(early):
        cells = message[:width].astype(f32)
        for tap in range(9):
            moved[tap * width : (tap + 1) * width, k * size : (k + 1) * size] = shifted(
                cells, tap // 3 - 1, tap % 3 - 1, half
            ).astype(bf16)
    columns = [
        jnp.concatenate([ends[:share], message[width:], ends[share:]], 0) for message, ends in zip(early, late)
    ]
    right = jnp.concatenate(columns, 1)
    result = lax.dot_general(moved[...], right, transposed, preferred_element_type=f32)
    for a in range(3):
        pieces = [
            result[k * plan.tall : (k + 1) * plan.tall, a * share : (a + 1) * share] for k in range(plan.pieces)
        ]
        totals[a * plan.tall : (a + 1) * plan.tall] = jnp.concatenate(pieces, 1)
    spare = totals.shape[0] - 3 * plan.tall
    totals[3 * plan.tall :] = jnp.zeros((spare, 128), f32)
    for slab in range(plan.slabs):
        out[slab] = totals[slab * plan.rows_b : (slab + 1) * plan.rows_b]


def blocks_kernel(plan, totals, *refs):
    got, blocks, first = refs[: plan.samples], refs[plan.samples : -1], refs[-1]
    total = got[0][...].astype(f32)
    for message in got[1:]:
        total += message[...].astype(f32)
    first[...] = total
    me = lax.axis_index("space")
    for distance, block in enumerate(blocks):
        for k in range(2):
            slab = me ^ distance ^ (k * plan.far)
            block[k, : plan.rows_b] = totals[slab].astype(bf16)
            row = pl.multiple_of(slab * plan.rows_a, plan.rows_a)
            block[k, plan.rows_b :] = first[pl.ds(row, plan.rows_a)].astype(bf16)


def near_kernel(*refs):
    total = refs[0][...].astype(f32)
    for part in refs[1:-1]:
        total += part[...].astype(f32)
    refs[-1][...] = total.astype(bf16)


def far_kernel(here, there, out):
    for k in range(2):
        out[k] = (here[k].astype(f32) + there[1 - k].astype(f32)).astype(bf16)


def stack_kernel(*refs):
    for k, part in enumerate(refs[:-1]):
        refs[-1][2 * k : 2 * k + 2] = part[...]


def last_kernel(plan, scale_a, scale_b, *refs):
    got, (out_a, out_b, shares, rows, sems) = refs[:-5], refs[-5:]
    me, here = lax.axis_index("dp"), lax.axis_index("space")
    for n, piece in enumerate(got):
        sample = me ^ (n // 3)
        for k in range(piece.shape[0]):
            slab = here ^ ((0, 1, plan.far - 1)[n % 3] + k // 2) ^ (k % 2 * plan.far)
            row = pl.multiple_of((sample * plan.slabs + slab) * plan.rows_a, plan.rows_a)

            @pl.when(row < out_a.shape[0])
            def _():
                out_a[pl.ds(row, plan.rows_a)] = piece[k, plan.rows_b :].astype(f32) * scale_a

            shares[sample, slab] = piece[k, : plan.rows_b]
    copies = []
    for a in range(3):
        for k in range(plan.pieces):
            parts = [
                shares[sample].reshape(-1, 128)[a * plan.tall : (a + 1) * plan.tall].astype(f32)[
                    :, k * plan.share : (k + 1) * plan.share
                ]
                for sample in range(plan.samples)
            ]
            row = (a * plan.pieces + k) * plan.tall
            place = pl.ds(row, plan.tall)
            rows[place] = jnp.concatenate(parts, 1) * scale_b
            copies.append(pltpu.make_async_copy(rows.at[place], out_b.at[place], sems.at[len(copies)]))
            copies[-1].start()
    for copy in copies:
        copy.wait()


class Plan:
    def __init__(self, samples, slabs, chan, width, width_b):
        self.samples, self.slabs, self.width = samples, slabs, width
        self.share = width_b // samples
        self.pieces = 128 // self.share
        self.tall = 9 * width // self.pieces
        self.rows_b = -(-3 * self.tall // (16 * slabs)) * 16
        self.rows_a = -(-27 * chan // (16 * samples * slabs)) * 16
        self.block = self.rows_b + self.rows_a
        self.far = slabs // 2


def hidden_kernel(side, weight, grad, before, after, hidden, grad_hidden, products):
    half = side // 2
    width = hidden.shape[1]
    block = 9 * width
    products[...] = jnp.dot(weight[:block], after[...], preferred_element_type=f32)
    products[...] += jnp.dot(weight[block : 2 * block], grad[...], preferred_element_type=f32)
    products[...] += jnp.dot(weight[2 * block :], before[...], preferred_element_type=f32)

    def part(b, c):
        tap = 3 * b + c
        return products[tap * width : (tap + 1) * width]

    back = gathered(part, half)
    high = back.astype(bf16)
    low = (back - high.astype(f32)).astype(bf16)
    pool = pool_matrix(side)
    spread = lax.dot_general(high, pool, transposed, preferred_element_type=f32)
    spread += lax.dot_general(low, pool, transposed, preferred_element_type=f32)
    for plane in range(2):
        slope = jnp.where(hidden[plane].astype(f32) > 0, 1.0, negative_slope)
        grad_hidden[plane * width : (plane + 1) * width] = (spread * slope).astype(bf16)


def sums_a_kernel(side, plan, grad_hidden, source, even_pairs, odd_pairs, *refs):
    messages, (moved, sums) = refs[:-2], refs[-2:]
    width = plan.width
    chan = source.shape[1]
    before, after = sides(even_pairs, odd_pairs)
    for index, plane in enumerate((before, source[0], source[1], after)):
        cells = plane.astype(f32)
        for tap in range(9):
            moved[index, tap * chan : (tap + 1) * chan] = shifted(
                cells, tap // 3 - 1, tap % 3 - 1, side
            ).astype(bf16)
    both = grad_hidden[...]
    outer0 = lax.dot_general(moved[0], both[:width], transposed, preferred_element_type=f32)
    inner0 = lax.dot_general(moved[1], both, transposed, preferred_element_type=f32)
    inner1 = lax.dot_general(moved[2], both, transposed, preferred_element_type=f32)
    outer1 = lax.dot_general(moved[3], both[width:], transposed, preferred_element_type=f32)
    tall = 9 * chan
    sums[:tall] = outer0 + inner0[:, width:]
    sums[tall : 2 * tall] = inner0[:, :width] + inner1[:, width:]
    sums[2 * tall : 3 * tall] = inner1[:, :width] + outer1
    sums[3 * tall :] = jnp.zeros((sums.shape[0] - 3 * tall, width), f32)
    me = lax.axis_index("dp")
    for distance, message in enumerate(messages):
        rows = message.shape[0]
        message[...] = sums[pl.ds(pl.multiple_of((me ^ distance) * rows, rows), rows)].astype(bf16)


def input_kernel(side, weight, grad_hidden, own, even_pairs, odd_pairs, products):
    width = weight.shape[1]
    tall = weight.shape[0] // 3
    chan = tall // 9
    both = grad_hidden[...]

    def part(b, c):
        tap = 3 * b + c
        return products[tap * chan : (tap + 1) * chan]

    products[...] = jnp.dot(weight[:tall], both[:width], preferred_element_type=f32)
    to_before = gathered(part, side).astype(bf16)
    products[...] = jnp.dot(weight[2 * tall :], both[width:], preferred_element_type=f32)
    to_after = gathered(part, side).astype(bf16)
    even_pairs[...], odd_pairs[...] = jnp.where(is_even(), to_after, to_before), jnp.where(
        is_even(), to_before, to_after
    )
    for plane in range(2):
        mixed = jnp.concatenate(
            [weight[(plane + 1) * tall : (plane + 2) * tall], weight[plane * tall : (plane + 1) * tall]], 1
        )
        products[...] = jnp.dot(mixed, both, preferred_element_type=f32)
        own[plane] = gathered(part, side)


def swapped(part, axis, distance):
    return lax.ppermute(part, axis, [(i, i ^ distance) for i in range(lax.axis_size(axis))])


def per_device(layer_input, hidden_pre, output_pre, output_grad, weight_a, weight_b):
    side = math.isqrt(layer_input.shape[3])
    half = side // 2
    size, small = side * side, half * half
    depth_a = layer_input.shape[2]
    samples, slabs = lax.axis_size("dp"), lax.axis_size("space")
    even, odd = (
        [(i + k, i + 1 - k) for i in range(start, slabs - 1, 2) for k in range(2)] for start in range(2)
    )
    shape = jax.ShapeDtypeStruct
    outer = output_pre[0, :, 0].astype(f32)
    grad = (output_grad[0, :, 0].astype(f32) * jnp.where(outer > 0, 1.0, negative_slope)).astype(bf16)
    grad, layer_input, hidden_pre = lax.optimization_barrier((grad, layer_input, hidden_pre))
    grad_sides = [lax.ppermute(grad, "space", pairs) for pairs in (even, odd)]
    source = layer_input[0].transpose(1, 0, 2)
    hidden = hidden_pre[0].transpose(1, 0, 2)
    chan = source.shape[1]
    width_a = hidden.shape[1]
    width_b = grad.shape[0]
    plan = Plan(samples, slabs, chan, width_a, width_b)
    pooled = call(lambda *refs: pool_kernel(side, *refs), shape((width_a, small), bf16), [], 1 << 28, hidden)
    early = call(
        lambda *refs: early_kernel(plan, *refs),
        [shape((plan.width + plan.share, small), bf16)] * samples,
        [],
        1 << 20,
        pooled,
        grad,
    )
    early = early[:1] + [swapped(early[k], "dp", k) for k in range(1, samples)]
    source, grad_sides, early = lax.optimization_barrier((source, grad_sides, early))
    source_sides = [
        lax.ppermute(jnp.where(is_even(), source[k], source[1 - k]), "space", pairs) for k, pairs in ((1, even), (0, odd))
    ]
    late = call(
        lambda *refs: late_kernel(plan, *refs),
        [shape((2 * plan.share, small), bf16)] * samples + [shape(grad.shape, bf16)] * 2,
        [],
        1 << 20,
        *grad_sides,
    )
    late, (before, after) = late[:samples], late[samples:]
    late = late[:1] + [swapped(late[k], "dp", k) for k in range(1, samples)]
    grad_hidden = call(
        lambda *refs: hidden_kernel(side, *refs),
        shape((2 * width_a, size), bf16),
        [pltpu.VMEM((9 * width_a, small), f32)],
        1 << 30,
        weight_b.reshape(27 * width_a, width_b),
        grad,
        before,
        after,
        hidden,
    )
    sums_a = call(
        lambda *refs: sums_a_kernel(side, plan, *refs),
        [shape((plan.rows_a * slabs, width_a), bf16)] * samples,
        [
            pltpu.VMEM((4, 9 * chan, size), bf16),
            pltpu.VMEM((plan.rows_a * samples * slabs, width_a), f32),
        ],
        1 << 30,
        grad_hidden,
        source,
        *source_sides,
    )
    got_a = sums_a[:1] + [swapped(sums_a[k], "dp", k) for k in range(1, samples)]
    totals = call(
        lambda *refs: share_kernel(plan, *refs),
        shape((slabs, plan.rows_b, 128), f32),
        [
            pltpu.VMEM((9 * width_a, samples * small), bf16),
            pltpu.VMEM((slabs * plan.rows_b, 128), f32),
        ],
        1 << 30,
        *early,
        *late,
    )
    far = plan.far
    blocks = call(
        lambda *refs: blocks_kernel(plan, *refs),
        [shape((2, plan.block, 128), bf16)] * far,
        [pltpu.VMEM((plan.rows_a * slabs, 128), f32)],
        1 << 20,
        totals,
        *got_a,
    )
    parts = blocks[:1] + [swapped(blocks[k], "space", k) for k in range(1, far)]
    own, even_part, odd_part = call(
        lambda *refs: input_kernel(side, *refs),
        [shape((2, chan, size), f32), shape((chan, size), bf16), shape((chan, size), bf16)],
        [pltpu.VMEM((9 * chan, size), f32)],
        1 << 29,
        weight_a.reshape(27 * chan, width_a),
        grad_hidden,
    )
    parts, own, even_part, odd_part = lax.optimization_barrier((parts, own, even_part, odd_part))
    both = call(near_kernel, shape((2, plan.block, 128), bf16), [], 1 << 20, *parts)
    there = swapped(both, "space", far)
    from_even = lax.ppermute(even_part, "space", even)
    there, from_even, odd_part = lax.optimization_barrier((there, from_even, odd_part))
    pair = call(far_kernel, shape(both.shape, bf16), [], 1 << 20, both, there)
    strides = [samples >> k for k in range(1, samples.bit_length())]

    def crossed(parts):
        return [[swapped(part, "dp", stride) for part in parts] for stride in strides[1:]]

    near = [swapped(pair, "space", k) for k in range(1, far - 1)]
    pair_hop = swapped(pair, "dp", strides[0])
    near, pair_hop, pair, odd_part = lax.optimization_barrier((near, pair_hop, pair, odd_part))
    group = call(stack_kernel, shape((2 * far - 4, plan.block, 128), bf16), [], 1 << 20, *near)
    group_hop = swapped(group, "dp", strides[0])
    last = swapped(pair, "space", far - 1)
    across_first = crossed([pair, group, pair_hop])
    group_hop, last, across_first, odd_part = lax.optimization_barrier((group_hop, last, across_first, odd_part))
    last_hop = swapped(last, "dp", strides[0])
    from_odd = lax.ppermute(odd_part, "space", odd)
    from_sides = [jnp.where(is_even(), a, b) for a, b in ((from_odd, from_even), (from_even, from_odd))]
    input_grad = own + jnp.stack(from_sides).astype(f32)
    input_grad = input_grad.astype(bf16).transpose(1, 0, 2)[None]
    across_second = crossed([last, group_hop])
    last_hop, input_grad, across_second = lax.optimization_barrier((last_hop, input_grad, across_second))
    shares = {0: [pair, group, last], strides[0]: [pair_hop, group_hop, last_hop]}
    for stride, first, second in zip(strides[1:], across_first, across_second):
        for k in list(shares):
            if k == 0:
                shares[stride] = [first[0], first[1], second[0]]
            elif k == strides[0]:
                shares[k ^ stride] = [first[2], second[1], swapped(last_hop, "dp", stride)]
            elif k ^ stride not in shares:
                shares[k ^ stride] = [swapped(piece, "dp", stride) for piece in shares[k]]
    planes_a = depth_a * slabs
    total_a, total_b = call(
        lambda *refs: last_kernel(
            plan,
            1.0 / math.sqrt(samples * planes_a * size),
            1.0 / math.sqrt(samples * (planes_a // 2) * small),
            *refs,
        ),
        [shape((27 * chan, width_a), f32), shape((27 * width_a, width_b), f32)],
        [
            pltpu.VMEM((samples, slabs, plan.rows_b, 128), bf16),
            pltpu.VMEM((27 * width_a, width_b), f32),
            pltpu.SemaphoreType.DMA((3 * plan.pieces,)),
        ],
        1 << 20,
        *[part for k in range(samples) for part in shares[k]],
        out_specs=[vmem, pl.BlockSpec(memory_space=pl.ANY)],
    )
    return (input_grad, total_a.reshape(weight_a.shape), total_b.reshape(weight_b.shape))


def solution(mesh):
    in_specs = (
        P("dp", None, "space", None),
        P("dp", None, "space", None),
        P("dp", None, "space", None),
        P("dp", None, "space", None),
        P(),
        P(),
    )
    out_specs = (P("dp", None, "space", None), P(), P())
    return jax.shard_map(
        per_device, mesh=mesh, in_specs=in_specs, out_specs=out_specs, check_vma=False
    )
```

```python
import math

import jax
import jax.numpy as jnp
from jax import lax
from jax.experimental import pallas as pl
from jax.experimental.pallas import tpu as pltpu
from jax.sharding import PartitionSpec as P

negative_slope = 0.3
f32 = jnp.float32
bf16 = jnp.bfloat16
vmem = pl.BlockSpec(memory_space=pltpu.VMEM)
transposed = (((1,), (1,)), ((), ()))


def shifted(cells, rows, columns, side):
    size = side * side
    offset = rows * side + columns
    if offset:
        cells = pltpu.roll(cells, (-offset) % size, 1)
    place = lax.broadcasted_iota(jnp.int32, cells.shape, 1)
    if rows:
        y = place // side + rows
        cells = jnp.where((y >= 0) & (y < side), cells, 0.0)
    if columns:
        x = place % side + columns
        cells = jnp.where((x >= 0) & (x < side), cells, 0.0)
    return cells


def gathered(parts, side):
    total = None
    for c in range(3):
        line = parts(1, c) + shifted(parts(0, c), 1, 0, side) + shifted(parts(2, c), -1, 0, side)
        line = shifted(line, 0, 1 - c, side)
        total = line if total is None else total + line
    return total


def pool_matrix(side):
    half = side // 2
    fine = lax.broadcasted_iota(jnp.int32, (side * side, half * half), 0)
    coarse = lax.broadcasted_iota(jnp.int32, (side * side, half * half), 1)
    parent = (fine // (2 * side)) * half + (fine % side) // 2
    return jnp.where(parent == coarse, 0.125, 0.0).astype(bf16)


def sides(even_pairs, odd_pairs):
    here = lax.axis_index("space")
    even = here % 2 == 0
    nothing = jnp.zeros(even_pairs.shape, bf16)
    before = jnp.where(here == 0, nothing, jnp.where(even, odd_pairs, even_pairs))
    after = jnp.where(here == lax.axis_size("space") - 1, nothing, jnp.where(even, even_pairs, odd_pairs))
    return before, after


def for_sides(before, after):
    even = lax.axis_index("space") % 2 == 0
    return jnp.where(even, after, before), jnp.where(even, before, after)


def call(kernel, out_shape, scratch, flops, *args, out_specs=None):
    result = pl.pallas_call(
        kernel,
        out_shape=out_shape,
        in_specs=[vmem] * len(args),
        out_specs=out_specs or jax.tree.map(lambda _: vmem, out_shape),
        scratch_shapes=scratch,
        compiler_params=pltpu.CompilerParams(vmem_limit_bytes=48 * 1024 * 1024),
        cost_estimate=pl.CostEstimate(flops=flops, bytes_accessed=2 << 20, transcendentals=0),
    )(*args)
    return list(result) if isinstance(out_shape, list) else result


def pool_kernel(side, hidden, pooled):
    width = hidden.shape[1]
    pool = pool_matrix(side)
    total = None
    for plane in range(2):
        cells = hidden[plane].astype(f32)
        stacked = jnp.concatenate([jnp.maximum(cells, 0.0), jnp.minimum(cells, 0.0)], 0).astype(bf16)
        part = jnp.dot(stacked, pool, preferred_element_type=f32)
        total = part if total is None else total + part
    pooled[...] = (total[:width] + negative_slope * total[width:]).astype(bf16)


def early_kernel(plan, pooled, grad, *messages):
    me = lax.axis_index("dp")
    for distance, message in enumerate(messages):
        message[: plan.width] = pooled[...]
        start = pl.multiple_of((me ^ distance) * plan.share, plan.share)
        message[plan.width :] = grad[pl.ds(start, plan.share)]


def late_kernel(plan, even_pairs, odd_pairs, *refs):
    me = lax.axis_index("dp")
    messages, (before, after) = refs[:-2], refs[-2:]
    before[...], after[...] = sides(even_pairs[...], odd_pairs[...])
    for distance, message in enumerate(messages):
        start = pl.multiple_of((me ^ distance) * plan.share, plan.share)
        for k, plane in enumerate((after, before)):
            message[k * plan.share : (k + 1) * plan.share] = plane[pl.ds(start, plan.share)]


def share_kernel(plan, *refs):
    early, late, (out, moved, totals) = refs[: plan.samples], refs[plan.samples : -3], refs[-3:]
    size = early[0].shape[1]
    half = math.isqrt(size)
    width, share = plan.width, plan.share
    for k, message in enumerate(early):
        cells = message[:width].astype(f32)
        for tap in range(9):
            moved[tap * width : (tap + 1) * width, k * size : (k + 1) * size] = shifted(
                cells, tap // 3 - 1, tap % 3 - 1, half
            ).astype(bf16)
    columns = [
        jnp.concatenate([ends[:share], message[width:], ends[share:]], 0) for message, ends in zip(early, late)
    ]
    right = jnp.concatenate(columns, 1)
    result = lax.dot_general(moved[...], right, transposed, preferred_element_type=f32)
    for a in range(3):
        pieces = [
            result[k * plan.tall : (k + 1) * plan.tall, a * share : (a + 1) * share] for k in range(plan.pieces)
        ]
        totals[a * plan.tall : (a + 1) * plan.tall] = jnp.concatenate(pieces, 1)
    spare = totals.shape[0] - 3 * plan.tall
    totals[3 * plan.tall :] = jnp.zeros((spare, 128), f32)
    for slab in range(plan.slabs):
        out[slab] = totals[slab * plan.rows_b : (slab + 1) * plan.rows_b]


def blocks_kernel(plan, totals, *refs):
    got, blocks, first = refs[: plan.samples], refs[plan.samples : -1], refs[-1]
    total = got[0][...].astype(f32)
    for message in got[1:]:
        total += message[...].astype(f32)
    first[...] = total
    me = lax.axis_index("space")
    for distance, block in enumerate(blocks):
        for k in range(2):
            slab = me ^ distance ^ (k * plan.far)
            block[k, : plan.rows_b] = totals[slab].astype(bf16)
            row = pl.multiple_of(slab * plan.rows_a, plan.rows_a)
            block[k, plan.rows_b :] = first[pl.ds(row, plan.rows_a)].astype(bf16)


def near_kernel(*refs):
    total = refs[0][...].astype(f32)
    for part in refs[1:-1]:
        total += part[...].astype(f32)
    refs[-1][...] = total.astype(bf16)


def far_kernel(plan, here, there, low, high):
    for k in range(2):
        total = (here[k].astype(f32) + there[1 - k].astype(f32)).astype(bf16)
        low[k], high[k] = total[: plan.low], total[plan.low :]


def stack_kernel(*refs):
    count = refs[0].shape[0]
    for k, part in enumerate(refs[:-1]):
        refs[-1][count * k : count * (k + 1)] = part[...]


def last_kernel(plan, scale_a, scale_b, *refs):
    got, (out_a, out_b, shares, rows, sems) = refs[:-5], refs[-5:]
    me, here = lax.axis_index("dp"), lax.axis_index("space")
    far, groups = plan.far, plan.samples // 2
    each = len(got) // groups
    for group in range(groups):
        lows, hops, *highs = got[group * each : (group + 1) * each]
        for hop in range(2):
            sample = me ^ group ^ (hop * groups)
            for k in range(plan.slabs):
                slab = here ^ (k // 2) ^ (k % 2 * far)
                shares[sample, slab, : plan.low] = (hops if hop else lows)[k]
                shares[sample, slab, plan.low :] = highs[k // 2][2 * hop + k % 2]
    for sample in range(plan.samples):
        for slab in range(plan.slabs):
            row = (sample * plan.slabs + slab) * plan.rows_a
            if row < out_a.shape[0]:
                out_a[row : row + plan.rows_a] = shares[sample, slab, plan.rows_b :].astype(f32) * scale_a
    columns = [shares[sample, :, : plan.rows_b].reshape(-1, 128) for sample in range(plan.samples)]
    copies = []
    for a in range(3):
        for k in range(plan.pieces):
            parts = [
                column[a * plan.tall : (a + 1) * plan.tall].astype(f32)[:, k * plan.share : (k + 1) * plan.share]
                for column in columns
            ]
            row = (a * plan.pieces + k) * plan.tall
            place = pl.ds(row, plan.tall)
            rows[place] = jnp.concatenate(parts, 1) * scale_b
            copies.append(pltpu.make_async_copy(rows.at[place], out_b.at[place], sems.at[len(copies)]))
            copies[-1].start()
    for copy in copies:
        copy.wait()


class Plan:
    def __init__(self, samples, slabs, chan, width, width_b):
        self.samples, self.slabs, self.width = samples, slabs, width
        self.share = width_b // samples
        self.pieces = 128 // self.share
        self.tall = 9 * width // self.pieces
        self.rows_b = -(-3 * self.tall // (16 * slabs)) * 16
        self.rows_a = -(-27 * chan // (16 * samples * slabs)) * 16
        self.block = self.rows_b + self.rows_a
        self.low = -(-self.block // 32) * 16
        self.far = slabs // 2


def hidden_kernel(side, weight, grad, before, after, hidden, grad_hidden, products):
    half = side // 2
    width = hidden.shape[1]
    block = 9 * width
    products[...] = jnp.dot(weight[:block], after[...], preferred_element_type=f32)
    products[...] += jnp.dot(weight[block : 2 * block], grad[...], preferred_element_type=f32)
    products[...] += jnp.dot(weight[2 * block :], before[...], preferred_element_type=f32)

    def part(b, c):
        tap = 3 * b + c
        return products[tap * width : (tap + 1) * width]

    back = gathered(part, half)
    high = back.astype(bf16)
    low = (back - high.astype(f32)).astype(bf16)
    pool = pool_matrix(side)
    spread = lax.dot_general(high, pool, transposed, preferred_element_type=f32)
    spread += lax.dot_general(low, pool, transposed, preferred_element_type=f32)
    for plane in range(2):
        slope = jnp.where(hidden[plane].astype(f32) > 0, 1.0, negative_slope)
        grad_hidden[plane * width : (plane + 1) * width] = (spread * slope).astype(bf16)


def sums_a_kernel(side, plan, grad_hidden, source, even_pairs, odd_pairs, *refs):
    messages, (moved, sums) = refs[:-2], refs[-2:]
    width = plan.width
    chan = source.shape[1]
    before, after = sides(even_pairs[...], odd_pairs[...])
    for index, plane in enumerate((before, source[0], source[1], after)):
        cells = plane.astype(f32)
        for tap in range(9):
            moved[index, tap * chan : (tap + 1) * chan] = shifted(
                cells, tap // 3 - 1, tap % 3 - 1, side
            ).astype(bf16)
    both = grad_hidden[...]
    outer0 = lax.dot_general(moved[0], both[:width], transposed, preferred_element_type=f32)
    inner0 = lax.dot_general(moved[1], both, transposed, preferred_element_type=f32)
    inner1 = lax.dot_general(moved[2], both, transposed, preferred_element_type=f32)
    outer1 = lax.dot_general(moved[3], both[width:], transposed, preferred_element_type=f32)
    tall = 9 * chan
    sums[:tall] = outer0 + inner0[:, width:]
    sums[tall : 2 * tall] = inner0[:, :width] + inner1[:, width:]
    sums[2 * tall : 3 * tall] = inner1[:, :width] + outer1
    sums[3 * tall :] = jnp.zeros((sums.shape[0] - 3 * tall, width), f32)
    me = lax.axis_index("dp")
    for distance, message in enumerate(messages):
        rows = message.shape[0]
        message[...] = sums[pl.ds(pl.multiple_of((me ^ distance) * rows, rows), rows)].astype(bf16)


def input_kernel(side, weight, grad_hidden, own, even_pairs, odd_pairs, products):
    width = weight.shape[1]
    tall = weight.shape[0] // 3
    chan = tall // 9
    both = grad_hidden[...]

    def part(b, c):
        tap = 3 * b + c
        return products[tap * chan : (tap + 1) * chan]

    products[...] = jnp.dot(weight[:tall], both[:width], preferred_element_type=f32)
    to_before = gathered(part, side).astype(bf16)
    products[...] = jnp.dot(weight[2 * tall :], both[width:], preferred_element_type=f32)
    to_after = gathered(part, side).astype(bf16)
    even_pairs[...], odd_pairs[...] = for_sides(to_before, to_after)
    for plane in range(2):
        mixed = jnp.concatenate(
            [weight[(plane + 1) * tall : (plane + 2) * tall], weight[plane * tall : (plane + 1) * tall]], 1
        )
        products[...] = jnp.dot(mixed, both, preferred_element_type=f32)
        own[plane] = gathered(part, side)


def swapped(part, axis, distance):
    return lax.ppermute(part, axis, [(i, i ^ distance) for i in range(lax.axis_size(axis))])


def per_device(layer_input, hidden_pre, output_pre, output_grad, weight_a, weight_b):
    side = math.isqrt(layer_input.shape[3])
    half = side // 2
    size, small = side * side, half * half
    depth_a = layer_input.shape[2]
    samples, slabs = lax.axis_size("dp"), lax.axis_size("space")
    even, odd = (
        [((i + k) % slabs, (i + 1 - k) % slabs) for i in range(start, slabs, 2) for k in range(2)] for start in range(2)
    )
    shape = jax.ShapeDtypeStruct
    outer = output_pre[0, :, 0].astype(f32)
    grad = (output_grad[0, :, 0].astype(f32) * jnp.where(outer > 0, 1.0, negative_slope)).astype(bf16)
    grad, layer_input, hidden_pre = lax.optimization_barrier((grad, layer_input, hidden_pre))
    grad_sides = [lax.ppermute(grad, "space", pairs) for pairs in (even, odd)]
    source = layer_input[0].transpose(1, 0, 2)
    hidden = hidden_pre[0].transpose(1, 0, 2)
    chan = source.shape[1]
    width_a = hidden.shape[1]
    width_b = grad.shape[0]
    plan = Plan(samples, slabs, chan, width_a, width_b)
    pooled = call(lambda *refs: pool_kernel(side, *refs), shape((width_a, small), bf16), [], 1 << 28, hidden)
    early = call(
        lambda *refs: early_kernel(plan, *refs),
        [shape((plan.width + plan.share, small), bf16)] * samples,
        [],
        1 << 20,
        pooled,
        grad,
    )
    early = early[:1] + [swapped(early[k], "dp", k) for k in range(1, samples)]
    source, grad_sides, early = lax.optimization_barrier((source, grad_sides, early))
    source_sides = [
        lax.ppermute(part, "space", pairs) for part, pairs in zip(for_sides(source[0], source[1]), (even, odd))
    ]
    late = call(
        lambda *refs: late_kernel(plan, *refs),
        [shape((2 * plan.share, small), bf16)] * samples + [shape(grad.shape, bf16)] * 2,
        [],
        1 << 20,
        *grad_sides,
    )
    late, (before, after) = late[:samples], late[samples:]
    late = late[:1] + [swapped(late[k], "dp", k) for k in range(1, samples)]
    grad_hidden = call(
        lambda *refs: hidden_kernel(side, *refs),
        shape((2 * width_a, size), bf16),
        [pltpu.VMEM((9 * width_a, small), f32)],
        1 << 30,
        weight_b.reshape(27 * width_a, width_b),
        grad,
        before,
        after,
        hidden,
    )
    own, even_part, odd_part = call(
        lambda *refs: input_kernel(side, *refs),
        [shape((2, chan, size), f32), shape((chan, size), bf16), shape((chan, size), bf16)],
        [pltpu.VMEM((9 * chan, size), f32)],
        1 << 29,
        weight_a.reshape(27 * chan, width_a),
        grad_hidden,
    )
    own, even_part, odd_part, source_sides = lax.optimization_barrier((own, even_part, odd_part, source_sides))
    sums_a = call(
        lambda *refs: sums_a_kernel(side, plan, *refs),
        [shape((plan.rows_a * slabs, width_a), bf16)] * samples,
        [
            pltpu.VMEM((4, 9 * chan, size), bf16),
            pltpu.VMEM((plan.rows_a * samples * slabs, width_a), f32),
        ],
        1 << 30,
        grad_hidden,
        source,
        *source_sides,
    )
    got_a = sums_a[:1] + [swapped(sums_a[k], "dp", k) for k in range(1, samples)]
    from_even, from_odd = lax.ppermute(even_part, "space", even), lax.ppermute(odd_part, "space", odd)
    totals = call(
        lambda *refs: share_kernel(plan, *refs),
        shape((slabs, plan.rows_b, 128), f32),
        [
            pltpu.VMEM((9 * width_a, samples * small), bf16),
            pltpu.VMEM((slabs * plan.rows_b, 128), f32),
        ],
        1 << 30,
        *early,
        *late,
    )
    got_a, from_even, from_odd = lax.optimization_barrier((got_a, from_even, from_odd))
    far = plan.far
    input_grad = own + jnp.stack(sides(from_even, from_odd)).astype(f32)
    input_grad = input_grad.astype(bf16).transpose(1, 0, 2)[None]
    blocks = call(
        lambda *refs: blocks_kernel(plan, *refs),
        [shape((2, plan.block, 128), bf16)] * far,
        [pltpu.VMEM((plan.rows_a * slabs, 128), f32)],
        1 << 20,
        totals,
        *got_a,
    )
    parts = blocks[:1] + [swapped(blocks[k], "space", k) for k in range(1, far)]
    both = call(near_kernel, shape((2, plan.block, 128), bf16), [], 1 << 20, *parts)
    there = swapped(both, "space", far)
    low, high = call(
        lambda *refs: far_kernel(plan, *refs),
        [shape((2, rows, 128), bf16) for rows in (plan.low, plan.block - plan.low)],
        [],
        1 << 20,
        both,
        there,
    )
    strides = [samples >> k for k in range(1, samples.bit_length())]

    def crossed(parts):
        return [[swapped(part, "dp", stride) for part in parts] for stride in strides[1:]]

    def stacked(parts):
        return call(stack_kernel, shape((2 * len(parts), *parts[0].shape[1:]), bf16), [], 1 << 20, *parts)

    high_hop = swapped(high, "dp", strides[0])
    low_near = [swapped(low, "space", k) for k in range(1, far)]
    low, high, low_near, high_hop = lax.optimization_barrier((low, high, low_near, high_hop))
    low_all = stacked([low, *low_near])
    high_both = stacked([high, high_hop])
    low_hop = swapped(low_all, "dp", strides[0])
    high_near = [swapped(high_both, "space", k) for k in range(1, far)]
    across_first = crossed([low_all, high_both])
    low_hop, high_near, across_first, input_grad = lax.optimization_barrier(
        (low_hop, high_near, across_first, input_grad)
    )
    highs = [high_both, *high_near]
    known = {0: (low_all, low_hop, highs)}
    for stride, (low_there, high_there) in zip(strides[1:], across_first):
        for k in list(known):
            lows, hops, parts = known[k]
            known[k ^ stride] = (
                swapped(lows, "dp", stride) if k else low_there,
                swapped(hops, "dp", stride),
                [swapped(part, "dp", stride) if k or n else high_there for n, part in enumerate(parts)],
            )
    shares = [known[k] for k in sorted(known)]
    planes_a = depth_a * slabs
    total_a, total_b = call(
        lambda *refs: last_kernel(
            plan,
            1.0 / math.sqrt(samples * planes_a * size),
            1.0 / math.sqrt(samples * (planes_a // 2) * small),
            *refs,
        ),
        [shape((27 * chan, width_a), f32), shape((27 * width_a, width_b), f32)],
        [
            pltpu.VMEM((samples, slabs, plan.block, 128), bf16),
            pltpu.VMEM((27 * width_a, width_b), f32),
            pltpu.SemaphoreType.DMA((3 * plan.pieces,)),
        ],
        1 << 20,
        *[part for lows, hops, parts in shares for part in (lows, hops, *parts)],
        out_specs=[vmem, pl.BlockSpec(memory_space=pl.ANY)],
    )
    return (input_grad, total_a.reshape(weight_a.shape), total_b.reshape(weight_b.shape))


def solution(mesh):
    in_specs = (
        P("dp", None, "space", None),
        P("dp", None, "space", None),
        P("dp", None, "space", None),
        P("dp", None, "space", None),
        P(),
        P(),
    )
    out_specs = (P("dp", None, "space", None), P(), P())
    return jax.shard_map(
        per_device, mesh=mesh, in_specs=in_specs, out_specs=out_specs, check_vma=False
    )
```

```python
import math

import jax
import jax.numpy as jnp
from jax import lax
from jax.experimental import pallas as pl
from jax.experimental.pallas import tpu as pltpu
from jax.sharding import PartitionSpec as P

negative_slope = 0.3
f32 = jnp.float32
bf16 = jnp.bfloat16
vmem = pl.BlockSpec(memory_space=pltpu.VMEM)
transposed = (((1,), (1,)), ((), ()))


def shifted(cells, rows, columns, side):
    size = side * side
    offset = rows * side + columns
    if offset:
        cells = pltpu.roll(cells, (-offset) % size, 1)
    place = lax.broadcasted_iota(jnp.int32, cells.shape, 1)
    if rows:
        y = place // side + rows
        cells = jnp.where((y >= 0) & (y < side), cells, 0.0)
    if columns:
        x = place % side + columns
        cells = jnp.where((x >= 0) & (x < side), cells, 0.0)
    return cells


def gathered(parts, side):
    total = None
    for c in range(3):
        line = parts(1, c) + shifted(parts(0, c), 1, 0, side) + shifted(parts(2, c), -1, 0, side)
        line = shifted(line, 0, 1 - c, side)
        total = line if total is None else total + line
    return total


def pool_matrix(side):
    half = side // 2
    fine = lax.broadcasted_iota(jnp.int32, (side * side, half * half), 0)
    coarse = lax.broadcasted_iota(jnp.int32, (side * side, half * half), 1)
    parent = (fine // (2 * side)) * half + (fine % side) // 2
    return jnp.where(parent == coarse, 0.125, 0.0).astype(bf16)


def sides(even_pairs, odd_pairs):
    here = lax.axis_index("space")
    even = here % 2 == 0
    nothing = jnp.zeros(even_pairs.shape, bf16)
    before = jnp.where(here == 0, nothing, jnp.where(even, odd_pairs, even_pairs))
    after = jnp.where(here == lax.axis_size("space") - 1, nothing, jnp.where(even, even_pairs, odd_pairs))
    return before, after


def for_sides(before, after):
    even = lax.axis_index("space") % 2 == 0
    return jnp.where(even, after, before), jnp.where(even, before, after)


def call(kernel, out_shape, scratch, flops, *args, out_specs=None):
    result = pl.pallas_call(
        kernel,
        out_shape=out_shape,
        in_specs=[vmem] * len(args),
        out_specs=out_specs or jax.tree.map(lambda _: vmem, out_shape),
        scratch_shapes=scratch,
        compiler_params=pltpu.CompilerParams(vmem_limit_bytes=48 * 1024 * 1024),
        cost_estimate=pl.CostEstimate(flops=flops, bytes_accessed=2 << 20, transcendentals=0),
    )(*args)
    return list(result) if isinstance(out_shape, list) else result


def pool_kernel(side, hidden, pooled):
    width = hidden.shape[1]
    pool = pool_matrix(side)
    total = None
    for plane in range(2):
        cells = hidden[plane].astype(f32)
        stacked = jnp.concatenate([jnp.maximum(cells, 0.0), jnp.minimum(cells, 0.0)], 0).astype(bf16)
        part = jnp.dot(stacked, pool, preferred_element_type=f32)
        total = part if total is None else total + part
    pooled[...] = (total[:width] + negative_slope * total[width:]).astype(bf16)


def pack_kernel(plan, pooled, grad, even_pairs, odd_pairs, *refs):
    me = lax.axis_index("dp")
    messages, (before, after) = refs[:-2], refs[-2:]
    before[...], after[...] = sides(even_pairs[...], odd_pairs[...])
    for distance, message in enumerate(messages):
        message[: plan.width] = pooled[...]
        start = pl.multiple_of((me ^ distance) * plan.share, plan.share)
        for a, plane in enumerate((after, grad, before)):
            row = plan.width + a * plan.share
            message[row : row + plan.share] = plane[pl.ds(start, plan.share)]


def share_kernel(plan, *refs):
    got, (out, moved, totals) = refs[:-3], refs[-3:]
    size = got[0].shape[1]
    half = math.isqrt(size)
    width, share = plan.width, plan.share
    for k, message in enumerate(got):
        cells = message[:width].astype(f32)
        for tap in range(9):
            moved[tap * width : (tap + 1) * width, k * size : (k + 1) * size] = shifted(
                cells, tap // 3 - 1, tap % 3 - 1, half
            ).astype(bf16)
    right = jnp.concatenate([message[width:] for message in got], 1)
    result = lax.dot_general(moved[...], right, transposed, preferred_element_type=f32)
    for a in range(3):
        pieces = [
            result[k * plan.tall : (k + 1) * plan.tall, a * share : (a + 1) * share] for k in range(plan.pieces)
        ]
        totals[a * plan.tall : (a + 1) * plan.tall] = jnp.concatenate(pieces, 1)
    spare = totals.shape[0] - 3 * plan.tall
    if spare:
        totals[3 * plan.tall :] = jnp.zeros((spare, 128), f32)
    for slab in range(plan.slabs):
        out[slab] = totals[slab * plan.rows_b : (slab + 1) * plan.rows_b]


def blocks_kernel(plan, totals, *refs):
    got, blocks, first = refs[: plan.samples], refs[plan.samples : -1], refs[-1]
    total = got[0][...].astype(f32)
    for message in got[1:]:
        total += message[...].astype(f32)
    first[...] = total
    me = lax.axis_index("space")
    for distance, block in enumerate(blocks):
        for k in range(2):
            slab = me ^ distance ^ (k * plan.far)
            row = pl.multiple_of(slab * plan.rows_a, plan.rows_a)
            parts = [totals[slab], first[pl.ds(row, plan.rows_a)]]
            spare = plan.block - plan.rows_b - plan.rows_a
            if spare:
                parts.append(jnp.zeros((spare, 128), f32))
            block[k] = jnp.concatenate(parts, 0).astype(bf16)


def near_kernel(*refs):
    total = refs[0][...].astype(f32)
    for part in refs[1:-1]:
        total += part[...].astype(f32)
    refs[-1][...] = total.astype(bf16)


def far_kernel(plan, here, there, low, high):
    for k in range(2):
        total = (here[k].astype(f32) + there[1 - k].astype(f32)).astype(bf16)
        low[k], high[k] = total[: plan.low], total[plan.low :]


def stack_kernel(*refs):
    count = refs[0].shape[0]
    for k, part in enumerate(refs[:-1]):
        refs[-1][count * k : count * (k + 1)] = part[...]


def last_kernel(plan, scale_a, scale_b, *refs):
    got, (out_a, out_b, shares, rows, sems) = refs[:-5], refs[-5:]
    me, here = lax.axis_index("dp"), lax.axis_index("space")
    far, groups = plan.far, plan.samples // 2
    each = len(got) // groups
    for group in range(groups):
        lows, hops, *highs = got[group * each : (group + 1) * each]
        for hop in range(2):
            sample = me ^ group ^ (hop * groups)
            for k in range(plan.slabs):
                slab = here ^ (k // 2) ^ (k % 2 * far)
                shares[sample, slab, : plan.low] = (hops if hop else lows)[k]
                shares[sample, slab, plan.low :] = highs[k // 2][2 * hop + k % 2]
    copies = []
    for slab in range(plan.slabs):
        blocks = [shares[sample, slab].astype(f32) for sample in range(plan.samples)]
        for sample, block in enumerate(blocks):
            row = (sample * plan.slabs + slab) * plan.rows_a
            height = min(plan.rows_a, out_a.shape[0] - row)
            if height > 0:
                out_a[row : row + height] = block[plan.rows_b : plan.rows_b + height] * scale_a
        for k in range(plan.pieces):
            lanes = slice(k * plan.share, (k + 1) * plan.share)
            wide = jnp.concatenate([block[: plan.rows_b, lanes] for block in blocks], 1) * scale_b
            start, stop = slab * plan.rows_b, min((slab + 1) * plan.rows_b, 3 * plan.tall)
            while start < stop:
                a = start // plan.tall
                end = min(stop, (a + 1) * plan.tall)
                row = (a * (plan.pieces - 1) + k) * plan.tall + start
                rows[row : row + end - start] = wide[start - slab * plan.rows_b : end - slab * plan.rows_b]
                start = end
        height = plan.pieces * plan.tall
        while len(copies) < 3 and (slab + 1) * plan.rows_b >= (len(copies) + 1) * plan.tall:
            place = pl.ds(len(copies) * height, height)
            copies.append(pltpu.make_async_copy(rows.at[place], out_b.at[place], sems.at[len(copies)]))
            copies[-1].start()
    for copy in copies:
        copy.wait()


class Plan:
    def __init__(self, samples, slabs, chan, width, width_b):
        self.samples, self.slabs, self.width = samples, slabs, width
        self.share = width_b // samples
        self.pieces = 128 // self.share
        self.tall = 9 * width // self.pieces
        self.rows_b = -(-3 * self.tall // (8 * slabs)) * 8
        self.rows_a = -(-27 * chan // (8 * samples * slabs)) * 8
        self.block = -(-(self.rows_b + self.rows_a) // 16) * 16
        self.low = -(-self.block // 32) * 16
        self.far = slabs // 2


def hidden_kernel(side, weight, grad, before, after, hidden, grad_hidden, products):
    half = side // 2
    width = hidden.shape[1]
    block = 9 * width
    products[...] = jnp.dot(weight[:block], after[...], preferred_element_type=f32)
    products[...] += jnp.dot(weight[block : 2 * block], grad[...], preferred_element_type=f32)
    products[...] += jnp.dot(weight[2 * block :], before[...], preferred_element_type=f32)

    def part(b, c):
        tap = 3 * b + c
        return products[tap * width : (tap + 1) * width]

    back = gathered(part, half)
    high = back.astype(bf16)
    low = (back - high.astype(f32)).astype(bf16)
    pool = pool_matrix(side)
    spread = lax.dot_general(high, pool, transposed, preferred_element_type=f32)
    spread += lax.dot_general(low, pool, transposed, preferred_element_type=f32)
    for plane in range(2):
        slope = jnp.where(hidden[plane].astype(f32) > 0, 1.0, negative_slope)
        grad_hidden[plane * width : (plane + 1) * width] = (spread * slope).astype(bf16)


def sums_a_kernel(side, plan, grad_hidden, source, even_pairs, odd_pairs, *refs):
    messages, (moved, sums) = refs[:-2], refs[-2:]
    width = plan.width
    chan = source.shape[1]
    before, after = sides(even_pairs[...], odd_pairs[...])
    for index, plane in enumerate((before, source[0], source[1], after)):
        cells = plane.astype(f32)
        for tap in range(9):
            moved[index, tap * chan : (tap + 1) * chan] = shifted(
                cells, tap // 3 - 1, tap % 3 - 1, side
            ).astype(bf16)
    both = grad_hidden[...]
    outer0 = lax.dot_general(moved[0], both[:width], transposed, preferred_element_type=f32)
    inner0 = lax.dot_general(moved[1], both, transposed, preferred_element_type=f32)
    inner1 = lax.dot_general(moved[2], both, transposed, preferred_element_type=f32)
    outer1 = lax.dot_general(moved[3], both[width:], transposed, preferred_element_type=f32)
    tall = 9 * chan
    sums[:tall] = outer0 + inner0[:, width:]
    sums[tall : 2 * tall] = inner0[:, :width] + inner1[:, width:]
    sums[2 * tall : 3 * tall] = inner1[:, :width] + outer1
    sums[3 * tall :] = jnp.zeros((sums.shape[0] - 3 * tall, width), f32)
    me = lax.axis_index("dp")
    for distance, message in enumerate(messages):
        rows = message.shape[0]
        message[...] = sums[pl.ds(pl.multiple_of((me ^ distance) * rows, rows), rows)].astype(bf16)


def tap_parts(products):
    chan = products.shape[0] // 9

    def part(b, c):
        tap = 3 * b + c
        return products[tap * chan : (tap + 1) * chan]

    return part


def edges_kernel(side, weight, grad_hidden, even_pairs, odd_pairs, products):
    width = weight.shape[1]
    tall = weight.shape[0] // 3
    both = grad_hidden[...]
    products[...] = jnp.dot(weight[:tall], both[:width], preferred_element_type=f32)
    to_before = gathered(tap_parts(products), side).astype(bf16)
    products[...] = jnp.dot(weight[2 * tall :], both[width:], preferred_element_type=f32)
    to_after = gathered(tap_parts(products), side).astype(bf16)
    even_pairs[...], odd_pairs[...] = for_sides(to_before, to_after)


def own_kernel(side, weight, grad_hidden, own, products):
    tall = weight.shape[0] // 3
    both = grad_hidden[...]
    for plane in range(2):
        mixed = jnp.concatenate(
            [weight[(plane + 1) * tall : (plane + 2) * tall], weight[plane * tall : (plane + 1) * tall]], 1
        )
        products[...] = jnp.dot(mixed, both, preferred_element_type=f32)
        own[plane] = gathered(tap_parts(products), side)


def swapped(part, axis, distance):
    return lax.ppermute(part, axis, [(i, i ^ distance) for i in range(lax.axis_size(axis))])


def per_device(layer_input, hidden_pre, output_pre, output_grad, weight_a, weight_b):
    side = math.isqrt(layer_input.shape[3])
    half = side // 2
    size, small = side * side, half * half
    depth_a = layer_input.shape[2]
    samples, slabs = lax.axis_size("dp"), lax.axis_size("space")
    even, odd = (
        [((i + k) % slabs, (i + 1 - k) % slabs) for i in range(start, slabs, 2) for k in range(2)] for start in range(2)
    )
    shape = jax.ShapeDtypeStruct
    outer = output_pre[0, :, 0].astype(f32)
    grad = (output_grad[0, :, 0].astype(f32) * jnp.where(outer > 0, 1.0, negative_slope)).astype(bf16)
    grad, layer_input, hidden_pre = lax.optimization_barrier((grad, layer_input, hidden_pre))
    grad_sides = [lax.ppermute(grad, "space", pairs) for pairs in (even, odd)]
    source = layer_input[0].transpose(1, 0, 2)
    hidden = hidden_pre[0].transpose(1, 0, 2)
    chan = source.shape[1]
    width_a = hidden.shape[1]
    width_b = grad.shape[0]
    plan = Plan(samples, slabs, chan, width_a, width_b)
    pooled = call(lambda *refs: pool_kernel(side, *refs), shape((width_a, small), bf16), [], 1 << 28, hidden)
    source, pooled = lax.optimization_barrier((source, pooled))
    source_sides = [
        lax.ppermute(part, "space", pairs) for part, pairs in zip(for_sides(source[0], source[1]), (even, odd))
    ]
    packed = call(
        lambda *refs: pack_kernel(plan, *refs),
        [shape((plan.width + 3 * plan.share, small), bf16)] * samples + [shape(grad.shape, bf16)] * 2,
        [],
        1 << 20,
        pooled,
        grad,
        *grad_sides,
    )
    packed, (before, after) = packed[:samples], packed[samples:]
    got_b = packed[:1] + [swapped(packed[k], "dp", k) for k in range(1, samples)]
    grad_hidden = call(
        lambda *refs: hidden_kernel(side, *refs),
        shape((2 * width_a, size), bf16),
        [pltpu.VMEM((9 * width_a, small), f32)],
        1 << 30,
        weight_b.reshape(27 * width_a, width_b),
        grad,
        before,
        after,
        hidden,
    )
    edges = call(
        lambda *refs: edges_kernel(side, *refs),
        [shape((chan, size), bf16)] * 2,
        [pltpu.VMEM((9 * chan, size), f32)],
        1 << 28,
        weight_a.reshape(27 * chan, width_a),
        grad_hidden,
    )
    edges, source_sides = lax.optimization_barrier((edges, source_sides))
    from_sides = [lax.ppermute(part, "space", pairs) for part, pairs in zip(edges, (even, odd))]
    sums_a = call(
        lambda *refs: sums_a_kernel(side, plan, *refs),
        [shape((plan.rows_a * slabs, width_a), bf16)] * samples,
        [
            pltpu.VMEM((4, 9 * chan, size), bf16),
            pltpu.VMEM((plan.rows_a * samples * slabs, width_a), f32),
        ],
        1 << 30,
        grad_hidden,
        source,
        *source_sides,
    )
    got_a = sums_a[:1] + [swapped(sums_a[k], "dp", k) for k in range(1, samples)]
    totals = call(
        lambda *refs: share_kernel(plan, *refs),
        shape((slabs, plan.rows_b, 128), f32),
        [
            pltpu.VMEM((9 * width_a, samples * small), bf16),
            pltpu.VMEM((slabs * plan.rows_b, 128), f32),
        ],
        1 << 30,
        *got_b,
    )
    totals, grad_hidden = lax.optimization_barrier((totals, grad_hidden))
    own = call(
        lambda *refs: own_kernel(side, *refs),
        shape((2, chan, size), f32),
        [pltpu.VMEM((9 * chan, size), f32)],
        1 << 28,
        weight_a.reshape(27 * chan, width_a),
        grad_hidden,
    )
    got_a, own, from_sides = lax.optimization_barrier((got_a, own, from_sides))
    far = plan.far
    blocks = call(
        lambda *refs: blocks_kernel(plan, *refs),
        [shape((2, plan.block, 128), bf16)] * far,
        [pltpu.VMEM((plan.rows_a * slabs, 128), f32)],
        1 << 20,
        totals,
        *got_a,
    )
    parts = blocks[:1] + [swapped(blocks[k], "space", k) for k in range(1, far)]
    input_grad = own + jnp.stack(sides(*from_sides)).astype(f32)
    input_grad = input_grad.astype(bf16).transpose(1, 0, 2)[None]
    both = call(near_kernel, shape((2, plan.block, 128), bf16), [], 1 << 20, *parts)
    there = swapped(both, "space", far)
    low, high = call(
        lambda *refs: far_kernel(plan, *refs),
        [shape((2, rows, 128), bf16) for rows in (plan.low, plan.block - plan.low)],
        [],
        1 << 20,
        both,
        there,
    )
    strides = [samples >> k for k in range(1, samples.bit_length())]

    def crossed(parts):
        return [[swapped(part, "dp", stride) for part in parts] for stride in strides[1:]]

    def stacked(parts):
        return call(stack_kernel, shape((2 * len(parts), *parts[0].shape[1:]), bf16), [], 1 << 20, *parts)

    high_hop = swapped(high, "dp", strides[0])
    low_near = [swapped(low, "space", k) for k in range(1, far)]
    low, high, low_near, high_hop = lax.optimization_barrier((low, high, low_near, high_hop))
    low_all = stacked([low, *low_near])
    high_both = stacked([high, high_hop])
    low_hop = swapped(low_all, "dp", strides[0])
    high_near = [swapped(high_both, "space", k) for k in range(1, far)]
    first_near, low_early, high_early = lax.optimization_barrier((high_near[0], low_all, high_both))
    high_near[0] = first_near
    across_first = crossed([low_early, high_early])
    low_hop, high_near, across_first, input_grad = lax.optimization_barrier(
        (low_hop, high_near, across_first, input_grad)
    )
    highs = [high_both, *high_near]
    known = {0: (low_all, low_hop, highs)}
    for stride, (low_there, high_there) in zip(strides[1:], across_first):
        for k in list(known):
            lows, hops, parts = known[k]
            known[k ^ stride] = (
                swapped(lows, "dp", stride) if k else low_there,
                swapped(hops, "dp", stride),
                [swapped(part, "dp", stride) if k or n else high_there for n, part in enumerate(parts)],
            )
    shares = [known[k] for k in sorted(known)]
    planes_a = depth_a * slabs
    total_a, total_b = call(
        lambda *refs: last_kernel(
            plan,
            1.0 / math.sqrt(samples * planes_a * size),
            1.0 / math.sqrt(samples * (planes_a // 2) * small),
            *refs,
        ),
        [shape((27 * chan, width_a), f32), shape((27 * width_a, width_b), f32)],
        [
            pltpu.VMEM((samples, slabs, plan.block, 128), bf16),
            pltpu.VMEM((27 * width_a, width_b), f32),
            pltpu.SemaphoreType.DMA((3 * plan.pieces,)),
        ],
        1 << 20,
        *[part for lows, hops, parts in shares for part in (lows, hops, *parts)],
        out_specs=[vmem, pl.BlockSpec(memory_space=pl.ANY)],
    )
    return (input_grad, total_a.reshape(weight_a.shape), total_b.reshape(weight_b.shape))


def solution(mesh):
    in_specs = (
        P("dp", None, "space", None),
        P("dp", None, "space", None),
        P("dp", None, "space", None),
        P("dp", None, "space", None),
        P(),
        P(),
    )
    out_specs = (P("dp", None, "space", None), P(), P())
    return jax.shard_map(
        per_device, mesh=mesh, in_specs=in_specs, out_specs=out_specs, check_vma=False
    )
```

```python
import math

import jax
import jax.numpy as jnp
from jax import lax
from jax.experimental import pallas as pl
from jax.experimental.pallas import tpu as pltpu
from jax.sharding import PartitionSpec as P

negative_slope = 0.3
f32 = jnp.float32
bf16 = jnp.bfloat16
vmem = pl.BlockSpec(memory_space=pltpu.VMEM)
transposed = (((1,), (1,)), ((), ()))


def shifted(cells, rows, columns, side):
    size = side * side
    offset = rows * side + columns
    if offset:
        cells = pltpu.roll(cells, (-offset) % size, 1)
    place = lax.broadcasted_iota(jnp.int32, cells.shape, 1)
    if rows:
        y = place // side + rows
        cells = jnp.where((y >= 0) & (y < side), cells, 0.0)
    if columns:
        x = place % side + columns
        cells = jnp.where((x >= 0) & (x < side), cells, 0.0)
    return cells


def gathered(parts, side):
    total = None
    for c in range(3):
        line = parts(1, c) + shifted(parts(0, c), 1, 0, side) + shifted(parts(2, c), -1, 0, side)
        line = shifted(line, 0, 1 - c, side)
        total = line if total is None else total + line
    return total


def pool_matrix(side):
    half = side // 2
    fine = lax.broadcasted_iota(jnp.int32, (side * side, half * half), 0)
    coarse = lax.broadcasted_iota(jnp.int32, (side * side, half * half), 1)
    parent = (fine // (2 * side)) * half + (fine % side) // 2
    return jnp.where(parent == coarse, 0.125, 0.0).astype(bf16)


def sides(even_pairs, odd_pairs):
    here = lax.axis_index("space")
    even = here % 2 == 0
    nothing = jnp.zeros(even_pairs.shape, bf16)
    before = jnp.where(here == 0, nothing, jnp.where(even, odd_pairs, even_pairs))
    after = jnp.where(here == lax.axis_size("space") - 1, nothing, jnp.where(even, even_pairs, odd_pairs))
    return before, after


def for_sides(before, after):
    even = lax.axis_index("space") % 2 == 0
    return jnp.where(even, after, before), jnp.where(even, before, after)


def call(kernel, out_shape, scratch, flops, *args, out_specs=None):
    result = pl.pallas_call(
        kernel,
        out_shape=out_shape,
        in_specs=[vmem] * len(args),
        out_specs=out_specs or jax.tree.map(lambda _: vmem, out_shape),
        scratch_shapes=scratch,
        compiler_params=pltpu.CompilerParams(vmem_limit_bytes=48 * 1024 * 1024),
        cost_estimate=pl.CostEstimate(flops=flops, bytes_accessed=2 << 20, transcendentals=0),
    )(*args)
    return list(result) if isinstance(out_shape, list) else result


def pool_kernel(side, hidden, pooled):
    width = hidden.shape[1]
    pool = pool_matrix(side)
    total = None
    for plane in range(2):
        cells = hidden[plane].astype(f32)
        stacked = jnp.concatenate([jnp.maximum(cells, 0.0), jnp.minimum(cells, 0.0)], 0).astype(bf16)
        part = jnp.dot(stacked, pool, preferred_element_type=f32)
        total = part if total is None else total + part
    pooled[...] = (total[:width] + negative_slope * total[width:]).astype(bf16)


def pack_kernel(plan, pooled, grad, even_pairs, odd_pairs, *refs):
    me = lax.axis_index("dp")
    messages, (before, after) = refs[:-2], refs[-2:]
    before[...], after[...] = sides(even_pairs[...], odd_pairs[...])
    for distance, message in enumerate(messages):
        message[: plan.width] = pooled[...]
        start = pl.multiple_of((me ^ distance) * plan.share, plan.share)
        for a, plane in enumerate((after, grad, before)):
            row = plan.width + a * plan.share
            message[row : row + plan.share] = plane[pl.ds(start, plan.share)]


def share_kernel(plan, *refs):
    got, (out, moved, totals) = refs[:-3], refs[-3:]
    size = got[0].shape[1]
    half = math.isqrt(size)
    width, share = plan.width, plan.share
    for k, message in enumerate(got):
        cells = message[:width].astype(f32)
        for tap in range(9):
            moved[tap * width : (tap + 1) * width, k * size : (k + 1) * size] = shifted(
                cells, tap // 3 - 1, tap % 3 - 1, half
            ).astype(bf16)
    right = jnp.concatenate([message[width:] for message in got], 1)
    result = lax.dot_general(moved[...], right, transposed, preferred_element_type=f32)
    for a in range(3):
        pieces = [
            result[k * plan.tall : (k + 1) * plan.tall, a * share : (a + 1) * share] for k in range(plan.pieces)
        ]
        totals[a * plan.tall : (a + 1) * plan.tall] = jnp.concatenate(pieces, 1)
    spare = totals.shape[0] - 3 * plan.tall
    if spare:
        totals[3 * plan.tall :] = jnp.zeros((spare, 128), f32)
    for slab in range(plan.slabs):
        out[slab] = totals[slab * plan.rows_b : (slab + 1) * plan.rows_b]


def blocks_kernel(plan, totals, *refs):
    got, blocks, first = refs[: plan.samples], refs[plan.samples : -1], refs[-1]
    total = got[0][...].astype(f32)
    for message in got[1:]:
        total += message[...].astype(f32)
    first[...] = total
    me = lax.axis_index("space")
    for distance, block in enumerate(blocks):
        for k in range(2):
            slab = me ^ distance ^ (k * plan.far)
            row = pl.multiple_of(slab * plan.rows_a, plan.rows_a)
            parts = [totals[slab], first[pl.ds(row, plan.rows_a)]]
            spare = plan.block - plan.rows_b - plan.rows_a
            if spare:
                parts.append(jnp.zeros((spare, 128), f32))
            block[k] = jnp.concatenate(parts, 0).astype(bf16)


def near_kernel(*refs):
    total = refs[0][...].astype(f32)
    for part in refs[1:-1]:
        total += part[...].astype(f32)
    refs[-1][...] = total.astype(bf16)


def far_kernel(plan, here, there, low, high):
    for k in range(2):
        total = (here[k].astype(f32) + there[1 - k].astype(f32)).astype(bf16)
        low[k], high[k] = total[: plan.low], total[plan.low :]


def stack_kernel(*refs):
    count = refs[0].shape[0]
    for k, part in enumerate(refs[:-1]):
        refs[-1][count * k : count * (k + 1)] = part[...]


def last_kernel(plan, scale_a, scale_b, *refs):
    got, (out_a, out_b, shares, rows_a, rows, sems) = refs[:-6], refs[-6:]
    me, here = lax.axis_index("dp"), lax.axis_index("space")
    far, groups = plan.far, plan.samples // 2
    each = len(got) // groups
    for group in range(groups):
        lows, hops, *highs = got[group * each : (group + 1) * each]
        for hop in range(2):
            sample = me ^ group ^ (hop * groups)
            for k in range(plan.slabs):
                slab = here ^ (k // 2) ^ (k % 2 * far)
                shares[sample, slab, : plan.low] = (hops if hop else lows)[k]
                shares[sample, slab, plan.low :] = highs[k // 2][2 * hop + k % 2]
    for sample in range(plan.samples):
        for slab in range(plan.slabs):
            row = (sample * plan.slabs + slab) * plan.rows_a
            height = min(plan.rows_a, out_a.shape[0] - row)
            if height > 0:
                base = plan.rows_b // 16 * 16
                block = shares[sample, slab, base:].astype(f32)[plan.rows_b - base :]
                rows_a[row : row + height] = block[:height] * scale_a
    copy_a = pltpu.make_async_copy(rows_a, out_a, sems.at[3])
    copy_a.start()
    copies = []
    for slab in range(plan.slabs):
        blocks = [shares[sample, slab].astype(f32) for sample in range(plan.samples)]
        for k in range(plan.pieces):
            lanes = slice(k * plan.share, (k + 1) * plan.share)
            wide = jnp.concatenate([block[: plan.rows_b, lanes] for block in blocks], 1) * scale_b
            start, stop = slab * plan.rows_b, min((slab + 1) * plan.rows_b, 3 * plan.tall)
            while start < stop:
                a = start // plan.tall
                end = min(stop, (a + 1) * plan.tall)
                row = (a * (plan.pieces - 1) + k) * plan.tall + start
                rows[row : row + end - start] = wide[start - slab * plan.rows_b : end - slab * plan.rows_b]
                start = end
        height = plan.pieces * plan.tall
        while len(copies) < 3 and (slab + 1) * plan.rows_b >= (len(copies) + 1) * plan.tall:
            place = pl.ds(len(copies) * height, height)
            copies.append(pltpu.make_async_copy(rows.at[place], out_b.at[place], sems.at[len(copies)]))
            copies[-1].start()
    for copy in (copy_a, *copies):
        copy.wait()


class Plan:
    def __init__(self, samples, slabs, chan, width, width_b):
        self.samples, self.slabs, self.width = samples, slabs, width
        self.share = width_b // samples
        self.pieces = 128 // self.share
        self.tall = 9 * width // self.pieces
        self.rows_b = -(-3 * self.tall // (8 * slabs)) * 8
        self.rows_a = -(-27 * chan // (8 * samples * slabs)) * 8
        self.block = -(-(self.rows_b + self.rows_a) // 16) * 16
        self.low = -(-self.block // 32) * 16
        self.far = slabs // 2


def hidden_kernel(side, weight, grad, before, after, hidden, grad_hidden, products):
    half = side // 2
    width = hidden.shape[1]
    block = 9 * width
    products[...] = jnp.dot(weight[:block], after[...], preferred_element_type=f32)
    products[...] += jnp.dot(weight[block : 2 * block], grad[...], preferred_element_type=f32)
    products[...] += jnp.dot(weight[2 * block :], before[...], preferred_element_type=f32)

    def part(b, c):
        tap = 3 * b + c
        return products[tap * width : (tap + 1) * width]

    back = gathered(part, half)
    high = back.astype(bf16)
    low = (back - high.astype(f32)).astype(bf16)
    pool = pool_matrix(side)
    spread = lax.dot_general(high, pool, transposed, preferred_element_type=f32)
    spread += lax.dot_general(low, pool, transposed, preferred_element_type=f32)
    for plane in range(2):
        slope = jnp.where(hidden[plane].astype(f32) > 0, 1.0, negative_slope)
        grad_hidden[plane * width : (plane + 1) * width] = (spread * slope).astype(bf16)


def sums_a_kernel(side, plan, grad_hidden, source, even_pairs, odd_pairs, *refs):
    messages, (moved, sums) = refs[:-2], refs[-2:]
    width = plan.width
    chan = source.shape[1]
    before, after = sides(even_pairs[...], odd_pairs[...])
    for index, plane in enumerate((before, source[0], source[1], after)):
        cells = plane.astype(f32)
        for tap in range(9):
            moved[index, tap * chan : (tap + 1) * chan] = shifted(
                cells, tap // 3 - 1, tap % 3 - 1, side
            ).astype(bf16)
    both = grad_hidden[...]
    outer0 = lax.dot_general(moved[0], both[:width], transposed, preferred_element_type=f32)
    inner0 = lax.dot_general(moved[1], both, transposed, preferred_element_type=f32)
    inner1 = lax.dot_general(moved[2], both, transposed, preferred_element_type=f32)
    outer1 = lax.dot_general(moved[3], both[width:], transposed, preferred_element_type=f32)
    tall = 9 * chan
    sums[:tall] = outer0 + inner0[:, width:]
    sums[tall : 2 * tall] = inner0[:, :width] + inner1[:, width:]
    sums[2 * tall : 3 * tall] = inner1[:, :width] + outer1
    sums[3 * tall :] = jnp.zeros((sums.shape[0] - 3 * tall, width), f32)
    me = lax.axis_index("dp")
    for distance, message in enumerate(messages):
        rows = message.shape[0]
        message[...] = sums[pl.ds(pl.multiple_of((me ^ distance) * rows, rows), rows)].astype(bf16)


def tap_parts(products):
    chan = products.shape[0] // 9

    def part(b, c):
        tap = 3 * b + c
        return products[tap * chan : (tap + 1) * chan]

    return part


def edges_kernel(side, weight, grad_hidden, even_pairs, odd_pairs, products):
    width = weight.shape[1]
    tall = weight.shape[0] // 3
    both = grad_hidden[...]
    products[...] = jnp.dot(weight[:tall], both[:width], preferred_element_type=f32)
    to_before = gathered(tap_parts(products), side).astype(bf16)
    products[...] = jnp.dot(weight[2 * tall :], both[width:], preferred_element_type=f32)
    to_after = gathered(tap_parts(products), side).astype(bf16)
    even_pairs[...], odd_pairs[...] = for_sides(to_before, to_after)


def own_kernel(side, weight, grad_hidden, own, products):
    tall = weight.shape[0] // 3
    both = grad_hidden[...]
    for plane in range(2):
        mixed = jnp.concatenate(
            [weight[(plane + 1) * tall : (plane + 2) * tall], weight[plane * tall : (plane + 1) * tall]], 1
        )
        products[...] = jnp.dot(mixed, both, preferred_element_type=f32)
        own[plane] = gathered(tap_parts(products), side)


def swapped(part, axis, distance):
    return lax.ppermute(part, axis, [(i, i ^ distance) for i in range(lax.axis_size(axis))])


def per_device(layer_input, hidden_pre, output_pre, output_grad, weight_a, weight_b):
    side = math.isqrt(layer_input.shape[3])
    half = side // 2
    size, small = side * side, half * half
    depth_a = layer_input.shape[2]
    samples, slabs = lax.axis_size("dp"), lax.axis_size("space")
    even = [(i, i ^ 1) for i in range(slabs)]
    odd = [(i, (i + 1 ^ 1) - 1 if 0 < i < slabs - 1 else i) for i in range(slabs)]
    shape = jax.ShapeDtypeStruct
    outer = output_pre[0, :, 0].astype(f32)
    grad = (output_grad[0, :, 0].astype(f32) * jnp.where(outer > 0, 1.0, negative_slope)).astype(bf16)
    grad, layer_input, hidden_pre = lax.optimization_barrier((grad, layer_input, hidden_pre))
    grad_sides = [lax.ppermute(grad, "space", pairs) for pairs in (even, odd)]
    source = layer_input[0].transpose(1, 0, 2)
    hidden = hidden_pre[0].transpose(1, 0, 2)
    chan = source.shape[1]
    width_a = hidden.shape[1]
    width_b = grad.shape[0]
    plan = Plan(samples, slabs, chan, width_a, width_b)
    pooled = call(lambda *refs: pool_kernel(side, *refs), shape((width_a, small), bf16), [], 1 << 28, hidden)
    source, pooled = lax.optimization_barrier((source, pooled))
    source_sides = [
        lax.ppermute(part, "space", pairs) for part, pairs in zip(for_sides(source[0], source[1]), (even, odd))
    ]
    packed = call(
        lambda *refs: pack_kernel(plan, *refs),
        [shape((plan.width + 3 * plan.share, small), bf16)] * samples + [shape(grad.shape, bf16)] * 2,
        [],
        1 << 20,
        pooled,
        grad,
        *grad_sides,
    )
    packed, (before, after) = packed[:samples], packed[samples:]
    got_b = packed[:1] + [swapped(packed[k], "dp", k) for k in range(1, samples)]
    grad_hidden = call(
        lambda *refs: hidden_kernel(side, *refs),
        shape((2 * width_a, size), bf16),
        [pltpu.VMEM((9 * width_a, small), f32)],
        1 << 30,
        weight_b.reshape(27 * width_a, width_b),
        grad,
        before,
        after,
        hidden,
    )
    sums_a = call(
        lambda *refs: sums_a_kernel(side, plan, *refs),
        [shape((plan.rows_a * slabs, width_a), bf16)] * samples,
        [
            pltpu.VMEM((4, 9 * chan, size), bf16),
            pltpu.VMEM((plan.rows_a * samples * slabs, width_a), f32),
        ],
        1 << 30,
        grad_hidden,
        source,
        *source_sides,
    )
    sums_a, grad_hidden = lax.optimization_barrier((sums_a, grad_hidden))
    got_a = sums_a[:1] + [swapped(sums_a[k], "dp", k) for k in range(1, samples)]
    edges = call(
        lambda *refs: edges_kernel(side, *refs),
        [shape((chan, size), bf16)] * 2,
        [pltpu.VMEM((9 * chan, size), f32)],
        1 << 28,
        weight_a.reshape(27 * chan, width_a),
        grad_hidden,
    )
    from_odd = lax.ppermute(edges[1], "space", odd)
    totals = call(
        lambda *refs: share_kernel(plan, *refs),
        shape((slabs, plan.rows_b, 128), f32),
        [
            pltpu.VMEM((9 * width_a, samples * small), bf16),
            pltpu.VMEM((slabs * plan.rows_b, 128), f32),
        ],
        1 << 30,
        *got_b,
    )
    totals, grad_hidden = lax.optimization_barrier((totals, grad_hidden))
    own = call(
        lambda *refs: own_kernel(side, *refs),
        shape((2, chan, size), f32),
        [pltpu.VMEM((9 * chan, size), f32)],
        1 << 28,
        weight_a.reshape(27 * chan, width_a),
        grad_hidden,
    )
    got_a, own, from_odd = lax.optimization_barrier((got_a, own, from_odd))
    far = plan.far
    blocks = call(
        lambda *refs: blocks_kernel(plan, *refs),
        [shape((2, plan.block, 128), bf16)] * far,
        [pltpu.VMEM((plan.rows_a * slabs, 128), f32)],
        1 << 20,
        totals,
        *got_a,
    )
    parts = blocks[:1] + [swapped(blocks[k], "space", k) for k in range(1, far)]
    both = call(near_kernel, shape((2, plan.block, 128), bf16), [], 1 << 20, *parts)
    there = swapped(both, "space", far)
    both, even_edge = lax.optimization_barrier((both, edges[0]))
    from_even = lax.ppermute(even_edge, "space", even)
    there, from_even = lax.optimization_barrier((there, from_even))
    input_grad = own + jnp.stack(sides(from_even, from_odd)).astype(f32)
    input_grad = input_grad.astype(bf16).transpose(1, 0, 2)[None]
    low, high = call(
        lambda *refs: far_kernel(plan, *refs),
        [shape((2, rows, 128), bf16) for rows in (plan.low, plan.block - plan.low)],
        [],
        1 << 20,
        both,
        there,
    )
    strides = [samples >> k for k in range(1, samples.bit_length())]

    def crossed(parts):
        return [[swapped(part, "dp", stride) for part in parts] for stride in strides[1:]]

    def stacked(parts):
        return call(stack_kernel, shape((2 * len(parts), *parts[0].shape[1:]), bf16), [], 1 << 20, *parts)

    high_hop = swapped(high, "dp", strides[0])
    low_near = [swapped(low, "space", k) for k in range(1, far)]
    low, high, low_near, high_hop = lax.optimization_barrier((low, high, low_near, high_hop))
    low_all = stacked([low, *low_near])
    high_both = stacked([high, high_hop])
    low_hop = swapped(low_all, "dp", strides[0])
    high_near = [swapped(high_both, "space", k) for k in range(1, far)]
    across_first = crossed([low_all, high_both])
    low_hop, high_near, across_first, input_grad = lax.optimization_barrier(
        (low_hop, high_near, across_first, input_grad)
    )
    highs = [high_both, *high_near]
    known = {0: (low_all, low_hop, highs)}
    for stride, (low_there, high_there) in zip(strides[1:], across_first):
        for k in list(known):
            lows, hops, parts = known[k]
            known[k ^ stride] = (
                swapped(lows, "dp", stride) if k else low_there,
                swapped(hops, "dp", stride),
                [swapped(part, "dp", stride) if k or n else high_there for n, part in enumerate(parts)],
            )
    shares = [known[k] for k in sorted(known)]
    planes_a = depth_a * slabs
    total_a, total_b = call(
        lambda *refs: last_kernel(
            plan,
            1.0 / math.sqrt(samples * planes_a * size),
            1.0 / math.sqrt(samples * (planes_a // 2) * small),
            *refs,
        ),
        [shape((27 * chan, width_a), f32), shape((27 * width_a, width_b), f32)],
        [
            pltpu.VMEM((samples, slabs, plan.block, 128), bf16),
            pltpu.VMEM((27 * chan, width_a), f32),
            pltpu.VMEM((27 * width_a, width_b), f32),
            pltpu.SemaphoreType.DMA((4,)),
        ],
        1 << 20,
        *[part for lows, hops, parts in shares for part in (lows, hops, *parts)],
        out_specs=[pl.BlockSpec(memory_space=pl.ANY)] * 2,
    )
    return (input_grad, total_a.reshape(weight_a.shape), total_b.reshape(weight_b.shape))


def solution(mesh):
    in_specs = (
        P("dp", None, "space", None),
        P("dp", None, "space", None),
        P("dp", None, "space", None),
        P("dp", None, "space", None),
        P(),
        P(),
    )
    out_specs = (P("dp", None, "space", None), P(), P())
    return jax.shard_map(
        per_device, mesh=mesh, in_specs=in_specs, out_specs=out_specs, check_vma=False
    )
```

```python
import math

import jax
import jax.numpy as jnp
from jax import lax
from jax.experimental import pallas as pl
from jax.experimental.pallas import tpu as pltpu
from jax.sharding import PartitionSpec as P

negative_slope = 0.3
f32 = jnp.float32
bf16 = jnp.bfloat16
vmem = pl.BlockSpec(memory_space=pltpu.VMEM)
transposed = (((1,), (1,)), ((), ()))


def shifted(cells, rows, columns, side):
    size = side * side
    offset = rows * side + columns
    if offset:
        cells = pltpu.roll(cells, (-offset) % size, 1)
    place = lax.broadcasted_iota(jnp.int32, cells.shape, 1)
    if rows:
        y = place // side + rows
        cells = jnp.where((y >= 0) & (y < side), cells, 0.0)
    if columns:
        x = place % side + columns
        cells = jnp.where((x >= 0) & (x < side), cells, 0.0)
    return cells


def gathered(parts, side):
    total = None
    for c in range(3):
        line = parts(1, c) + shifted(parts(0, c), 1, 0, side) + shifted(parts(2, c), -1, 0, side)
        line = shifted(line, 0, 1 - c, side)
        total = line if total is None else total + line
    return total


def pool_matrix(side):
    half = side // 2
    fine = lax.broadcasted_iota(jnp.int32, (side * side, half * half), 0)
    coarse = lax.broadcasted_iota(jnp.int32, (side * side, half * half), 1)
    parent = (fine // (2 * side)) * half + (fine % side) // 2
    return jnp.where(parent == coarse, 0.125, 0.0).astype(bf16)


def sides(even_pairs, odd_pairs):
    here = lax.axis_index("space")
    even = here % 2 == 0
    nothing = jnp.zeros(even_pairs.shape, bf16)
    before = jnp.where(here == 0, nothing, jnp.where(even, odd_pairs, even_pairs))
    after = jnp.where(here == lax.axis_size("space") - 1, nothing, jnp.where(even, even_pairs, odd_pairs))
    return before, after


def for_sides(before, after):
    even = lax.axis_index("space") % 2 == 0
    return jnp.where(even, after, before), jnp.where(even, before, after)


def call(kernel, out_shape, scratch, flops, *args, out_specs=None):
    result = pl.pallas_call(
        kernel,
        out_shape=out_shape,
        in_specs=[vmem] * len(args),
        out_specs=out_specs or jax.tree.map(lambda _: vmem, out_shape),
        scratch_shapes=scratch,
        compiler_params=pltpu.CompilerParams(vmem_limit_bytes=48 * 1024 * 1024),
        cost_estimate=pl.CostEstimate(flops=flops, bytes_accessed=2 << 20, transcendentals=0),
    )(*args)
    return list(result) if isinstance(out_shape, list) else result


def pool_kernel(side, hidden, pooled):
    width = hidden.shape[1]
    pool = pool_matrix(side)
    total = None
    for plane in range(2):
        cells = hidden[plane].astype(f32)
        stacked = jnp.concatenate([jnp.maximum(cells, 0.0), jnp.minimum(cells, 0.0)], 0).astype(bf16)
        part = jnp.dot(stacked, pool, preferred_element_type=f32)
        total = part if total is None else total + part
    pooled[...] = (total[:width] + negative_slope * total[width:]).astype(bf16)


def pack_kernel(plan, pooled, grad, even_pairs, odd_pairs, *refs):
    me = lax.axis_index("dp")
    messages, (before, after) = refs[:-2], refs[-2:]
    before[...], after[...] = sides(even_pairs[...], odd_pairs[...])
    for distance, message in enumerate(messages):
        message[: plan.width] = pooled[...]
        start = pl.multiple_of((me ^ distance) * plan.share, plan.share)
        for a, plane in enumerate((after, grad, before)):
            row = plan.width + a * plan.share
            message[row : row + plan.share] = plane[pl.ds(start, plan.share)]


def share_kernel(plan, *refs):
    got, (out, moved, totals) = refs[:-3], refs[-3:]
    size = got[0].shape[1]
    half = math.isqrt(size)
    width, share = plan.width, plan.share
    for k, message in enumerate(got):
        cells = message[:width].astype(f32)
        for tap in range(9):
            moved[tap * width : (tap + 1) * width, k * size : (k + 1) * size] = shifted(
                cells, tap // 3 - 1, tap % 3 - 1, half
            ).astype(bf16)
    right = jnp.concatenate([message[width:] for message in got], 1)
    result = lax.dot_general(moved[...], right, transposed, preferred_element_type=f32)
    for a in range(3):
        pieces = [
            result[k * plan.tall : (k + 1) * plan.tall, a * share : (a + 1) * share] for k in range(plan.pieces)
        ]
        totals[a * plan.tall : (a + 1) * plan.tall] = jnp.concatenate(pieces, 1)
    spare = totals.shape[0] - 3 * plan.tall
    if spare:
        totals[3 * plan.tall :] = jnp.zeros((spare, 128), f32)
    for slab in range(plan.slabs):
        out[slab] = totals[slab * plan.rows_b : (slab + 1) * plan.rows_b]


def blocks_kernel(plan, totals, *refs):
    got, blocks, first = refs[: plan.samples], refs[plan.samples : -1], refs[-1]
    total = got[0][...].astype(f32)
    for message in got[1:]:
        total += message[...].astype(f32)
    first[...] = total
    me = lax.axis_index("space")
    for distance, block in enumerate(blocks):
        for k in range(2):
            slab = me ^ distance ^ (k * plan.far)
            row = pl.multiple_of(slab * plan.rows_a, plan.rows_a)
            parts = [totals[slab], first[pl.ds(row, plan.rows_a)]]
            spare = plan.block - plan.rows_b - plan.rows_a
            if spare:
                parts.append(jnp.zeros((spare, 128), f32))
            block[k] = jnp.concatenate(parts, 0).astype(bf16)


def near_kernel(*refs):
    total = refs[0][...].astype(f32)
    for part in refs[1:-1]:
        total += part[...].astype(f32)
    refs[-1][...] = total.astype(bf16)


def far_kernel(plan, here, there, low, high):
    for k in range(2):
        total = (here[k].astype(f32) + there[1 - k].astype(f32)).astype(bf16)
        low[k], high[k] = total[: plan.low], total[plan.low :]


def stack_kernel(*refs):
    count = refs[0].shape[0]
    for k, part in enumerate(refs[:-1]):
        refs[-1][count * k : count * (k + 1)] = part[...]


def last_kernel(plan, scale_a, scale_b, *refs):
    got, (out_a, out_b, shares, rows_a, rows, sems) = refs[:-6], refs[-6:]
    me, here = lax.axis_index("dp"), lax.axis_index("space")
    far, groups = plan.far, plan.samples // 2
    each = len(got) // groups
    for group in range(groups):
        lows, hops, *highs = got[group * each : (group + 1) * each]
        for hop in range(2):
            sample = me ^ group ^ (hop * groups)
            for k in range(plan.slabs):
                slab = here ^ (k // 2) ^ (k % 2 * far)
                shares[sample, slab, : plan.low] = (hops if hop else lows)[k]
                shares[sample, slab, plan.low :] = highs[k // 2][2 * hop + k % 2]
    for sample in range(plan.samples):
        for slab in range(plan.slabs):
            row = (sample * plan.slabs + slab) * plan.rows_a
            height = min(plan.rows_a, out_a.shape[0] - row)
            if height > 0:
                base = plan.rows_b // 16 * 16
                block = shares[sample, slab, base:].astype(f32)[plan.rows_b - base :]
                rows_a[row : row + height] = block[:height] * scale_a
    copy_a = pltpu.make_async_copy(rows_a, out_a, sems.at[3])
    copy_a.start()
    copies = []
    for slab in range(plan.slabs):
        blocks = [shares[sample, slab].astype(f32) for sample in range(plan.samples)]
        for k in range(plan.pieces):
            lanes = slice(k * plan.share, (k + 1) * plan.share)
            wide = jnp.concatenate([block[: plan.rows_b, lanes] for block in blocks], 1) * scale_b
            start, stop = slab * plan.rows_b, min((slab + 1) * plan.rows_b, 3 * plan.tall)
            while start < stop:
                a = start // plan.tall
                end = min(stop, (a + 1) * plan.tall)
                row = (a * (plan.pieces - 1) + k) * plan.tall + start
                rows[row : row + end - start] = wide[start - slab * plan.rows_b : end - slab * plan.rows_b]
                start = end
        height = plan.pieces * plan.tall
        while len(copies) < 3 and (slab + 1) * plan.rows_b >= (len(copies) + 1) * plan.tall:
            place = pl.ds(len(copies) * height, height)
            copies.append(pltpu.make_async_copy(rows.at[place], out_b.at[place], sems.at[len(copies)]))
            copies[-1].start()
    for copy in (copy_a, *copies):
        copy.wait()


class Plan:
    def __init__(self, samples, slabs, chan, width, width_b):
        self.samples, self.slabs, self.width = samples, slabs, width
        self.share = width_b // samples
        self.pieces = 128 // self.share
        self.tall = 9 * width // self.pieces
        self.rows_b = -(-3 * self.tall // (8 * slabs)) * 8
        self.rows_a = -(-27 * chan // (8 * samples * slabs)) * 8
        self.block = -(-(self.rows_b + self.rows_a) // 16) * 16
        self.low = -(-self.block // 32) * 16
        self.far = slabs // 2


def hidden_kernel(side, weight, grad, before, after, hidden, grad_hidden, products):
    half = side // 2
    width = hidden.shape[1]
    block = 9 * width
    products[...] = jnp.dot(weight[:block], after[...], preferred_element_type=f32)
    products[...] += jnp.dot(weight[block : 2 * block], grad[...], preferred_element_type=f32)
    products[...] += jnp.dot(weight[2 * block :], before[...], preferred_element_type=f32)

    def part(b, c):
        tap = 3 * b + c
        return products[tap * width : (tap + 1) * width]

    back = gathered(part, half)
    high = back.astype(bf16)
    low = (back - high.astype(f32)).astype(bf16)
    pool = pool_matrix(side)
    spread = lax.dot_general(high, pool, transposed, preferred_element_type=f32)
    spread += lax.dot_general(low, pool, transposed, preferred_element_type=f32)
    for plane in range(2):
        slope = jnp.where(hidden[plane].astype(f32) > 0, 1.0, negative_slope)
        grad_hidden[plane * width : (plane + 1) * width] = (spread * slope).astype(bf16)


def sums_a_kernel(side, plan, grad_hidden, source, even_pairs, odd_pairs, *refs):
    messages, (moved, sums) = refs[:-2], refs[-2:]
    width = plan.width
    chan = source.shape[1]
    before, after = sides(even_pairs[...], odd_pairs[...])
    for index, plane in enumerate((before, source[0], source[1], after)):
        cells = plane.astype(f32)
        for tap in range(9):
            moved[index, tap * chan : (tap + 1) * chan] = shifted(
                cells, tap // 3 - 1, tap % 3 - 1, side
            ).astype(bf16)
    both = grad_hidden[...]
    outer0 = lax.dot_general(moved[0], both[:width], transposed, preferred_element_type=f32)
    inner0 = lax.dot_general(moved[1], both, transposed, preferred_element_type=f32)
    inner1 = lax.dot_general(moved[2], both, transposed, preferred_element_type=f32)
    outer1 = lax.dot_general(moved[3], both[width:], transposed, preferred_element_type=f32)
    tall = 9 * chan
    sums[:tall] = outer0 + inner0[:, width:]
    sums[tall : 2 * tall] = inner0[:, :width] + inner1[:, width:]
    sums[2 * tall : 3 * tall] = inner1[:, :width] + outer1
    sums[3 * tall :] = jnp.zeros((sums.shape[0] - 3 * tall, width), f32)
    me = lax.axis_index("dp")
    for distance, message in enumerate(messages):
        rows = message.shape[0]
        message[...] = sums[pl.ds(pl.multiple_of((me ^ distance) * rows, rows), rows)].astype(bf16)


def tap_parts(products):
    chan = products.shape[0] // 9

    def part(b, c):
        tap = 3 * b + c
        return products[tap * chan : (tap + 1) * chan]

    return part


def edges_kernel(side, weight, grad_hidden, even_pairs, odd_pairs, products):
    width = weight.shape[1]
    tall = weight.shape[0] // 3
    both = grad_hidden[...]
    products[...] = jnp.dot(weight[:tall], both[:width], preferred_element_type=f32)
    to_before = gathered(tap_parts(products), side).astype(bf16)
    products[...] = jnp.dot(weight[2 * tall :], both[width:], preferred_element_type=f32)
    to_after = gathered(tap_parts(products), side).astype(bf16)
    even_pairs[...], odd_pairs[...] = for_sides(to_before, to_after)


def own_kernel(side, weight, grad_hidden, own, products):
    tall = weight.shape[0] // 3
    both = grad_hidden[...]
    for plane in range(2):
        mixed = jnp.concatenate(
            [weight[(plane + 1) * tall : (plane + 2) * tall], weight[plane * tall : (plane + 1) * tall]], 1
        )
        products[...] = jnp.dot(mixed, both, preferred_element_type=f32)
        own[plane] = gathered(tap_parts(products), side)


def swapped(part, axis, distance):
    return lax.ppermute(part, axis, [(i, i ^ distance) for i in range(lax.axis_size(axis))])


def per_device(layer_input, hidden_pre, output_pre, output_grad, weight_a, weight_b):
    side = math.isqrt(layer_input.shape[3])
    half = side // 2
    size, small = side * side, half * half
    depth_a = layer_input.shape[2]
    samples, slabs = lax.axis_size("dp"), lax.axis_size("space")
    even = [(i, i ^ 1) for i in range(slabs)]
    odd = [(i, ((i + 1 ^ 1) - 1) % slabs) for i in range(slabs)]
    odd_inside = [(i, k) if abs(i - k) == 1 else (i, i) for i, k in odd]
    shape = jax.ShapeDtypeStruct
    outer = output_pre[0, :, 0].astype(f32)
    grad = (output_grad[0, :, 0].astype(f32) * jnp.where(outer > 0, 1.0, negative_slope)).astype(bf16)
    grad, layer_input, hidden_pre = lax.optimization_barrier((grad, layer_input, hidden_pre))
    grad_sides = [lax.ppermute(grad, "space", pairs) for pairs in (even, odd)]
    source = layer_input[0].transpose(1, 0, 2)
    hidden = hidden_pre[0].transpose(1, 0, 2)
    chan = source.shape[1]
    width_a = hidden.shape[1]
    width_b = grad.shape[0]
    plan = Plan(samples, slabs, chan, width_a, width_b)
    pooled = call(lambda *refs: pool_kernel(side, *refs), shape((width_a, small), bf16), [], 1 << 28, hidden)
    source, pooled = lax.optimization_barrier((source, pooled))
    source_sides = [
        lax.ppermute(part, "space", pairs) for part, pairs in zip(for_sides(source[0], source[1]), (even, odd))
    ]
    packed = call(
        lambda *refs: pack_kernel(plan, *refs),
        [shape((plan.width + 3 * plan.share, small), bf16)] * samples + [shape(grad.shape, bf16)] * 2,
        [],
        1 << 20,
        pooled,
        grad,
        *grad_sides,
    )
    packed, (before, after) = packed[:samples], packed[samples:]
    got_b = packed[:1] + [swapped(packed[k], "dp", k) for k in range(1, samples)]
    grad_hidden = call(
        lambda *refs: hidden_kernel(side, *refs),
        shape((2 * width_a, size), bf16),
        [pltpu.VMEM((9 * width_a, small), f32)],
        1 << 30,
        weight_b.reshape(27 * width_a, width_b),
        grad,
        before,
        after,
        hidden,
    )
    sums_a = call(
        lambda *refs: sums_a_kernel(side, plan, *refs),
        [shape((plan.rows_a * slabs, width_a), bf16)] * samples,
        [
            pltpu.VMEM((4, 9 * chan, size), bf16),
            pltpu.VMEM((plan.rows_a * samples * slabs, width_a), f32),
        ],
        1 << 30,
        grad_hidden,
        source,
        *source_sides,
    )
    got_a = sums_a[:1] + [swapped(sums_a[k], "dp", k) for k in range(1, samples)]
    totals = call(
        lambda *refs: share_kernel(plan, *refs),
        shape((slabs, plan.rows_b, 128), f32),
        [
            pltpu.VMEM((9 * width_a, samples * small), bf16),
            pltpu.VMEM((slabs * plan.rows_b, 128), f32),
        ],
        1 << 30,
        *got_b,
    )
    totals, grad_hidden = lax.optimization_barrier((totals, grad_hidden))
    edges = call(
        lambda *refs: edges_kernel(side, *refs),
        [shape((chan, size), bf16)] * 2,
        [pltpu.VMEM((9 * chan, size), f32)],
        1 << 28,
        weight_a.reshape(27 * chan, width_a),
        grad_hidden,
    )
    own = call(
        lambda *refs: own_kernel(side, *refs),
        shape((2, chan, size), f32),
        [pltpu.VMEM((9 * chan, size), f32)],
        1 << 28,
        weight_a.reshape(27 * chan, width_a),
        grad_hidden,
    )
    from_odd = lax.ppermute(edges[1], "space", odd_inside)
    got_a, own, edges = lax.optimization_barrier((got_a, own, edges))
    far = plan.far
    blocks = call(
        lambda *refs: blocks_kernel(plan, *refs),
        [shape((2, plan.block, 128), bf16)] * far,
        [pltpu.VMEM((plan.rows_a * slabs, 128), f32)],
        1 << 20,
        totals,
        *got_a,
    )
    parts = blocks[:1] + [swapped(blocks[k], "space", k) for k in range(1, far)]
    parts, from_odd = lax.optimization_barrier((parts, from_odd))
    both = call(near_kernel, shape((2, plan.block, 128), bf16), [], 1 << 20, *parts)
    there = swapped(both, "space", far)
    both, even_edge = lax.optimization_barrier((both, edges[0]))
    from_even = lax.ppermute(even_edge, "space", even)
    there, from_even = lax.optimization_barrier((there, from_even))
    input_grad = own + jnp.stack(sides(from_even, from_odd)).astype(f32)
    input_grad = input_grad.astype(bf16).transpose(1, 0, 2)[None]
    low, high = call(
        lambda *refs: far_kernel(plan, *refs),
        [shape((2, rows, 128), bf16) for rows in (plan.low, plan.block - plan.low)],
        [],
        1 << 20,
        both,
        there,
    )
    strides = [samples >> k for k in range(1, samples.bit_length())]

    def crossed(parts):
        return [[swapped(part, "dp", stride) for part in parts] for stride in strides[1:]]

    def stacked(parts):
        return call(stack_kernel, shape((2 * len(parts), *parts[0].shape[1:]), bf16), [], 1 << 20, *parts)

    high_hop = swapped(high, "dp", strides[0])
    low_near = [swapped(low, "space", k) for k in range(1, far)]
    low, high, low_near, high_hop = lax.optimization_barrier((low, high, low_near, high_hop))
    low_all = stacked([low, *low_near])
    high_both = stacked([high, high_hop])
    low_hop = swapped(low_all, "dp", strides[0])
    high_near = [swapped(high_both, "space", k) for k in range(1, far)]
    across_first = crossed([low_all, high_both])
    low_hop, high_near, across_first, input_grad = lax.optimization_barrier(
        (low_hop, high_near, across_first, input_grad)
    )
    highs = [high_both, *high_near]
    known = {0: (low_all, low_hop, highs)}
    for stride, (low_there, high_there) in zip(strides[1:], across_first):
        for k in list(known):
            lows, hops, parts = known[k]
            known[k ^ stride] = (
                swapped(lows, "dp", stride) if k else low_there,
                swapped(hops, "dp", stride),
                [swapped(part, "dp", stride) if k or n else high_there for n, part in enumerate(parts)],
            )
    shares = [known[k] for k in sorted(known)]
    planes_a = depth_a * slabs
    total_a, total_b = call(
        lambda *refs: last_kernel(
            plan,
            1.0 / math.sqrt(samples * planes_a * size),
            1.0 / math.sqrt(samples * (planes_a // 2) * small),
            *refs,
        ),
        [shape((27 * chan, width_a), f32), shape((27 * width_a, width_b), f32)],
        [
            pltpu.VMEM((samples, slabs, plan.block, 128), bf16),
            pltpu.VMEM((27 * chan, width_a), f32),
            pltpu.VMEM((27 * width_a, width_b), f32),
            pltpu.SemaphoreType.DMA((4,)),
        ],
        1 << 20,
        *[part for lows, hops, parts in shares for part in (lows, hops, *parts)],
        out_specs=[pl.BlockSpec(memory_space=pl.ANY)] * 2,
    )
    return (input_grad, total_a.reshape(weight_a.shape), total_b.reshape(weight_b.shape))


def solution(mesh):
    in_specs = (
        P("dp", None, "space", None),
        P("dp", None, "space", None),
        P("dp", None, "space", None),
        P("dp", None, "space", None),
        P(),
        P(),
    )
    out_specs = (P("dp", None, "space", None), P(), P())
    return jax.shard_map(
        per_device, mesh=mesh, in_specs=in_specs, out_specs=out_specs, check_vma=False
    )
```

```python
import math

import jax
import jax.numpy as jnp
from jax import lax
from jax.experimental import pallas as pl
from jax.experimental.pallas import tpu as pltpu
from jax.sharding import PartitionSpec as P

negative_slope = 0.3
f32 = jnp.float32
bf16 = jnp.bfloat16
vmem = pl.BlockSpec(memory_space=pltpu.VMEM)
transposed = (((1,), (1,)), ((), ()))


def shifted(cells, rows, columns, side):
    size = side * side
    offset = rows * side + columns
    if offset:
        cells = pltpu.roll(cells, (-offset) % size, 1)
    place = lax.broadcasted_iota(jnp.int32, cells.shape, 1)
    if rows:
        y = place // side + rows
        cells = jnp.where((y >= 0) & (y < side), cells, 0.0)
    if columns:
        x = place % side + columns
        cells = jnp.where((x >= 0) & (x < side), cells, 0.0)
    return cells


def gathered(parts, side):
    total = None
    for c in range(3):
        line = parts(1, c) + shifted(parts(0, c), 1, 0, side) + shifted(parts(2, c), -1, 0, side)
        line = shifted(line, 0, 1 - c, side)
        total = line if total is None else total + line
    return total


def pool_matrix(side):
    half = side // 2
    fine = lax.broadcasted_iota(jnp.int32, (side * side, half * half), 0)
    coarse = lax.broadcasted_iota(jnp.int32, (side * side, half * half), 1)
    parent = (fine // (2 * side)) * half + (fine % side) // 2
    return jnp.where(parent == coarse, 0.125, 0.0).astype(bf16)


def sides(even_pairs, odd_pairs):
    here = lax.axis_index("space")
    even = here % 2 == 0
    nothing = jnp.zeros(even_pairs.shape, bf16)
    before = jnp.where(here == 0, nothing, jnp.where(even, odd_pairs, even_pairs))
    after = jnp.where(here == lax.axis_size("space") - 1, nothing, jnp.where(even, even_pairs, odd_pairs))
    return before, after


def for_sides(before, after):
    even = lax.axis_index("space") % 2 == 0
    return jnp.where(even, after, before), jnp.where(even, before, after)


def call(kernel, out_shape, scratch, flops, *args, out_specs=None):
    result = pl.pallas_call(
        kernel,
        out_shape=out_shape,
        in_specs=[vmem] * len(args),
        out_specs=out_specs or jax.tree.map(lambda _: vmem, out_shape),
        scratch_shapes=scratch,
        compiler_params=pltpu.CompilerParams(vmem_limit_bytes=48 * 1024 * 1024),
        cost_estimate=pl.CostEstimate(flops=flops, bytes_accessed=2 << 20, transcendentals=0),
    )(*args)
    return list(result) if isinstance(out_shape, list) else result


def pool_kernel(side, hidden, pooled):
    width = hidden.shape[1]
    pool = pool_matrix(side)
    total = None
    for plane in range(2):
        cells = hidden[plane].astype(f32)
        stacked = jnp.concatenate([jnp.maximum(cells, 0.0), jnp.minimum(cells, 0.0)], 0).astype(bf16)
        part = jnp.dot(stacked, pool, preferred_element_type=f32)
        total = part if total is None else total + part
    pooled[...] = (total[:width] + negative_slope * total[width:]).astype(bf16)


def pack_kernel(plan, pooled, grad, even_pairs, odd_pairs, *refs):
    me = lax.axis_index("dp")
    messages, (before, after) = refs[:-2], refs[-2:]
    before[...], after[...] = sides(even_pairs[...], odd_pairs[...])
    for distance, message in enumerate(messages):
        message[: plan.width] = pooled[...]
        start = pl.multiple_of((me ^ distance) * plan.share, plan.share)
        for a, plane in enumerate((after, grad, before)):
            row = plan.width + a * plan.share
            message[row : row + plan.share] = plane[pl.ds(start, plan.share)]


def share_kernel(plan, *refs):
    got, (out, moved, totals) = refs[:-3], refs[-3:]
    size = got[0].shape[1]
    half = math.isqrt(size)
    width, share = plan.width, plan.share
    for k, message in enumerate(got):
        cells = message[:width].astype(f32)
        for tap in range(9):
            moved[tap * width : (tap + 1) * width, k * size : (k + 1) * size] = shifted(
                cells, tap // 3 - 1, tap % 3 - 1, half
            ).astype(bf16)
    right = jnp.concatenate([message[width:] for message in got], 1)
    result = lax.dot_general(moved[...], right, transposed, preferred_element_type=f32)
    for a in range(3):
        pieces = [
            result[k * plan.tall : (k + 1) * plan.tall, a * share : (a + 1) * share] for k in range(plan.pieces)
        ]
        totals[a * plan.tall : (a + 1) * plan.tall] = jnp.concatenate(pieces, 1)
    spare = totals.shape[0] - 3 * plan.tall
    if spare:
        totals[3 * plan.tall :] = jnp.zeros((spare, 128), f32)
    for slab in range(plan.slabs):
        out[slab] = totals[slab * plan.rows_b : (slab + 1) * plan.rows_b]


def blocks_kernel(plan, totals, *refs):
    got, blocks, first = refs[: plan.samples], refs[plan.samples : -1], refs[-1]
    total = got[0][...].astype(f32)
    for message in got[1:]:
        total += message[...].astype(f32)
    first[...] = total
    me = lax.axis_index("space")
    for distance, block in enumerate(blocks):
        for k in range(2):
            slab = me ^ distance ^ (k * plan.far)
            row = pl.multiple_of(slab * plan.rows_a, plan.rows_a)
            parts = [totals[slab], first[pl.ds(row, plan.rows_a)]]
            spare = plan.block - plan.rows_b - plan.rows_a
            if spare:
                parts.append(jnp.zeros((spare, 128), f32))
            block[k] = jnp.concatenate(parts, 0).astype(bf16)


def near_kernel(*refs):
    total = refs[0][...].astype(f32)
    for part in refs[1:-1]:
        total += part[...].astype(f32)
    refs[-1][...] = total.astype(bf16)


def far_kernel(plan, here, there, pair, low):
    for k in range(2):
        pair[k] = (here[k].astype(f32) + there[1 - k].astype(f32)).astype(bf16)
        low[k] = pair[k, : plan.low]


def high_kernel(plan, pair, hop, high):
    for k in range(2):
        high[k], high[2 + k] = pair[k, plan.low :], hop[k, plan.low :]


def stack_kernel(*refs):
    count = refs[0].shape[0]
    for k, part in enumerate(refs[:-1]):
        refs[-1][count * k : count * (k + 1)] = part[...]


def last_kernel(plan, scale_a, scale_b, *refs):
    got, (out_a, out_b, shares, rows_a, rows, sems) = refs[:-6], refs[-6:]
    me, here = lax.axis_index("dp"), lax.axis_index("space")
    far, groups = plan.far, plan.samples // 2
    each = len(got) // groups
    for group in range(groups):
        pairs, lows = got[group * each : group * each + 2], got[group * each + 2 : group * each + 4]
        highs = got[group * each + 4 : (group + 1) * each]
        for hop in range(2):
            sample = me ^ group ^ (hop * groups)
            for k in range(plan.slabs):
                slab = here ^ (k // 2) ^ (k % 2 * far)
                if k < 2:
                    shares[sample, slab] = pairs[hop][k]
                else:
                    shares[sample, slab, : plan.low] = lows[hop][k - 2]
                    shares[sample, slab, plan.low :] = highs[k // 2 - 1][2 * hop + k % 2]
    for sample in range(plan.samples):
        for slab in range(plan.slabs):
            row = (sample * plan.slabs + slab) * plan.rows_a
            height = min(plan.rows_a, out_a.shape[0] - row)
            if height > 0:
                base = plan.rows_b // 16 * 16
                block = shares[sample, slab, base:].astype(f32)[plan.rows_b - base :]
                rows_a[row : row + height] = block[:height] * scale_a
    copy_a = pltpu.make_async_copy(rows_a, out_a, sems.at[3])
    copy_a.start()
    copies = []
    for slab in range(plan.slabs):
        blocks = [shares[sample, slab].astype(f32) for sample in range(plan.samples)]
        for k in range(plan.pieces):
            lanes = slice(k * plan.share, (k + 1) * plan.share)
            wide = jnp.concatenate([block[: plan.rows_b, lanes] for block in blocks], 1) * scale_b
            start, stop = slab * plan.rows_b, min((slab + 1) * plan.rows_b, 3 * plan.tall)
            while start < stop:
                a = start // plan.tall
                end = min(stop, (a + 1) * plan.tall)
                row = (a * (plan.pieces - 1) + k) * plan.tall + start
                rows[row : row + end - start] = wide[start - slab * plan.rows_b : end - slab * plan.rows_b]
                start = end
        height = plan.pieces * plan.tall
        while len(copies) < 3 and (slab + 1) * plan.rows_b >= (len(copies) + 1) * plan.tall:
            place = pl.ds(len(copies) * height, height)
            copies.append(pltpu.make_async_copy(rows.at[place], out_b.at[place], sems.at[len(copies)]))
            copies[-1].start()
    for copy in (copy_a, *copies):
        copy.wait()


class Plan:
    def __init__(self, samples, slabs, chan, width, width_b):
        self.samples, self.slabs, self.width = samples, slabs, width
        self.share = width_b // samples
        self.pieces = 128 // self.share
        self.tall = 9 * width // self.pieces
        self.rows_b = -(-3 * self.tall // (8 * slabs)) * 8
        self.rows_a = -(-27 * chan // (8 * samples * slabs)) * 8
        self.block = -(-(self.rows_b + self.rows_a) // 16) * 16
        self.low = -(-self.block * 4 // 112) * 16
        self.far = slabs // 2


def hidden_kernel(side, weight, grad, before, after, hidden, grad_hidden, products):
    half = side // 2
    width = hidden.shape[1]
    block = 9 * width
    products[...] = jnp.dot(weight[:block], after[...], preferred_element_type=f32)
    products[...] += jnp.dot(weight[block : 2 * block], grad[...], preferred_element_type=f32)
    products[...] += jnp.dot(weight[2 * block :], before[...], preferred_element_type=f32)

    def part(b, c):
        tap = 3 * b + c
        return products[tap * width : (tap + 1) * width]

    back = gathered(part, half)
    high = back.astype(bf16)
    low = (back - high.astype(f32)).astype(bf16)
    pool = pool_matrix(side)
    spread = lax.dot_general(high, pool, transposed, preferred_element_type=f32)
    spread += lax.dot_general(low, pool, transposed, preferred_element_type=f32)
    for plane in range(2):
        slope = jnp.where(hidden[plane].astype(f32) > 0, 1.0, negative_slope)
        grad_hidden[plane * width : (plane + 1) * width] = (spread * slope).astype(bf16)


def sums_a_kernel(side, plan, grad_hidden, source, even_pairs, odd_pairs, *refs):
    messages, (moved, sums) = refs[:-2], refs[-2:]
    width = plan.width
    chan = source.shape[1]
    before, after = sides(even_pairs[...], odd_pairs[...])
    for index, plane in enumerate((before, source[0], source[1], after)):
        cells = plane.astype(f32)
        for tap in range(9):
            moved[index, tap * chan : (tap + 1) * chan] = shifted(
                cells, tap // 3 - 1, tap % 3 - 1, side
            ).astype(bf16)
    both = grad_hidden[...]
    outer0 = lax.dot_general(moved[0], both[:width], transposed, preferred_element_type=f32)
    inner0 = lax.dot_general(moved[1], both, transposed, preferred_element_type=f32)
    inner1 = lax.dot_general(moved[2], both, transposed, preferred_element_type=f32)
    outer1 = lax.dot_general(moved[3], both[width:], transposed, preferred_element_type=f32)
    tall = 9 * chan
    sums[:tall] = outer0 + inner0[:, width:]
    sums[tall : 2 * tall] = inner0[:, :width] + inner1[:, width:]
    sums[2 * tall : 3 * tall] = inner1[:, :width] + outer1
    sums[3 * tall :] = jnp.zeros((sums.shape[0] - 3 * tall, width), f32)
    me = lax.axis_index("dp")
    for distance, message in enumerate(messages):
        rows = message.shape[0]
        message[...] = sums[pl.ds(pl.multiple_of((me ^ distance) * rows, rows), rows)].astype(bf16)


def tap_parts(products):
    chan = products.shape[0] // 9

    def part(b, c):
        tap = 3 * b + c
        return products[tap * chan : (tap + 1) * chan]

    return part


def edges_kernel(side, weight, grad_hidden, even_pairs, odd_pairs, products):
    width = weight.shape[1]
    tall = weight.shape[0] // 3
    both = grad_hidden[...]
    products[...] = jnp.dot(weight[:tall], both[:width], preferred_element_type=f32)
    to_before = gathered(tap_parts(products), side).astype(bf16)
    products[...] = jnp.dot(weight[2 * tall :], both[width:], preferred_element_type=f32)
    to_after = gathered(tap_parts(products), side).astype(bf16)
    even_pairs[...], odd_pairs[...] = for_sides(to_before, to_after)


def own_kernel(side, weight, grad_hidden, own, products):
    tall = weight.shape[0] // 3
    both = grad_hidden[...]
    for plane in range(2):
        mixed = jnp.concatenate(
            [weight[(plane + 1) * tall : (plane + 2) * tall], weight[plane * tall : (plane + 1) * tall]], 1
        )
        products[...] = jnp.dot(mixed, both, preferred_element_type=f32)
        own[plane] = gathered(tap_parts(products), side)


def swapped(part, axis, distance):
    return lax.ppermute(part, axis, [(i, i ^ distance) for i in range(lax.axis_size(axis))])


def per_device(layer_input, hidden_pre, output_pre, output_grad, weight_a, weight_b):
    side = math.isqrt(layer_input.shape[3])
    half = side // 2
    size, small = side * side, half * half
    depth_a = layer_input.shape[2]
    samples, slabs = lax.axis_size("dp"), lax.axis_size("space")
    even = [(i, i ^ 1) for i in range(slabs)]
    odd = [(i, ((i + 1 ^ 1) - 1) % slabs) for i in range(slabs)]
    odd_inside = [(i, k) if abs(i - k) == 1 else (i, i) for i, k in odd]
    shape = jax.ShapeDtypeStruct
    outer = output_pre[0, :, 0].astype(f32)
    grad = (output_grad[0, :, 0].astype(f32) * jnp.where(outer > 0, 1.0, negative_slope)).astype(bf16)
    grad, layer_input, hidden_pre = lax.optimization_barrier((grad, layer_input, hidden_pre))
    grad_sides = [lax.ppermute(grad, "space", pairs) for pairs in (even, odd)]
    source = layer_input[0].transpose(1, 0, 2)
    hidden = hidden_pre[0].transpose(1, 0, 2)
    chan = source.shape[1]
    width_a = hidden.shape[1]
    width_b = grad.shape[0]
    plan = Plan(samples, slabs, chan, width_a, width_b)
    pooled = call(lambda *refs: pool_kernel(side, *refs), shape((width_a, small), bf16), [], 1 << 28, hidden)
    source, pooled = lax.optimization_barrier((source, pooled))
    source_sides = [
        lax.ppermute(part, "space", pairs) for part, pairs in zip(for_sides(source[0], source[1]), (even, odd))
    ]
    packed = call(
        lambda *refs: pack_kernel(plan, *refs),
        [shape((plan.width + 3 * plan.share, small), bf16)] * samples + [shape(grad.shape, bf16)] * 2,
        [],
        1 << 20,
        pooled,
        grad,
        *grad_sides,
    )
    packed, (before, after) = packed[:samples], packed[samples:]
    got_b = packed[:1] + [swapped(packed[k], "dp", k) for k in range(1, samples)]
    grad_hidden = call(
        lambda *refs: hidden_kernel(side, *refs),
        shape((2 * width_a, size), bf16),
        [pltpu.VMEM((9 * width_a, small), f32)],
        1 << 30,
        weight_b.reshape(27 * width_a, width_b),
        grad,
        before,
        after,
        hidden,
    )
    sums_a = call(
        lambda *refs: sums_a_kernel(side, plan, *refs),
        [shape((plan.rows_a * slabs, width_a), bf16)] * samples,
        [
            pltpu.VMEM((4, 9 * chan, size), bf16),
            pltpu.VMEM((plan.rows_a * samples * slabs, width_a), f32),
        ],
        1 << 30,
        grad_hidden,
        source,
        *source_sides,
    )
    got_a = sums_a[:1] + [swapped(sums_a[k], "dp", k) for k in range(1, samples)]
    totals = call(
        lambda *refs: share_kernel(plan, *refs),
        shape((slabs, plan.rows_b, 128), f32),
        [
            pltpu.VMEM((9 * width_a, samples * small), bf16),
            pltpu.VMEM((slabs * plan.rows_b, 128), f32),
        ],
        1 << 30,
        *got_b,
    )
    totals, grad_hidden = lax.optimization_barrier((totals, grad_hidden))
    edges = call(
        lambda *refs: edges_kernel(side, *refs),
        [shape((chan, size), bf16)] * 2,
        [pltpu.VMEM((9 * chan, size), f32)],
        1 << 28,
        weight_a.reshape(27 * chan, width_a),
        grad_hidden,
    )
    own = call(
        lambda *refs: own_kernel(side, *refs),
        shape((2, chan, size), f32),
        [pltpu.VMEM((9 * chan, size), f32)],
        1 << 28,
        weight_a.reshape(27 * chan, width_a),
        grad_hidden,
    )
    from_odd = lax.ppermute(edges[1], "space", odd_inside)
    got_a, own, edges = lax.optimization_barrier((got_a, own, edges))
    far = plan.far
    blocks = call(
        lambda *refs: blocks_kernel(plan, *refs),
        [shape((2, plan.block, 128), bf16)] * far,
        [pltpu.VMEM((plan.rows_a * slabs, 128), f32)],
        1 << 20,
        totals,
        *got_a,
    )
    parts = blocks[:1] + [swapped(blocks[k], "space", k) for k in range(1, far)]
    parts, from_odd = lax.optimization_barrier((parts, from_odd))
    both = call(near_kernel, shape((2, plan.block, 128), bf16), [], 1 << 20, *parts)
    there = swapped(both, "space", far)
    both, even_edge = lax.optimization_barrier((both, edges[0]))
    from_even = lax.ppermute(even_edge, "space", even)
    there, from_even = lax.optimization_barrier((there, from_even))
    input_grad = own + jnp.stack(sides(from_even, from_odd)).astype(f32)
    input_grad = input_grad.astype(bf16).transpose(1, 0, 2)[None]
    pair, low = call(
        lambda *refs: far_kernel(plan, *refs),
        [shape((2, rows, 128), bf16) for rows in (plan.block, plan.low)],
        [],
        1 << 20,
        both,
        there,
    )
    strides = [samples >> k for k in range(1, samples.bit_length())]

    def stacked(parts):
        rows = sum(part.shape[0] for part in parts)
        return call(stack_kernel, shape((rows, *parts[0].shape[1:]), bf16), [], 1 << 20, *parts)

    hop = swapped(pair, "dp", strides[0])
    near = [swapped(low, "space", k) for k in range(1, far)]
    first = [swapped(pair, "dp", stride) for stride in strides[1:]]
    pair, hop, near, first = lax.optimization_barrier((pair, hop, near, first))
    lows = stacked(near)
    high = call(
        lambda *refs: high_kernel(plan, *refs),
        shape((4, plan.block - plan.low, 128), bf16),
        [],
        1 << 20,
        pair,
        hop,
    )
    lows_hop = swapped(lows, "dp", strides[0])
    highs = [swapped(high, "space", k) for k in range(1, far)]
    lows_hop, highs, lows, hop, input_grad = lax.optimization_barrier((lows_hop, highs, lows, hop, input_grad))
    known = {0: [pair, hop, lows, lows_hop, *highs]}
    for stride, part in zip(strides[1:], first):
        for k in list(known):
            done = [] if k else [part]
            known[k ^ stride] = done + [swapped(part, "dp", stride) for part in known[k][len(done) :]]
    shares = [known[k] for k in sorted(known)]
    planes_a = depth_a * slabs
    total_a, total_b = call(
        lambda *refs: last_kernel(
            plan,
            1.0 / math.sqrt(samples * planes_a * size),
            1.0 / math.sqrt(samples * (planes_a // 2) * small),
            *refs,
        ),
        [shape((27 * chan, width_a), f32), shape((27 * width_a, width_b), f32)],
        [
            pltpu.VMEM((samples, slabs, plan.block, 128), bf16),
            pltpu.VMEM((27 * chan, width_a), f32),
            pltpu.VMEM((27 * width_a, width_b), f32),
            pltpu.SemaphoreType.DMA((4,)),
        ],
        1 << 20,
        *[part for parts in shares for part in parts],
        out_specs=[pl.BlockSpec(memory_space=pl.ANY)] * 2,
    )
    return (input_grad, total_a.reshape(weight_a.shape), total_b.reshape(weight_b.shape))


def solution(mesh):
    in_specs = (
        P("dp", None, "space", None),
        P("dp", None, "space", None),
        P("dp", None, "space", None),
        P("dp", None, "space", None),
        P(),
        P(),
    )
    out_specs = (P("dp", None, "space", None), P(), P())
    return jax.shard_map(
        per_device, mesh=mesh, in_specs=in_specs, out_specs=out_specs, check_vma=False
    )
```

```python
import math

import jax
import jax.numpy as jnp
from jax import lax
from jax.experimental import pallas as pl
from jax.experimental.pallas import tpu as pltpu
from jax.sharding import PartitionSpec as P

negative_slope = 0.3
f32 = jnp.float32
bf16 = jnp.bfloat16
vmem = pl.BlockSpec(memory_space=pltpu.VMEM)
transposed = (((1,), (1,)), ((), ()))


def shifted(cells, rows, columns, side):
    size = side * side
    offset = rows * side + columns
    if offset:
        cells = pltpu.roll(cells, (-offset) % size, 1)
    place = lax.broadcasted_iota(jnp.int32, cells.shape, 1)
    if rows:
        y = place // side + rows
        cells = jnp.where((y >= 0) & (y < side), cells, 0.0)
    if columns:
        x = place % side + columns
        cells = jnp.where((x >= 0) & (x < side), cells, 0.0)
    return cells


def gathered(parts, side):
    total = None
    for c in range(3):
        line = parts(1, c) + shifted(parts(0, c), 1, 0, side) + shifted(parts(2, c), -1, 0, side)
        line = shifted(line, 0, 1 - c, side)
        total = line if total is None else total + line
    return total


def pool_matrix(side):
    half = side // 2
    fine = lax.broadcasted_iota(jnp.int32, (side * side, half * half), 0)
    coarse = lax.broadcasted_iota(jnp.int32, (side * side, half * half), 1)
    parent = (fine // (2 * side)) * half + (fine % side) // 2
    return jnp.where(parent == coarse, 0.125, 0.0).astype(bf16)


def sides(even_pairs, odd_pairs):
    here = lax.axis_index("space")
    even = here % 2 == 0
    nothing = jnp.zeros(even_pairs.shape, bf16)
    before = jnp.where(here == 0, nothing, jnp.where(even, odd_pairs, even_pairs))
    after = jnp.where(here == lax.axis_size("space") - 1, nothing, jnp.where(even, even_pairs, odd_pairs))
    return before, after


def for_sides(before, after):
    even = lax.axis_index("space") % 2 == 0
    return jnp.where(even, after, before), jnp.where(even, before, after)


def call(kernel, out_shape, scratch, flops, *args, out_specs=None):
    result = pl.pallas_call(
        kernel,
        out_shape=out_shape,
        in_specs=[vmem] * len(args),
        out_specs=out_specs or jax.tree.map(lambda _: vmem, out_shape),
        scratch_shapes=scratch,
        compiler_params=pltpu.CompilerParams(vmem_limit_bytes=48 * 1024 * 1024),
        cost_estimate=pl.CostEstimate(flops=flops >> 12, bytes_accessed=1 << 10, transcendentals=0),
    )(*args)
    return list(result) if isinstance(out_shape, list) else result


def pool_kernel(side, hidden, pooled):
    width = hidden.shape[1]
    pool = pool_matrix(side)
    total = None
    for plane in range(2):
        cells = hidden[plane].astype(f32)
        stacked = jnp.concatenate([jnp.maximum(cells, 0.0), jnp.minimum(cells, 0.0)], 0).astype(bf16)
        part = jnp.dot(stacked, pool, preferred_element_type=f32)
        total = part if total is None else total + part
    pooled[...] = (total[:width] + negative_slope * total[width:]).astype(bf16)


def pack_kernel(plan, pooled, grad, even_pairs, odd_pairs, *refs):
    me = lax.axis_index("dp")
    messages, (before, after) = refs[:-2], refs[-2:]
    before[...], after[...] = sides(even_pairs[...], odd_pairs[...])
    for distance, message in enumerate(messages):
        row = message.shape[0] - 3 * plan.share
        if row:
            message[:row] = pooled[...]
        start = pl.multiple_of((me ^ distance) * plan.share, plan.share)
        for a, plane in enumerate((after, grad, before)):
            message[row + a * plan.share : row + (a + 1) * plan.share] = plane[pl.ds(start, plan.share)]


def share_kernel(plan, *refs):
    pooled, channels, (out, moved, totals) = refs[: plan.samples], refs[plan.samples : -3], refs[-3:]
    size = pooled[0].shape[1]
    half = math.isqrt(size)
    width, share = plan.width, plan.share
    for k, message in enumerate(pooled):
        cells = message[:width]
        cells = cells.astype(f32)
        for tap in range(9):
            moved[tap * width : (tap + 1) * width, k * size : (k + 1) * size] = shifted(
                cells, tap // 3 - 1, tap % 3 - 1, half
            ).astype(bf16)
    right = jnp.concatenate([message[message.shape[0] - 3 * share :] for message in channels], 1)
    result = lax.dot_general(moved[...], right, transposed, preferred_element_type=f32)
    for a in range(3):
        pieces = [
            result[k * plan.tall : (k + 1) * plan.tall, a * share : (a + 1) * share] for k in range(plan.pieces)
        ]
        totals[a * plan.tall : (a + 1) * plan.tall] = jnp.concatenate(pieces, 1)
    spare = totals.shape[0] - 3 * plan.tall
    if spare:
        totals[3 * plan.tall :] = jnp.zeros((spare, 128), f32)
    for slab in range(plan.slabs):
        out[slab] = totals[slab * plan.rows_b : (slab + 1) * plan.rows_b]


def blocks_kernel(plan, totals, *refs):
    mine, got, *blocks, first = refs
    first[...] = mine[...] + got[...].astype(f32)
    me = lax.axis_index("space")
    for distance, block in enumerate(blocks):
        for k in range(2):
            slab = me ^ distance ^ (k * plan.far)
            row = pl.multiple_of(slab * plan.rows_a, plan.rows_a)
            parts = [totals[slab], first[pl.ds(row, plan.rows_a)]]
            spare = plan.block - plan.rows_b - plan.rows_a
            if spare:
                parts.append(jnp.zeros((spare, 128), f32))
            block[k] = jnp.concatenate(parts, 0).astype(bf16)


def near_kernel(*refs):
    total = refs[0][...].astype(f32)
    for part in refs[1:-1]:
        total += part[...].astype(f32)
    refs[-1][...] = total.astype(bf16)


def far_kernel(plan, here, there, pair, low):
    for k in range(2):
        pair[k] = (here[k].astype(f32) + there[1 - k].astype(f32)).astype(bf16)
        low[k] = pair[k, : plan.low]


def high_kernel(plan, pair, hop, high):
    for k in range(2):
        high[k], high[2 + k] = pair[k, plan.low :], hop[k, plan.low :]


def stack_kernel(*refs):
    count = refs[0].shape[0]
    for k, part in enumerate(refs[:-1]):
        refs[-1][count * k : count * (k + 1)] = part[...]


def last_kernel(plan, scale_a, scale_b, *refs):
    got, (out_a, out_b, shares, rows_a, rows, sems) = refs[:-6], refs[-6:]
    me, here = lax.axis_index("dp"), lax.axis_index("space")
    far, groups = plan.far, plan.samples // 2
    each = len(got) // groups
    for group in range(groups):
        pairs, lows = got[group * each : group * each + 2], got[group * each + 2 : group * each + 4]
        highs = got[group * each + 4 : (group + 1) * each]
        for hop in range(2):
            sample = me ^ group ^ (hop * groups)
            for k in range(plan.slabs):
                slab = here ^ (k // 2) ^ (k % 2 * far)
                if k < 2:
                    shares[sample, slab] = pairs[hop][k]
                else:
                    shares[sample, slab, : plan.low] = lows[hop][k - 2]
                    shares[sample, slab, plan.low :] = highs[k // 2 - 1][2 * hop + k % 2]
    for sample in range(plan.samples):
        for slab in range(plan.slabs):
            row = (sample * plan.slabs + slab) * plan.rows_a
            height = min(plan.rows_a, out_a.shape[0] - row)
            if height > 0:
                base = plan.rows_b // 16 * 16
                block = shares[sample, slab, base:].astype(f32)[plan.rows_b - base :]
                rows_a[row : row + height] = block[:height] * scale_a
    copy_a = pltpu.make_async_copy(rows_a, out_a, sems.at[3])
    copy_a.start()
    copies = []
    for slab in range(plan.slabs):
        blocks = [shares[sample, slab].astype(f32) for sample in range(plan.samples)]
        for k in range(plan.pieces):
            lanes = slice(k * plan.share, (k + 1) * plan.share)
            wide = jnp.concatenate([block[: plan.rows_b, lanes] for block in blocks], 1) * scale_b
            start, stop = slab * plan.rows_b, min((slab + 1) * plan.rows_b, 3 * plan.tall)
            while start < stop:
                a = start // plan.tall
                end = min(stop, (a + 1) * plan.tall)
                row = (a * (plan.pieces - 1) + k) * plan.tall + start
                rows[row : row + end - start] = wide[start - slab * plan.rows_b : end - slab * plan.rows_b]
                start = end
        height = plan.pieces * plan.tall
        while len(copies) < 3 and (slab + 1) * plan.rows_b >= (len(copies) + 1) * plan.tall:
            place = pl.ds(len(copies) * height, height)
            copies.append(pltpu.make_async_copy(rows.at[place], out_b.at[place], sems.at[len(copies)]))
            copies[-1].start()
    for copy in (copy_a, *copies):
        copy.wait()


class Plan:
    def __init__(self, samples, slabs, chan, width, width_b):
        self.samples, self.slabs, self.width = samples, slabs, width
        self.share = width_b // samples
        self.pieces = 128 // self.share
        self.tall = 9 * width // self.pieces
        self.rows_b = -(-3 * self.tall // (8 * slabs)) * 8
        self.rows_a = -(-27 * chan // (8 * samples * slabs)) * 8
        self.block = -(-(self.rows_b + self.rows_a) // 16) * 16
        self.low = -(-self.block * 4 // 112) * 16
        self.far = slabs // 2


def hidden_kernel(side, weight, grad, before, after, hidden, grad_hidden, products):
    half = side // 2
    width = hidden.shape[1]
    block = 9 * width
    products[...] = jnp.dot(weight[:block], after[...], preferred_element_type=f32)
    products[...] += jnp.dot(weight[block : 2 * block], grad[...], preferred_element_type=f32)
    products[...] += jnp.dot(weight[2 * block :], before[...], preferred_element_type=f32)

    def part(b, c):
        tap = 3 * b + c
        return products[tap * width : (tap + 1) * width]

    back = gathered(part, half)
    high = back.astype(bf16)
    low = (back - high.astype(f32)).astype(bf16)
    pool = pool_matrix(side)
    spread = lax.dot_general(high, pool, transposed, preferred_element_type=f32)
    spread += lax.dot_general(low, pool, transposed, preferred_element_type=f32)
    for plane in range(2):
        slope = jnp.where(hidden[plane].astype(f32) > 0, 1.0, negative_slope)
        grad_hidden[plane * width : (plane + 1) * width] = (spread * slope).astype(bf16)


def sums_a_kernel(side, plan, grad_hidden, source, even_pairs, odd_pairs, *refs):
    half = plan.samples // 2
    keep, send, (moved, sums) = refs[:half], refs[half:-2], refs[-2:]
    width = plan.width
    chan = source.shape[1]
    before, after = sides(even_pairs[...], odd_pairs[...])
    for index, plane in enumerate((before, source[0], source[1], after)):
        cells = plane.astype(f32)
        for tap in range(9):
            moved[index, tap * chan : (tap + 1) * chan] = shifted(
                cells, tap // 3 - 1, tap % 3 - 1, side
            ).astype(bf16)
    both = grad_hidden[...]
    outer0 = lax.dot_general(moved[0], both[:width], transposed, preferred_element_type=f32)
    inner0 = lax.dot_general(moved[1], both, transposed, preferred_element_type=f32)
    inner1 = lax.dot_general(moved[2], both, transposed, preferred_element_type=f32)
    outer1 = lax.dot_general(moved[3], both[width:], transposed, preferred_element_type=f32)
    tall = 9 * chan
    sums[:tall] = outer0 + inner0[:, width:]
    sums[tall : 2 * tall] = inner0[:, :width] + inner1[:, width:]
    sums[2 * tall : 3 * tall] = inner1[:, :width] + outer1
    sums[3 * tall :] = jnp.zeros((sums.shape[0] - 3 * tall, width), f32)
    me = lax.axis_index("dp")
    rows = keep[0].shape[0]
    for k in range(plan.samples):
        part = sums[pl.ds(pl.multiple_of((me ^ k) * rows, rows), rows)]
        if k % 2:
            send[k // 2][...] = part.astype(bf16)
        else:
            keep[k // 2][...] = part


def halve_kernel(*refs):
    count = len(refs) // 3
    mine, got, out = refs[:count], refs[count : 2 * count], refs[2 * count :]
    for k in range(count):
        total = mine[k][...] + got[k][...].astype(f32)
        out[k // 2 + k % 2 * (count // 2)][...] = total.astype(out[k // 2 + k % 2 * (count // 2)].dtype)


def tap_parts(products):
    chan = products.shape[0] // 9

    def part(b, c):
        tap = 3 * b + c
        return products[tap * chan : (tap + 1) * chan]

    return part


def edges_kernel(side, weight, grad_hidden, even_pairs, odd_pairs, products):
    width = weight.shape[1]
    tall = weight.shape[0] // 3
    both = grad_hidden[...]
    products[...] = jnp.dot(weight[:tall], both[:width], preferred_element_type=f32)
    to_before = gathered(tap_parts(products), side).astype(bf16)
    products[...] = jnp.dot(weight[2 * tall :], both[width:], preferred_element_type=f32)
    to_after = gathered(tap_parts(products), side).astype(bf16)
    even_pairs[...], odd_pairs[...] = for_sides(to_before, to_after)


def own_kernel(side, weight, grad_hidden, own, products):
    tall = weight.shape[0] // 3
    both = grad_hidden[...]
    for plane in range(2):
        mixed = jnp.concatenate(
            [weight[(plane + 1) * tall : (plane + 2) * tall], weight[plane * tall : (plane + 1) * tall]], 1
        )
        products[...] = jnp.dot(mixed, both, preferred_element_type=f32)
        own[plane] = gathered(tap_parts(products), side)


def swapped(part, axis, distance):
    return lax.ppermute(part, axis, [(i, i ^ distance) for i in range(lax.axis_size(axis))])


def per_device(layer_input, hidden_pre, output_pre, output_grad, weight_a, weight_b):
    side = math.isqrt(layer_input.shape[3])
    half = side // 2
    size, small = side * side, half * half
    depth_a = layer_input.shape[2]
    samples, slabs = lax.axis_size("dp"), lax.axis_size("space")
    even = [(i, i ^ 1) for i in range(slabs)]
    odd = [(i, ((i + 1 ^ 1) - 1) % slabs) for i in range(slabs)]
    odd_inside = [(i, k) if abs(i - k) == 1 else (i, i) for i, k in odd]
    shape = jax.ShapeDtypeStruct
    outer = output_pre[0, :, 0].astype(f32)
    grad = (output_grad[0, :, 0].astype(f32) * jnp.where(outer > 0, 1.0, negative_slope)).astype(bf16)
    grad, layer_input, hidden_pre = lax.optimization_barrier((grad, layer_input, hidden_pre))
    grad_sides = [lax.ppermute(grad, "space", pairs) for pairs in (even, odd)]
    source = layer_input[0].transpose(1, 0, 2)
    hidden = hidden_pre[0].transpose(1, 0, 2)
    chan = source.shape[1]
    width_a = hidden.shape[1]
    width_b = grad.shape[0]
    plan = Plan(samples, slabs, chan, width_a, width_b)
    pooled = call(lambda *refs: pool_kernel(side, *refs), shape((width_a, small), bf16), [], 1 << 28, hidden)
    source, pooled = lax.optimization_barrier((source, pooled))
    source_sides = [
        lax.ppermute(part, "space", pairs) for part, pairs in zip(for_sides(source[0], source[1]), (even, odd))
    ]
    channels = 3 * plan.share
    heights = [channels + (plan.width if k == 1 or k % 2 == 0 else 0) for k in range(samples)]
    packed = call(
        lambda *refs: pack_kernel(plan, *refs),
        [shape((height, small), bf16) for height in heights] + [shape(grad.shape, bf16)] * 2,
        [],
        1 << 20,
        pooled,
        grad,
        *grad_sides,
    )
    packed, (before, after) = packed[:-2], packed[-2:]
    crossed = [swapped(packed[k], "dp", k // 2 * 2) for k in range(2, samples)]
    core_b = swapped(packed[1], "dp", 1)
    grad_hidden = call(
        lambda *refs: hidden_kernel(side, *refs),
        shape((2 * width_a, size), bf16),
        [pltpu.VMEM((9 * width_a, small), f32)],
        1 << 30,
        weight_b.reshape(27 * width_a, width_b),
        grad,
        before,
        after,
        hidden,
    )
    halves = call(
        lambda *refs: sums_a_kernel(side, plan, *refs),
        [shape((plan.rows_a * slabs, width_a), kind) for kind in (f32, bf16) for _ in range(samples // 2)],
        [
            pltpu.VMEM((4, 9 * chan, size), bf16),
            pltpu.VMEM((plan.rows_a * samples * slabs, width_a), f32),
        ],
        1 << 30,
        grad_hidden,
        source,
        *source_sides,
    )
    keep, send = halves[: samples // 2], halves[samples // 2 :]
    edges = call(
        lambda *refs: edges_kernel(side, *refs),
        [shape((chan, size), bf16)] * 2,
        [pltpu.VMEM((9 * chan, size), f32)],
        1 << 28,
        weight_a.reshape(27 * chan, width_a),
        grad_hidden,
    )
    got_a, edges = lax.optimization_barrier(([swapped(part, "dp", 1) for part in send], edges))
    for stride in [1 << k for k in range(1, samples.bit_length() - 1)]:
        count = len(keep) // 2
        halves = call(
            halve_kernel,
            [shape(keep[0].shape, kind) for kind in (f32, bf16) for _ in range(count)],
            [],
            1 << 20,
            *keep,
            *got_a,
        )
        keep, send = halves[:count], halves[count:]
        got_a = [swapped(part, "dp", stride) for part in send]
    crossed, keep = lax.optimization_barrier((crossed, keep))
    pooled_parts, channel_parts = [packed[0], core_b], [packed[0], core_b]
    for first, second in zip(crossed[::2], crossed[1::2]):
        pooled_parts += [first, swapped(first[: plan.width], "dp", 1)]
        channel_parts += [first, swapped(second, "dp", 1)]
    totals = call(
        lambda *refs: share_kernel(plan, *refs),
        shape((slabs, plan.rows_b, 128), f32),
        [
            pltpu.VMEM((9 * width_a, samples * small), bf16),
            pltpu.VMEM((slabs * plan.rows_b, 128), f32),
        ],
        1 << 30,
        *pooled_parts,
        *channel_parts,
    )
    from_odd = lax.ppermute(edges[1], "space", odd_inside)
    far = plan.far
    blocks = call(
        lambda *refs: blocks_kernel(plan, *refs),
        [shape((2, plan.block, 128), bf16)] * far,
        [pltpu.VMEM((plan.rows_a * slabs, 128), f32)],
        1 << 20,
        totals,
        keep[0],
        got_a[0],
    )
    parts = blocks[:1] + [swapped(blocks[k], "space", k) for k in range(1, far)]
    own = call(
        lambda *refs: own_kernel(side, *refs),
        shape((2, chan, size), f32),
        [pltpu.VMEM((9 * chan, size), f32)],
        1 << 28,
        weight_a.reshape(27 * chan, width_a),
        grad_hidden,
    )
    parts, from_odd, own = lax.optimization_barrier((parts, from_odd, own))
    both = call(near_kernel, shape((2, plan.block, 128), bf16), [], 1 << 20, *parts)
    there = swapped(both, "space", far)
    both, even_edge = lax.optimization_barrier((both, edges[0]))
    from_even = lax.ppermute(even_edge, "space", even)
    there, from_even = lax.optimization_barrier((there, from_even))
    input_grad = own + jnp.stack(sides(from_even, from_odd)).astype(f32)
    input_grad = input_grad.astype(bf16).transpose(1, 0, 2)[None]
    pair, low = call(
        lambda *refs: far_kernel(plan, *refs),
        [shape((2, rows, 128), bf16) for rows in (plan.block, plan.low)],
        [],
        1 << 20,
        both,
        there,
    )
    strides = [samples >> k for k in range(1, samples.bit_length())]

    def stacked(parts):
        rows = sum(part.shape[0] for part in parts)
        return call(stack_kernel, shape((rows, *parts[0].shape[1:]), bf16), [], 1 << 20, *parts)

    hop = swapped(pair, "dp", strides[0])
    near = [swapped(low, "space", k) for k in range(1, far)]
    first = [swapped(pair, "dp", stride) for stride in strides[1:]]
    pair, hop, near, first = lax.optimization_barrier((pair, hop, near, first))
    lows = stacked(near)
    high = call(
        lambda *refs: high_kernel(plan, *refs),
        shape((4, plan.block - plan.low, 128), bf16),
        [],
        1 << 20,
        pair,
        hop,
    )
    lows_hop = swapped(lows, "dp", strides[0])
    highs = [swapped(high, "space", k) for k in range(1, far)]
    lows_hop, highs, lows, hop, input_grad = lax.optimization_barrier((lows_hop, highs, lows, hop, input_grad))
    known = {0: [pair, hop, lows, lows_hop, *highs]}
    for stride, part in zip(strides[1:], first):
        for k in list(known):
            done = [] if k else [part]
            known[k ^ stride] = done + [swapped(part, "dp", stride) for part in known[k][len(done) :]]
    shares = [known[k] for k in sorted(known)]
    planes_a = depth_a * slabs
    total_a, total_b = call(
        lambda *refs: last_kernel(
            plan,
            1.0 / math.sqrt(samples * planes_a * size),
            1.0 / math.sqrt(samples * (planes_a // 2) * small),
            *refs,
        ),
        [shape((27 * chan, width_a), f32), shape((27 * width_a, width_b), f32)],
        [
            pltpu.VMEM((samples, slabs, plan.block, 128), bf16),
            pltpu.VMEM((27 * chan, width_a), f32),
            pltpu.VMEM((27 * width_a, width_b), f32),
            pltpu.SemaphoreType.DMA((4,)),
        ],
        1 << 20,
        *[part for parts in shares for part in parts],
        out_specs=[pl.BlockSpec(memory_space=pl.ANY)] * 2,
    )
    return (input_grad, total_a.reshape(weight_a.shape), total_b.reshape(weight_b.shape))


def solution(mesh):
    in_specs = (
        P("dp", None, "space", None),
        P("dp", None, "space", None),
        P("dp", None, "space", None),
        P("dp", None, "space", None),
        P(),
        P(),
    )
    out_specs = (P("dp", None, "space", None), P(), P())
    return jax.shard_map(
        per_device, mesh=mesh, in_specs=in_specs, out_specs=out_specs, check_vma=False
    )
```

```python
import math

import jax
import jax.numpy as jnp
from jax import lax
from jax.experimental import pallas as pl
from jax.experimental.pallas import tpu as pltpu
from jax.sharding import PartitionSpec as P

negative_slope = 0.3
f32 = jnp.float32
bf16 = jnp.bfloat16
vmem = pl.BlockSpec(memory_space=pltpu.VMEM)
transposed = (((1,), (1,)), ((), ()))


def shifted(cells, rows, columns, side):
    size = side * side
    offset = rows * side + columns
    if offset:
        cells = pltpu.roll(cells, (-offset) % size, 1)
    place = lax.broadcasted_iota(jnp.int32, cells.shape, 1)
    if rows:
        y = place // side + rows
        cells = jnp.where((y >= 0) & (y < side), cells, 0.0)
    if columns:
        x = place % side + columns
        cells = jnp.where((x >= 0) & (x < side), cells, 0.0)
    return cells


def gathered(parts, side):
    total = None
    for c in range(3):
        line = parts(1, c) + shifted(parts(0, c), 1, 0, side) + shifted(parts(2, c), -1, 0, side)
        line = shifted(line, 0, 1 - c, side)
        total = line if total is None else total + line
    return total


def pool_matrix(side):
    half = side // 2
    fine = lax.broadcasted_iota(jnp.int32, (side * side, half * half), 0)
    coarse = lax.broadcasted_iota(jnp.int32, (side * side, half * half), 1)
    parent = (fine // (2 * side)) * half + (fine % side) // 2
    return jnp.where(parent == coarse, 0.125, 0.0).astype(bf16)


def sides(even_pairs, odd_pairs):
    here = lax.axis_index("space")
    even = here % 2 == 0
    nothing = jnp.zeros(even_pairs.shape, bf16)
    before = jnp.where(here == 0, nothing, jnp.where(even, odd_pairs, even_pairs))
    after = jnp.where(here == lax.axis_size("space") - 1, nothing, jnp.where(even, even_pairs, odd_pairs))
    return before, after


def for_sides(before, after):
    even = lax.axis_index("space") % 2 == 0
    return jnp.where(even, after, before), jnp.where(even, before, after)


def call(kernel, out_shape, scratch, flops, *args, out_specs=None):
    result = pl.pallas_call(
        kernel,
        out_shape=out_shape,
        in_specs=[vmem] * len(args),
        out_specs=out_specs or jax.tree.map(lambda _: vmem, out_shape),
        scratch_shapes=scratch,
        compiler_params=pltpu.CompilerParams(vmem_limit_bytes=48 * 1024 * 1024),
        cost_estimate=pl.CostEstimate(flops=flops >> 12, bytes_accessed=1 << 10, transcendentals=0),
    )(*args)
    return list(result) if isinstance(out_shape, list) else result


def pool_kernel(side, hidden, pooled):
    width = hidden.shape[1]
    pool = pool_matrix(side)
    total = None
    for plane in range(2):
        cells = hidden[plane].astype(f32)
        stacked = jnp.concatenate([jnp.maximum(cells, 0.0), jnp.minimum(cells, 0.0)], 0).astype(bf16)
        part = jnp.dot(stacked, pool, preferred_element_type=f32)
        total = part if total is None else total + part
    pooled[...] = (total[:width] + negative_slope * total[width:]).astype(bf16)


def pack_kernel(plan, pooled, grad, even_pairs, odd_pairs, *refs):
    me = lax.axis_index("dp")
    messages, (before, after) = refs[:-2], refs[-2:]
    before[...], after[...] = sides(even_pairs[...], odd_pairs[...])
    for distance, message in enumerate(messages):
        row = message.shape[0] - 3 * plan.share
        if row:
            message[:row] = pooled[...]
        start = pl.multiple_of((me ^ distance) * plan.share, plan.share)
        for a, plane in enumerate((after, grad, before)):
            message[row + a * plan.share : row + (a + 1) * plan.share] = plane[pl.ds(start, plan.share)]


def share_kernel(plan, *refs):
    pooled, channels, (out, moved, totals) = refs[: plan.samples], refs[plan.samples : -3], refs[-3:]
    size = pooled[0].shape[1]
    half = math.isqrt(size)
    width, share = plan.width, plan.share
    for k, message in enumerate(pooled):
        cells = message[:width]
        cells = cells.astype(f32)
        for tap in range(9):
            moved[tap * width : (tap + 1) * width, k * size : (k + 1) * size] = shifted(
                cells, tap // 3 - 1, tap % 3 - 1, half
            ).astype(bf16)
    right = jnp.concatenate([message[message.shape[0] - 3 * share :] for message in channels], 1)
    result = lax.dot_general(moved[...], right, transposed, preferred_element_type=f32)
    for a in range(3):
        pieces = [
            result[k * plan.tall : (k + 1) * plan.tall, a * share : (a + 1) * share] for k in range(plan.pieces)
        ]
        totals[a * plan.tall : (a + 1) * plan.tall] = jnp.concatenate(pieces, 1)
    spare = totals.shape[0] - 3 * plan.tall
    if spare:
        totals[3 * plan.tall :] = jnp.zeros((spare, 128), f32)
    for slab in range(plan.slabs):
        out[slab] = totals[slab * plan.rows_b : (slab + 1) * plan.rows_b]


def blocks_kernel(plan, totals, *refs):
    mine, got, *blocks, first = refs
    first[...] = mine[...] + got[...].astype(f32)
    me = lax.axis_index("space")
    for distance, block in enumerate(blocks):
        for k in range(2):
            slab = me ^ distance ^ (k * plan.far)
            row = pl.multiple_of(slab * plan.rows_a, plan.rows_a)
            parts = [totals[slab], first[pl.ds(row, plan.rows_a)]]
            spare = plan.block - plan.rows_b - plan.rows_a
            if spare:
                parts.append(jnp.zeros((spare, 128), f32))
            block[k] = jnp.concatenate(parts, 0).astype(bf16)


def near_kernel(*refs):
    total = refs[0][...].astype(f32)
    for part in refs[1:-1]:
        total += part[...].astype(f32)
    refs[-1][...] = total.astype(bf16)


def far_kernel(plan, here, there, pair, low):
    for k in range(2):
        pair[k] = (here[k].astype(f32) + there[1 - k].astype(f32)).astype(bf16)
        low[k] = pair[k, : plan.low]


def flat_kernel(*refs):
    row = 0
    for part in refs[:-1]:
        for k in range(part.shape[0]):
            refs[-1][row : row + part.shape[1]] = part[k]
            row += part.shape[1]


def high_kernel(plan, pair, hop, high):
    for k in range(2):
        high[k], high[2 + k] = pair[k, plan.low :], hop[k, plan.low :]


def stack_kernel(*refs):
    count = refs[0].shape[0]
    for k, part in enumerate(refs[:-1]):
        refs[-1][count * k : count * (k + 1)] = part[...]


def last_kernel(plan, scale_a, scale_b, *refs):
    got, (out_a, out_b, shares, rows_a, rows, sems) = refs[:-6], refs[-6:]
    me, here = lax.axis_index("dp"), lax.axis_index("space")
    far, groups = plan.far, plan.samples // 2
    each = len(got) // groups
    for group in range(groups):
        flat, lows_hop, *highs = got[group * each : (group + 1) * each]
        for hop in range(2):
            sample = me ^ group ^ (hop * groups)
            for k in range(plan.slabs):
                slab = here ^ (k // 2) ^ (k % 2 * far)
                if k < 2:
                    row = (2 * hop + k) * plan.block
                    shares[sample, slab] = flat[row : row + plan.block]
                else:
                    row = 4 * plan.block + (k - 2) * plan.low
                    shares[sample, slab, : plan.low] = lows_hop[k - 2] if hop else flat[row : row + plan.low]
                    shares[sample, slab, plan.low :] = highs[k // 2 - 1][2 * hop + k % 2]
    for sample in range(plan.samples):
        for slab in range(plan.slabs):
            row = (sample * plan.slabs + slab) * plan.rows_a
            height = min(plan.rows_a, out_a.shape[0] - row)
            if height > 0:
                base = plan.rows_b // 16 * 16
                block = shares[sample, slab, base:].astype(f32)[plan.rows_b - base :]
                rows_a[row : row + height] = block[:height] * scale_a
    copy_a = pltpu.make_async_copy(rows_a, out_a, sems.at[3])
    copy_a.start()
    copies = []
    for slab in range(plan.slabs):
        blocks = [shares[sample, slab].astype(f32) for sample in range(plan.samples)]
        for k in range(plan.pieces):
            lanes = slice(k * plan.share, (k + 1) * plan.share)
            wide = jnp.concatenate([block[: plan.rows_b, lanes] for block in blocks], 1) * scale_b
            start, stop = slab * plan.rows_b, min((slab + 1) * plan.rows_b, 3 * plan.tall)
            while start < stop:
                a = start // plan.tall
                end = min(stop, (a + 1) * plan.tall)
                row = (a * (plan.pieces - 1) + k) * plan.tall + start
                rows[row : row + end - start] = wide[start - slab * plan.rows_b : end - slab * plan.rows_b]
                start = end
        height = plan.pieces * plan.tall
        while len(copies) < 3 and (slab + 1) * plan.rows_b >= (len(copies) + 1) * plan.tall:
            place = pl.ds(len(copies) * height, height)
            copies.append(pltpu.make_async_copy(rows.at[place], out_b.at[place], sems.at[len(copies)]))
            copies[-1].start()
    for copy in (copy_a, *copies):
        copy.wait()


class Plan:
    def __init__(self, samples, slabs, chan, width, width_b):
        self.samples, self.slabs, self.width = samples, slabs, width
        self.share = width_b // samples
        self.pieces = 128 // self.share
        self.tall = 9 * width // self.pieces
        self.rows_b = -(-3 * self.tall // (8 * slabs)) * 8
        self.rows_a = -(-27 * chan // (8 * samples * slabs)) * 8
        self.block = -(-(self.rows_b + self.rows_a) // 16) * 16
        self.low = -(-self.block * 4 // 112) * 16
        self.far = slabs // 2


def hidden_kernel(side, weight, grad, before, after, hidden, grad_hidden, products):
    half = side // 2
    width = hidden.shape[1]
    block = 9 * width
    products[...] = jnp.dot(weight[:block], after[...], preferred_element_type=f32)
    products[...] += jnp.dot(weight[block : 2 * block], grad[...], preferred_element_type=f32)
    products[...] += jnp.dot(weight[2 * block :], before[...], preferred_element_type=f32)

    def part(b, c):
        tap = 3 * b + c
        return products[tap * width : (tap + 1) * width]

    back = gathered(part, half)
    high = back.astype(bf16)
    low = (back - high.astype(f32)).astype(bf16)
    pool = pool_matrix(side)
    spread = lax.dot_general(high, pool, transposed, preferred_element_type=f32)
    spread += lax.dot_general(low, pool, transposed, preferred_element_type=f32)
    for plane in range(2):
        slope = jnp.where(hidden[plane].astype(f32) > 0, 1.0, negative_slope)
        grad_hidden[plane * width : (plane + 1) * width] = (spread * slope).astype(bf16)


def sums_a_kernel(side, plan, grad_hidden, source, even_pairs, odd_pairs, *refs):
    half = plan.samples // 2
    keep, send, (moved, sums) = refs[:half], refs[half:-2], refs[-2:]
    width = plan.width
    chan = source.shape[1]
    before, after = sides(even_pairs[...], odd_pairs[...])
    for index, plane in enumerate((before, source[0], source[1], after)):
        cells = plane.astype(f32)
        for tap in range(9):
            moved[index, tap * chan : (tap + 1) * chan] = shifted(
                cells, tap // 3 - 1, tap % 3 - 1, side
            ).astype(bf16)
    both = grad_hidden[...]
    outer0 = lax.dot_general(moved[0], both[:width], transposed, preferred_element_type=f32)
    inner0 = lax.dot_general(moved[1], both, transposed, preferred_element_type=f32)
    inner1 = lax.dot_general(moved[2], both, transposed, preferred_element_type=f32)
    outer1 = lax.dot_general(moved[3], both[width:], transposed, preferred_element_type=f32)
    tall = 9 * chan
    sums[:tall] = outer0 + inner0[:, width:]
    sums[tall : 2 * tall] = inner0[:, :width] + inner1[:, width:]
    sums[2 * tall : 3 * tall] = inner1[:, :width] + outer1
    sums[3 * tall :] = jnp.zeros((sums.shape[0] - 3 * tall, width), f32)
    me = lax.axis_index("dp")
    rows = keep[0].shape[0]
    for k in range(plan.samples):
        part = sums[pl.ds(pl.multiple_of((me ^ k) * rows, rows), rows)]
        if k % 2:
            send[k // 2][...] = part.astype(bf16)
        else:
            keep[k // 2][...] = part


def halve_kernel(*refs):
    count = len(refs) // 3
    mine, got, out = refs[:count], refs[count : 2 * count], refs[2 * count :]
    for k in range(count):
        total = mine[k][...] + got[k][...].astype(f32)
        out[k // 2 + k % 2 * (count // 2)][...] = total.astype(out[k // 2 + k % 2 * (count // 2)].dtype)


def tap_parts(products):
    chan = products.shape[0] // 9

    def part(b, c):
        tap = 3 * b + c
        return products[tap * chan : (tap + 1) * chan]

    return part


def edges_kernel(side, weight, grad_hidden, even_pairs, odd_pairs, products):
    width = weight.shape[1]
    tall = weight.shape[0] // 3
    both = grad_hidden[...]
    products[...] = jnp.dot(weight[:tall], both[:width], preferred_element_type=f32)
    to_before = gathered(tap_parts(products), side).astype(bf16)
    products[...] = jnp.dot(weight[2 * tall :], both[width:], preferred_element_type=f32)
    to_after = gathered(tap_parts(products), side).astype(bf16)
    even_pairs[...], odd_pairs[...] = for_sides(to_before, to_after)


def own_kernel(side, weight, grad_hidden, own, products):
    tall = weight.shape[0] // 3
    both = grad_hidden[...]
    for plane in range(2):
        mixed = jnp.concatenate(
            [weight[(plane + 1) * tall : (plane + 2) * tall], weight[plane * tall : (plane + 1) * tall]], 1
        )
        products[...] = jnp.dot(mixed, both, preferred_element_type=f32)
        own[plane] = gathered(tap_parts(products), side)


def swapped(part, axis, distance):
    return lax.ppermute(part, axis, [(i, i ^ distance) for i in range(lax.axis_size(axis))])


def per_device(layer_input, hidden_pre, output_pre, output_grad, weight_a, weight_b):
    side = math.isqrt(layer_input.shape[3])
    half = side // 2
    size, small = side * side, half * half
    depth_a = layer_input.shape[2]
    samples, slabs = lax.axis_size("dp"), lax.axis_size("space")
    even = [(i, i ^ 1) for i in range(slabs)]
    odd = [(i, ((i + 1 ^ 1) - 1) % slabs) for i in range(slabs)]
    odd_inside = [(i, k) if abs(i - k) == 1 else (i, i) for i, k in odd]
    shape = jax.ShapeDtypeStruct
    outer = output_pre[0, :, 0].astype(f32)
    grad = (output_grad[0, :, 0].astype(f32) * jnp.where(outer > 0, 1.0, negative_slope)).astype(bf16)
    grad, layer_input, hidden_pre = lax.optimization_barrier((grad, layer_input, hidden_pre))
    grad_sides = [lax.ppermute(grad, "space", pairs) for pairs in (even, odd)]
    source = layer_input[0].transpose(1, 0, 2)
    hidden = hidden_pre[0].transpose(1, 0, 2)
    chan = source.shape[1]
    width_a = hidden.shape[1]
    width_b = grad.shape[0]
    plan = Plan(samples, slabs, chan, width_a, width_b)
    pooled = call(lambda *refs: pool_kernel(side, *refs), shape((width_a, small), bf16), [], 1 << 28, hidden)
    source, pooled = lax.optimization_barrier((source, pooled))
    source_sides = [
        lax.ppermute(part, "space", pairs) for part, pairs in zip(for_sides(source[0], source[1]), (even, odd))
    ]
    channels = 3 * plan.share
    heights = [channels + (plan.width if k == 1 or k % 2 == 0 else 0) for k in range(samples)]
    packed = call(
        lambda *refs: pack_kernel(plan, *refs),
        [shape((height, small), bf16) for height in heights] + [shape(grad.shape, bf16)] * 2,
        [],
        1 << 20,
        pooled,
        grad,
        *grad_sides,
    )
    packed, (before, after) = packed[:-2], packed[-2:]
    crossed = [swapped(packed[k], "dp", k // 2 * 2) for k in range(2, samples)]
    core_b = swapped(packed[1], "dp", 1)
    grad_hidden = call(
        lambda *refs: hidden_kernel(side, *refs),
        shape((2 * width_a, size), bf16),
        [pltpu.VMEM((9 * width_a, small), f32)],
        1 << 30,
        weight_b.reshape(27 * width_a, width_b),
        grad,
        before,
        after,
        hidden,
    )
    halves = call(
        lambda *refs: sums_a_kernel(side, plan, *refs),
        [shape((plan.rows_a * slabs, width_a), kind) for kind in (f32, bf16) for _ in range(samples // 2)],
        [
            pltpu.VMEM((4, 9 * chan, size), bf16),
            pltpu.VMEM((plan.rows_a * samples * slabs, width_a), f32),
        ],
        1 << 30,
        grad_hidden,
        source,
        *source_sides,
    )
    keep, send = halves[: samples // 2], halves[samples // 2 :]
    edges = call(
        lambda *refs: edges_kernel(side, *refs),
        [shape((chan, size), bf16)] * 2,
        [pltpu.VMEM((9 * chan, size), f32)],
        1 << 28,
        weight_a.reshape(27 * chan, width_a),
        grad_hidden,
    )
    got_a, edges = lax.optimization_barrier(([swapped(part, "dp", 1) for part in send], edges))
    for stride in [1 << k for k in range(1, samples.bit_length() - 1)]:
        count = len(keep) // 2
        halves = call(
            halve_kernel,
            [shape(keep[0].shape, kind) for kind in (f32, bf16) for _ in range(count)],
            [],
            1 << 20,
            *keep,
            *got_a,
        )
        keep, send = halves[:count], halves[count:]
        got_a = [swapped(part, "dp", stride) for part in send]
    crossed, keep = lax.optimization_barrier((crossed, keep))
    pooled_parts, channel_parts = [packed[0], core_b], [packed[0], core_b]
    for first, second in zip(crossed[::2], crossed[1::2]):
        pooled_parts += [first, swapped(first[: plan.width], "dp", 1)]
        channel_parts += [first, swapped(second, "dp", 1)]
    totals = call(
        lambda *refs: share_kernel(plan, *refs),
        shape((slabs, plan.rows_b, 128), f32),
        [
            pltpu.VMEM((9 * width_a, samples * small), bf16),
            pltpu.VMEM((slabs * plan.rows_b, 128), f32),
        ],
        1 << 30,
        *pooled_parts,
        *channel_parts,
    )
    from_odd = lax.ppermute(edges[1], "space", odd_inside)
    far = plan.far
    blocks = call(
        lambda *refs: blocks_kernel(plan, *refs),
        [shape((2, plan.block, 128), bf16)] * far,
        [pltpu.VMEM((plan.rows_a * slabs, 128), f32)],
        1 << 20,
        totals,
        keep[0],
        got_a[0],
    )
    parts = blocks[:1] + [swapped(blocks[k], "space", k) for k in range(1, far)]
    own = call(
        lambda *refs: own_kernel(side, *refs),
        shape((2, chan, size), f32),
        [pltpu.VMEM((9 * chan, size), f32)],
        1 << 28,
        weight_a.reshape(27 * chan, width_a),
        grad_hidden,
    )
    parts, from_odd, own = lax.optimization_barrier((parts, from_odd, own))
    both = call(near_kernel, shape((2, plan.block, 128), bf16), [], 1 << 20, *parts)
    there = swapped(both, "space", far)
    both, even_edge = lax.optimization_barrier((both, edges[0]))
    from_even = lax.ppermute(even_edge, "space", even)
    there, from_even = lax.optimization_barrier((there, from_even))
    input_grad = own + jnp.stack(sides(from_even, from_odd)).astype(f32)
    input_grad = input_grad.astype(bf16).transpose(1, 0, 2)[None]
    pair, low = call(
        lambda *refs: far_kernel(plan, *refs),
        [shape((2, rows, 128), bf16) for rows in (plan.block, plan.low)],
        [],
        1 << 20,
        both,
        there,
    )
    strides = [samples >> k for k in range(1, samples.bit_length())]

    def stacked(parts):
        rows = sum(part.shape[0] for part in parts)
        return call(stack_kernel, shape((rows, *parts[0].shape[1:]), bf16), [], 1 << 20, *parts)

    hop = swapped(pair, "dp", strides[0])
    near = [swapped(low, "space", k) for k in range(1, far)]
    pair, hop, near = lax.optimization_barrier((pair, hop, near))
    lows = stacked(near)
    rows = 4 * plan.block + (slabs - 2) * plan.low
    flat = call(flat_kernel, shape((rows, 128), bf16), [], 1 << 20, pair, hop, *near)
    first = [swapped(flat, "dp", stride) for stride in strides[1:]]
    high = call(
        lambda *refs: high_kernel(plan, *refs),
        shape((4, plan.block - plan.low, 128), bf16),
        [],
        1 << 20,
        pair,
        hop,
    )
    lows_hop = swapped(lows, "dp", strides[0])
    highs = [swapped(high, "space", k) for k in range(1, far)]
    lows_hop, highs, first, input_grad = lax.optimization_barrier((lows_hop, highs, first, input_grad))
    known = {0: [flat, lows_hop, *highs]}
    for stride, part in zip(strides[1:], first):
        for k in list(known):
            done = [] if k else [part]
            known[k ^ stride] = done + [swapped(part, "dp", stride) for part in known[k][len(done) :]]
    shares = [known[k] for k in sorted(known)]
    planes_a = depth_a * slabs
    total_a, total_b = call(
        lambda *refs: last_kernel(
            plan,
            1.0 / math.sqrt(samples * planes_a * size),
            1.0 / math.sqrt(samples * (planes_a // 2) * small),
            *refs,
        ),
        [shape((27 * chan, width_a), f32), shape((27 * width_a, width_b), f32)],
        [
            pltpu.VMEM((samples, slabs, plan.block, 128), bf16),
            pltpu.VMEM((27 * chan, width_a), f32),
            pltpu.VMEM((27 * width_a, width_b), f32),
            pltpu.SemaphoreType.DMA((4,)),
        ],
        1 << 20,
        *[part for parts in shares for part in parts],
        out_specs=[pl.BlockSpec(memory_space=pl.ANY)] * 2,
    )
    return (input_grad, total_a.reshape(weight_a.shape), total_b.reshape(weight_b.shape))


def solution(mesh):
    in_specs = (
        P("dp", None, "space", None),
        P("dp", None, "space", None),
        P("dp", None, "space", None),
        P("dp", None, "space", None),
        P(),
        P(),
    )
    out_specs = (P("dp", None, "space", None), P(), P())
    return jax.shard_map(
        per_device, mesh=mesh, in_specs=in_specs, out_specs=out_specs, check_vma=False
    )
```

```python
import math

import jax
import jax.numpy as jnp
from jax import lax
from jax.experimental import pallas as pl
from jax.experimental.pallas import tpu as pltpu
from jax.sharding import PartitionSpec as P

negative_slope = 0.3
f32 = jnp.float32
bf16 = jnp.bfloat16
vmem = pl.BlockSpec(memory_space=pltpu.VMEM)
transposed = (((1,), (1,)), ((), ()))


def shifted(cells, rows, columns, side):
    size = side * side
    offset = rows * side + columns
    if offset:
        cells = pltpu.roll(cells, (-offset) % size, 1)
    place = lax.broadcasted_iota(jnp.int32, cells.shape, 1)
    if rows:
        y = place // side + rows
        cells = jnp.where((y >= 0) & (y < side), cells, 0.0)
    if columns:
        x = place % side + columns
        cells = jnp.where((x >= 0) & (x < side), cells, 0.0)
    return cells


def gathered(parts, side):
    total = None
    for c in range(3):
        line = parts(1, c) + shifted(parts(0, c), 1, 0, side) + shifted(parts(2, c), -1, 0, side)
        line = shifted(line, 0, 1 - c, side)
        total = line if total is None else total + line
    return total


def pool_matrix(side):
    half = side // 2
    fine = lax.broadcasted_iota(jnp.int32, (side * side, half * half), 0)
    coarse = lax.broadcasted_iota(jnp.int32, (side * side, half * half), 1)
    parent = (fine // (2 * side)) * half + (fine % side) // 2
    return jnp.where(parent == coarse, 0.125, 0.0).astype(bf16)


def sides(even_pairs, odd_pairs):
    here = lax.axis_index("space")
    even = here % 2 == 0
    nothing = jnp.zeros(even_pairs.shape, bf16)
    before = jnp.where(here == 0, nothing, jnp.where(even, odd_pairs, even_pairs))
    after = jnp.where(here == lax.axis_size("space") - 1, nothing, jnp.where(even, even_pairs, odd_pairs))
    return before, after


def for_sides(before, after):
    even = lax.axis_index("space") % 2 == 0
    return jnp.where(even, after, before), jnp.where(even, before, after)


def call(kernel, out_shape, scratch, flops, *args, out_specs=None):
    result = pl.pallas_call(
        kernel,
        out_shape=out_shape,
        in_specs=[vmem] * len(args),
        out_specs=out_specs or jax.tree.map(lambda _: vmem, out_shape),
        scratch_shapes=scratch,
        compiler_params=pltpu.CompilerParams(vmem_limit_bytes=48 * 1024 * 1024),
        cost_estimate=pl.CostEstimate(flops=flops >> 12, bytes_accessed=1 << 10, transcendentals=0),
    )(*args)
    return list(result) if isinstance(out_shape, list) else result


def pool_kernel(side, hidden, pooled):
    width = hidden.shape[1]
    pool = pool_matrix(side)
    total = None
    for plane in range(2):
        cells = hidden[plane].astype(f32)
        stacked = jnp.concatenate([jnp.maximum(cells, 0.0), jnp.minimum(cells, 0.0)], 0).astype(bf16)
        part = jnp.dot(stacked, pool, preferred_element_type=f32)
        total = part if total is None else total + part
    pooled[...] = (total[:width] + negative_slope * total[width:]).astype(bf16)


def pack_kernel(plan, pooled, grad, even_pairs, odd_pairs, *refs):
    me = lax.axis_index("dp")
    messages, (before, after) = refs[:-2], refs[-2:]
    before[...], after[...] = sides(even_pairs[...], odd_pairs[...])
    for distance, message in enumerate(messages):
        row = message.shape[0] - 3 * plan.share
        if row:
            message[:row] = pooled[...]
        start = pl.multiple_of((me ^ distance) * plan.share, plan.share)
        for a, plane in enumerate((after, grad, before)):
            message[row + a * plan.share : row + (a + 1) * plan.share] = plane[pl.ds(start, plan.share)]


def share_kernel(plan, *refs):
    pooled, channels, (out, moved, totals) = refs[: plan.samples], refs[plan.samples : -3], refs[-3:]
    size = pooled[0].shape[1]
    half = math.isqrt(size)
    width, share = plan.width, plan.share
    for k, message in enumerate(pooled):
        cells = message[:width]
        cells = cells.astype(f32)
        for tap in range(9):
            moved[tap * width : (tap + 1) * width, k * size : (k + 1) * size] = shifted(
                cells, tap // 3 - 1, tap % 3 - 1, half
            ).astype(bf16)
    right = jnp.concatenate([message[message.shape[0] - 3 * share :] for message in channels], 1)
    result = lax.dot_general(moved[...], right, transposed, preferred_element_type=f32)
    for a in range(3):
        pieces = [
            result[k * plan.tall : (k + 1) * plan.tall, a * share : (a + 1) * share] for k in range(plan.pieces)
        ]
        totals[a * plan.tall : (a + 1) * plan.tall] = jnp.concatenate(pieces, 1)
    spare = totals.shape[0] - 3 * plan.tall
    if spare:
        totals[3 * plan.tall :] = jnp.zeros((spare, 128), f32)
    for slab in range(plan.slabs):
        out[slab] = totals[slab * plan.rows_b : (slab + 1) * plan.rows_b]


def blocks_kernel(plan, totals, *refs):
    mine, got, *blocks, first = refs
    first[...] = mine[...] + got[...].astype(f32)
    me = lax.axis_index("space")
    for distance, block in enumerate(blocks):
        for k in range(2):
            slab = me ^ distance ^ (k * plan.far)
            row = pl.multiple_of(slab * plan.rows_a, plan.rows_a)
            parts = [totals[slab], first[pl.ds(row, plan.rows_a)]]
            spare = plan.block - plan.rows_b - plan.rows_a
            if spare:
                parts.append(jnp.zeros((spare, 128), f32))
            block[k] = jnp.concatenate(parts, 0).astype(bf16)


def near_kernel(*refs):
    total = refs[0][...].astype(f32)
    for part in refs[1:-1]:
        total += part[...].astype(f32)
    refs[-1][...] = total.astype(bf16)


def far_kernel(plan, here, there, pair, low):
    for k in range(2):
        pair[k] = (here[k].astype(f32) + there[1 - k].astype(f32)).astype(bf16)
        low[k] = pair[k, : plan.low]


def flat_kernel(*refs):
    row = 0
    for part in refs[:-1]:
        for k in range(part.shape[0]):
            refs[-1][row : row + part.shape[1]] = part[k]
            row += part.shape[1]


def high_kernel(plan, pair, hop, high):
    for k in range(2):
        high[k], high[2 + k] = pair[k, plan.low :], hop[k, plan.low :]


def stack_kernel(*refs):
    count = refs[0].shape[0]
    for k, part in enumerate(refs[:-1]):
        refs[-1][count * k : count * (k + 1)] = part[...]


def last_kernel(plan, scale_a, scale_b, *refs):
    got, (out_a, out_b, shares, rows_a, rows, sems) = refs[:-6], refs[-6:]
    me, here = lax.axis_index("dp"), lax.axis_index("space")
    far, groups = plan.far, plan.samples // 2
    each = len(got) // groups
    for group in range(groups):
        flat, lows_hop, *highs = got[group * each : (group + 1) * each]
        for hop in range(2):
            sample = me ^ group ^ (hop * groups)
            for k in range(plan.slabs):
                slab = here ^ (k // 2) ^ (k % 2 * far)
                if k < 2:
                    row = (2 * hop + k) * plan.block
                    shares[sample, slab] = flat[row : row + plan.block]
                else:
                    row = 4 * plan.block + (k - 2) * plan.low
                    shares[sample, slab, : plan.low] = lows_hop[k - 2] if hop else flat[row : row + plan.low]
                    shares[sample, slab, plan.low :] = highs[k // 2 - 1][2 * hop + k % 2]
    for sample in range(plan.samples):
        for slab in range(plan.slabs):
            row = (sample * plan.slabs + slab) * plan.rows_a
            height = min(plan.rows_a, out_a.shape[0] - row)
            if height > 0:
                base = plan.rows_b // 16 * 16
                block = shares[sample, slab, base:].astype(f32)[plan.rows_b - base :]
                rows_a[row : row + height] = block[:height] * scale_a
    copy_a = pltpu.make_async_copy(rows_a, out_a, sems.at[0])
    copy_a.start()
    copies = []
    for slab in range(plan.slabs):
        blocks = [shares[sample, slab].astype(f32) for sample in range(plan.samples)]
        for k in range(plan.pieces):
            lanes = slice(k * plan.share, (k + 1) * plan.share)
            wide = jnp.concatenate([block[: plan.rows_b, lanes] for block in blocks], 1) * scale_b
            start, stop = slab * plan.rows_b, min((slab + 1) * plan.rows_b, 3 * plan.tall)
            while start < stop:
                a = start // plan.tall
                end = min(stop, (a + 1) * plan.tall)
                row = (a * (plan.pieces - 1) + k) * plan.tall + start
                place = pl.ds(row, end - start)
                rows[place] = wide[start - slab * plan.rows_b : end - slab * plan.rows_b]
                copies.append(pltpu.make_async_copy(rows.at[place], out_b.at[place], sems.at[len(copies) + 1]))
                copies[-1].start()
                start = end
    for copy in (copy_a, *copies):
        copy.wait()


class Plan:
    def __init__(self, samples, slabs, chan, width, width_b):
        self.samples, self.slabs, self.width = samples, slabs, width
        self.share = width_b // samples
        self.pieces = 128 // self.share
        self.tall = 9 * width // self.pieces
        self.rows_b = -(-3 * self.tall // (8 * slabs)) * 8
        self.rows_a = -(-27 * chan // (8 * samples * slabs)) * 8
        self.block = -(-(self.rows_b + self.rows_a) // 16) * 16
        self.low = -(-self.block * 4 // 112) * 16
        self.far = slabs // 2


def hidden_kernel(side, weight, grad, before, after, hidden, grad_hidden, products):
    half = side // 2
    width = hidden.shape[1]
    block = 9 * width
    products[...] = jnp.dot(weight[:block], after[...], preferred_element_type=f32)
    products[...] += jnp.dot(weight[block : 2 * block], grad[...], preferred_element_type=f32)
    products[...] += jnp.dot(weight[2 * block :], before[...], preferred_element_type=f32)

    def part(b, c):
        tap = 3 * b + c
        return products[tap * width : (tap + 1) * width]

    back = gathered(part, half)
    high = back.astype(bf16)
    low = (back - high.astype(f32)).astype(bf16)
    pool = pool_matrix(side)
    spread = lax.dot_general(high, pool, transposed, preferred_element_type=f32)
    spread += lax.dot_general(low, pool, transposed, preferred_element_type=f32)
    for plane in range(2):
        slope = jnp.where(hidden[plane].astype(f32) > 0, 1.0, negative_slope)
        grad_hidden[plane * width : (plane + 1) * width] = (spread * slope).astype(bf16)


def sums_a_kernel(side, plan, grad_hidden, source, even_pairs, odd_pairs, *refs):
    half = plan.samples // 2
    keep, send, (moved, sums) = refs[:half], refs[half:-2], refs[-2:]
    width = plan.width
    chan = source.shape[1]
    before, after = sides(even_pairs[...], odd_pairs[...])
    for index, plane in enumerate((before, source[0], source[1], after)):
        cells = plane.astype(f32)
        for tap in range(9):
            moved[index, tap * chan : (tap + 1) * chan] = shifted(
                cells, tap // 3 - 1, tap % 3 - 1, side
            ).astype(bf16)
    both = grad_hidden[...]
    outer0 = lax.dot_general(moved[0], both[:width], transposed, preferred_element_type=f32)
    inner0 = lax.dot_general(moved[1], both, transposed, preferred_element_type=f32)
    inner1 = lax.dot_general(moved[2], both, transposed, preferred_element_type=f32)
    outer1 = lax.dot_general(moved[3], both[width:], transposed, preferred_element_type=f32)
    tall = 9 * chan
    sums[:tall] = outer0 + inner0[:, width:]
    sums[tall : 2 * tall] = inner0[:, :width] + inner1[:, width:]
    sums[2 * tall : 3 * tall] = inner1[:, :width] + outer1
    sums[3 * tall :] = jnp.zeros((sums.shape[0] - 3 * tall, width), f32)
    me = lax.axis_index("dp")
    rows = keep[0].shape[0]
    for k in range(plan.samples):
        part = sums[pl.ds(pl.multiple_of((me ^ k) * rows, rows), rows)]
        if k % 2:
            send[k // 2][...] = part.astype(bf16)
        else:
            keep[k // 2][...] = part


def halve_kernel(*refs):
    count = len(refs) // 3
    mine, got, out = refs[:count], refs[count : 2 * count], refs[2 * count :]
    for k in range(count):
        total = mine[k][...] + got[k][...].astype(f32)
        out[k // 2 + k % 2 * (count // 2)][...] = total.astype(out[k // 2 + k % 2 * (count // 2)].dtype)


def tap_parts(products):
    chan = products.shape[0] // 9

    def part(b, c):
        tap = 3 * b + c
        return products[tap * chan : (tap + 1) * chan]

    return part


def edges_kernel(side, weight, grad_hidden, even_pairs, odd_pairs, products):
    width = weight.shape[1]
    tall = weight.shape[0] // 3
    both = grad_hidden[...]
    products[...] = jnp.dot(weight[:tall], both[:width], preferred_element_type=f32)
    to_before = gathered(tap_parts(products), side).astype(bf16)
    products[...] = jnp.dot(weight[2 * tall :], both[width:], preferred_element_type=f32)
    to_after = gathered(tap_parts(products), side).astype(bf16)
    even_pairs[...], odd_pairs[...] = for_sides(to_before, to_after)


def own_kernel(side, weight, grad_hidden, own, products):
    tall = weight.shape[0] // 3
    both = grad_hidden[...]
    for plane in range(2):
        mixed = jnp.concatenate(
            [weight[(plane + 1) * tall : (plane + 2) * tall], weight[plane * tall : (plane + 1) * tall]], 1
        )
        products[...] = jnp.dot(mixed, both, preferred_element_type=f32)
        own[plane] = gathered(tap_parts(products), side)


def swapped(part, axis, distance):
    return lax.ppermute(part, axis, [(i, i ^ distance) for i in range(lax.axis_size(axis))])


def per_device(layer_input, hidden_pre, output_pre, output_grad, weight_a, weight_b):
    side = math.isqrt(layer_input.shape[3])
    half = side // 2
    size, small = side * side, half * half
    depth_a = layer_input.shape[2]
    samples, slabs = lax.axis_size("dp"), lax.axis_size("space")
    even = [(i, i ^ 1) for i in range(slabs)]
    odd = [(i, ((i + 1 ^ 1) - 1) % slabs) for i in range(slabs)]
    shape = jax.ShapeDtypeStruct
    outer = output_pre[0, :, 0].astype(f32)
    grad = (output_grad[0, :, 0].astype(f32) * jnp.where(outer > 0, 1.0, negative_slope)).astype(bf16)
    grad, layer_input, hidden_pre = lax.optimization_barrier((grad, layer_input, hidden_pre))
    grad_sides = [lax.ppermute(grad, "space", pairs) for pairs in (even, odd)]
    source = layer_input[0].transpose(1, 0, 2)
    hidden = hidden_pre[0].transpose(1, 0, 2)
    chan = source.shape[1]
    width_a = hidden.shape[1]
    width_b = grad.shape[0]
    plan = Plan(samples, slabs, chan, width_a, width_b)
    pooled = call(lambda *refs: pool_kernel(side, *refs), shape((width_a, small), bf16), [], 1 << 28, hidden)
    source, pooled = lax.optimization_barrier((source, pooled))
    source_sides = [
        lax.ppermute(part, "space", pairs) for part, pairs in zip(for_sides(source[0], source[1]), (even, odd))
    ]
    channels = 3 * plan.share
    heights = [channels + (plan.width if k == 1 or k % 2 == 0 else 0) for k in range(samples)]
    packed = call(
        lambda *refs: pack_kernel(plan, *refs),
        [shape((height, small), bf16) for height in heights] + [shape(grad.shape, bf16)] * 2,
        [],
        1 << 20,
        pooled,
        grad,
        *grad_sides,
    )
    packed, (before, after) = packed[:-2], packed[-2:]
    crossed = [swapped(packed[k], "dp", k // 2 * 2) for k in range(2, samples)]
    core_b = swapped(packed[1], "dp", 1)
    grad_hidden = call(
        lambda *refs: hidden_kernel(side, *refs),
        shape((2 * width_a, size), bf16),
        [pltpu.VMEM((9 * width_a, small), f32)],
        1 << 30,
        weight_b.reshape(27 * width_a, width_b),
        grad,
        before,
        after,
        hidden,
    )
    halves = call(
        lambda *refs: sums_a_kernel(side, plan, *refs),
        [shape((plan.rows_a * slabs, width_a), kind) for kind in (f32, bf16) for _ in range(samples // 2)],
        [
            pltpu.VMEM((4, 9 * chan, size), bf16),
            pltpu.VMEM((plan.rows_a * samples * slabs, width_a), f32),
        ],
        1 << 30,
        grad_hidden,
        source,
        *source_sides,
    )
    keep, send = halves[: samples // 2], halves[samples // 2 :]
    edges = call(
        lambda *refs: edges_kernel(side, *refs),
        [shape((chan, size), bf16)] * 2,
        [pltpu.VMEM((9 * chan, size), f32)],
        1 << 28,
        weight_a.reshape(27 * chan, width_a),
        grad_hidden,
    )
    got_a, edges = lax.optimization_barrier(([swapped(part, "dp", 1) for part in send], edges))
    for stride in [1 << k for k in range(1, samples.bit_length() - 1)]:
        count = len(keep) // 2
        halves = call(
            halve_kernel,
            [shape(keep[0].shape, kind) for kind in (f32, bf16) for _ in range(count)],
            [],
            1 << 20,
            *keep,
            *got_a,
        )
        keep, send = halves[:count], halves[count:]
        got_a = [swapped(part, "dp", stride) for part in send]
    crossed, keep = lax.optimization_barrier((crossed, keep))
    pooled_parts, channel_parts = [packed[0], core_b], [packed[0], core_b]
    for first, second in zip(crossed[::2], crossed[1::2]):
        pooled_parts += [first, swapped(first[: plan.width], "dp", 1)]
        channel_parts += [first, swapped(second, "dp", 1)]
    totals = call(
        lambda *refs: share_kernel(plan, *refs),
        shape((slabs, plan.rows_b, 128), f32),
        [
            pltpu.VMEM((9 * width_a, samples * small), bf16),
            pltpu.VMEM((slabs * plan.rows_b, 128), f32),
        ],
        1 << 30,
        *pooled_parts,
        *channel_parts,
    )
    from_odd = lax.ppermute(edges[1], "space", odd)
    far = plan.far
    blocks = call(
        lambda *refs: blocks_kernel(plan, *refs),
        [shape((2, plan.block, 128), bf16)] * far,
        [pltpu.VMEM((plan.rows_a * slabs, 128), f32)],
        1 << 20,
        totals,
        keep[0],
        got_a[0],
    )
    blocks[far - 1], from_odd = lax.optimization_barrier((blocks[far - 1], from_odd))
    parts = blocks[:1] + [swapped(blocks[k], "space", k) for k in range(1, far)]
    own = call(
        lambda *refs: own_kernel(side, *refs),
        shape((2, chan, size), f32),
        [pltpu.VMEM((9 * chan, size), f32)],
        1 << 28,
        weight_a.reshape(27 * chan, width_a),
        grad_hidden,
    )
    parts, own = lax.optimization_barrier((parts, own))
    both = call(near_kernel, shape((2, plan.block, 128), bf16), [], 1 << 20, *parts)
    there = swapped(both, "space", far)
    both, even_edge = lax.optimization_barrier((both, edges[0]))
    from_even = lax.ppermute(even_edge, "space", even)
    there, from_even = lax.optimization_barrier((there, from_even))
    input_grad = own + jnp.stack(sides(from_even, from_odd)).astype(f32)
    input_grad = input_grad.astype(bf16).transpose(1, 0, 2)[None]
    pair, low = call(
        lambda *refs: far_kernel(plan, *refs),
        [shape((2, rows, 128), bf16) for rows in (plan.block, plan.low)],
        [],
        1 << 20,
        both,
        there,
    )
    strides = [samples >> k for k in range(1, samples.bit_length())]

    def stacked(parts):
        rows = sum(part.shape[0] for part in parts)
        return call(stack_kernel, shape((rows, *parts[0].shape[1:]), bf16), [], 1 << 20, *parts)

    hop = swapped(pair, "dp", strides[0])
    near = [swapped(low, "space", k) for k in range(1, far)]
    pair, hop, near = lax.optimization_barrier((pair, hop, near))
    lows = stacked(near)
    rows = 4 * plan.block + (slabs - 2) * plan.low
    flat = call(flat_kernel, shape((rows, 128), bf16), [], 1 << 20, pair, hop, *near)
    first = [swapped(flat, "dp", stride) for stride in strides[1:]]
    high = call(
        lambda *refs: high_kernel(plan, *refs),
        shape((4, plan.block - plan.low, 128), bf16),
        [],
        1 << 20,
        pair,
        hop,
    )
    lows_hop = swapped(lows, "dp", strides[0])
    highs = [swapped(high, "space", k) for k in range(1, far)]
    lows_hop, highs, first, input_grad = lax.optimization_barrier((lows_hop, highs, first, input_grad))
    known = {0: [flat, lows_hop, *highs]}
    for stride, part in zip(strides[1:], first):
        for k in list(known):
            done = [] if k else [part]
            known[k ^ stride] = done + [swapped(part, "dp", stride) for part in known[k][len(done) :]]
    shares = [known[k] for k in sorted(known)]
    planes_a = depth_a * slabs
    total_a, total_b = call(
        lambda *refs: last_kernel(
            plan,
            1.0 / math.sqrt(samples * planes_a * size),
            1.0 / math.sqrt(samples * (planes_a // 2) * small),
            *refs,
        ),
        [shape((27 * chan, width_a), f32), shape((27 * width_a, width_b), f32)],
        [
            pltpu.VMEM((samples, slabs, plan.block, 128), bf16),
            pltpu.VMEM((27 * chan, width_a), f32),
            pltpu.VMEM((27 * width_a, width_b), f32),
            pltpu.SemaphoreType.DMA((1 + plan.pieces * (slabs + 2),)),
        ],
        1 << 20,
        *[part for parts in shares for part in parts],
        out_specs=[pl.BlockSpec(memory_space=pl.ANY)] * 2,
    )
    return (input_grad, total_a.reshape(weight_a.shape), total_b.reshape(weight_b.shape))


def solution(mesh):
    in_specs = (
        P("dp", None, "space", None),
        P("dp", None, "space", None),
        P("dp", None, "space", None),
        P("dp", None, "space", None),
        P(),
        P(),
    )
    out_specs = (P("dp", None, "space", None), P(), P())
    return jax.shard_map(
        per_device, mesh=mesh, in_specs=in_specs, out_specs=out_specs, check_vma=False
    )
```

```python
import math

import jax
import jax.numpy as jnp
from jax import lax
from jax.experimental import pallas as pl
from jax.experimental.pallas import tpu as pltpu
from jax.sharding import PartitionSpec as P

negative_slope = 0.3
f32 = jnp.float32
bf16 = jnp.bfloat16
vmem = pl.BlockSpec(memory_space=pltpu.VMEM)
transposed = (((1,), (1,)), ((), ()))


def shifted(cells, rows, columns, side):
    size = side * side
    offset = rows * side + columns
    if offset:
        cells = pltpu.roll(cells, (-offset) % size, 1)
    place = lax.broadcasted_iota(jnp.int32, cells.shape, 1)
    if rows:
        y = place // side + rows
        cells = jnp.where((y >= 0) & (y < side), cells, 0.0)
    if columns:
        x = place % side + columns
        cells = jnp.where((x >= 0) & (x < side), cells, 0.0)
    return cells


def gathered(parts, side):
    total = None
    for c in range(3):
        line = parts(1, c) + shifted(parts(0, c), 1, 0, side) + shifted(parts(2, c), -1, 0, side)
        line = shifted(line, 0, 1 - c, side)
        total = line if total is None else total + line
    return total


def pool_matrix(side):
    half = side // 2
    fine = lax.broadcasted_iota(jnp.int32, (side * side, half * half), 0)
    coarse = lax.broadcasted_iota(jnp.int32, (side * side, half * half), 1)
    parent = (fine // (2 * side)) * half + (fine % side) // 2
    return jnp.where(parent == coarse, 0.125, 0.0).astype(bf16)


def sides(even_pairs, odd_pairs):
    here = lax.axis_index("space")
    even = here % 2 == 0
    nothing = jnp.zeros(even_pairs.shape, bf16)
    before = jnp.where(here == 0, nothing, jnp.where(even, odd_pairs, even_pairs))
    after = jnp.where(here == lax.axis_size("space") - 1, nothing, jnp.where(even, even_pairs, odd_pairs))
    return before, after


def for_sides(before, after):
    even = lax.axis_index("space") % 2 == 0
    return jnp.where(even, after, before), jnp.where(even, before, after)


def call(kernel, out_shape, scratch, flops, *args, out_specs=None):
    result = pl.pallas_call(
        kernel,
        out_shape=out_shape,
        in_specs=[vmem] * len(args),
        out_specs=out_specs or jax.tree.map(lambda _: vmem, out_shape),
        scratch_shapes=scratch,
        compiler_params=pltpu.CompilerParams(vmem_limit_bytes=48 * 1024 * 1024),
        cost_estimate=pl.CostEstimate(flops=flops >> 12, bytes_accessed=1 << 10, transcendentals=0),
    )(*args)
    return list(result) if isinstance(out_shape, list) else result


def pool_kernel(side, hidden, pooled, matrix):
    width = hidden.shape[1]
    pool = pool_matrix(side)
    matrix[...] = pool
    total = None
    for plane in range(2):
        cells = hidden[plane].astype(f32)
        stacked = jnp.concatenate([jnp.maximum(cells, 0.0), jnp.minimum(cells, 0.0)], 0).astype(bf16)
        part = jnp.dot(stacked, pool, preferred_element_type=f32)
        total = part if total is None else total + part
    pooled[...] = (total[:width] + negative_slope * total[width:]).astype(bf16)


def pack_kernel(plan, pooled, grad, even_pairs, odd_pairs, *refs):
    me = lax.axis_index("dp")
    messages, (before, after) = refs[:-2], refs[-2:]
    before[...], after[...] = sides(even_pairs[...], odd_pairs[...])
    for distance, message in enumerate(messages):
        row = message.shape[0] - 3 * plan.share
        if row:
            message[:row] = pooled[...]
        start = pl.multiple_of((me ^ distance) * plan.share, plan.share)
        for a, plane in enumerate((after, grad, before)):
            message[row + a * plan.share : row + (a + 1) * plan.share] = plane[pl.ds(start, plan.share)]


def share_kernel(plan, *refs):
    pooled, channels, (out, moved, totals) = refs[: plan.samples], refs[plan.samples : -3], refs[-3:]
    size = pooled[0].shape[1]
    half = math.isqrt(size)
    width, share = plan.width, plan.share
    for k, message in enumerate(pooled):
        cells = message[:width]
        cells = cells.astype(f32)
        for tap in range(9):
            moved[tap * width : (tap + 1) * width, k * size : (k + 1) * size] = shifted(
                cells, tap // 3 - 1, tap % 3 - 1, half
            ).astype(bf16)
    right = jnp.concatenate([message[message.shape[0] - 3 * share :] for message in channels], 1)
    result = lax.dot_general(moved[...], right, transposed, preferred_element_type=f32)
    for a in range(3):
        pieces = [
            result[k * plan.tall : (k + 1) * plan.tall, a * share : (a + 1) * share] for k in range(plan.pieces)
        ]
        totals[a * plan.tall : (a + 1) * plan.tall] = jnp.concatenate(pieces, 1)
    spare = totals.shape[0] - 3 * plan.tall
    if spare:
        totals[3 * plan.tall :] = jnp.zeros((spare, 128), f32)
    for slab in range(plan.slabs):
        out[slab] = totals[slab * plan.rows_b : (slab + 1) * plan.rows_b]


def blocks_kernel(plan, totals, *refs):
    mine, got, *blocks, first = refs
    first[...] = mine[...] + got[...].astype(f32)
    me = lax.axis_index("space")
    for distance, block in enumerate(blocks):
        for k in range(2):
            slab = me ^ distance ^ (k * plan.far)
            row = pl.multiple_of(slab * plan.rows_a, plan.rows_a)
            parts = [totals[slab], first[pl.ds(row, plan.rows_a)]]
            spare = plan.block - plan.rows_b - plan.rows_a
            if spare:
                parts.append(jnp.zeros((spare, 128), f32))
            block[k] = jnp.concatenate(parts, 0).astype(bf16)


def near_kernel(*refs):
    total = refs[0][...].astype(f32)
    for part in refs[1:-1]:
        total += part[...].astype(f32)
    refs[-1][...] = total.astype(bf16)


def far_kernel(plan, here, there, pair, low):
    for k in range(2):
        pair[k] = (here[k].astype(f32) + there[1 - k].astype(f32)).astype(bf16)
        low[k] = pair[k, : plan.low]


def flat_kernel(*refs):
    row = 0
    for part in refs[:-1]:
        for k in range(part.shape[0]):
            refs[-1][row : row + part.shape[1]] = part[k]
            row += part.shape[1]


def high_kernel(plan, pair, hop, high):
    for k in range(2):
        high[k], high[2 + k] = pair[k, plan.low :], hop[k, plan.low :]


def stack_kernel(*refs):
    count = refs[0].shape[0]
    for k, part in enumerate(refs[:-1]):
        refs[-1][count * k : count * (k + 1)] = part[...]


def last_kernel(plan, scale_a, scale_b, *refs):
    got, (out_a, out_b, shares, rows_a, rows, sems) = refs[:-6], refs[-6:]
    me, here = lax.axis_index("dp"), lax.axis_index("space")
    far, groups = plan.far, plan.samples // 2
    each = len(got) // groups
    for group in range(groups):
        flat, lows_hop, *highs = got[group * each : (group + 1) * each]
        for hop in range(2):
            sample = me ^ group ^ (hop * groups)
            for k in range(plan.slabs):
                slab = here ^ (k // 2) ^ (k % 2 * far)
                if k < 2:
                    row = (2 * hop + k) * plan.block
                    shares[sample, slab] = flat[row : row + plan.block]
                else:
                    row = 4 * plan.block + (k - 2) * plan.low
                    shares[sample, slab, : plan.low] = lows_hop[k - 2] if hop else flat[row : row + plan.low]
                    shares[sample, slab, plan.low :] = highs[k // 2 - 1][2 * hop + k % 2]
    for sample in range(plan.samples):
        for slab in range(plan.slabs):
            row = (sample * plan.slabs + slab) * plan.rows_a
            height = min(plan.rows_a, out_a.shape[0] - row)
            if height > 0:
                base = plan.rows_b // 16 * 16
                block = shares[sample, slab, base:].astype(f32)[plan.rows_b - base :]
                rows_a[row : row + height] = block[:height] * scale_a
    copy_a = pltpu.make_async_copy(rows_a, out_a, sems.at[3])
    copy_a.start()
    copies = []
    for slab in range(plan.slabs):
        blocks = [shares[sample, slab].astype(f32) for sample in range(plan.samples)]
        for k in range(plan.pieces):
            lanes = slice(k * plan.share, (k + 1) * plan.share)
            wide = jnp.concatenate([block[: plan.rows_b, lanes] for block in blocks], 1) * scale_b
            start, stop = slab * plan.rows_b, min((slab + 1) * plan.rows_b, 3 * plan.tall)
            while start < stop:
                a = start // plan.tall
                end = min(stop, (a + 1) * plan.tall)
                row = (a * (plan.pieces - 1) + k) * plan.tall + start
                rows[row : row + end - start] = wide[start - slab * plan.rows_b : end - slab * plan.rows_b]
                start = end
        height = plan.pieces * plan.tall
        while len(copies) < 3 and (slab + 1) * plan.rows_b >= (len(copies) + 1) * plan.tall:
            place = pl.ds(len(copies) * height, height)
            copies.append(pltpu.make_async_copy(rows.at[place], out_b.at[place], sems.at[len(copies)]))
            copies[-1].start()
    for copy in (copy_a, *copies):
        copy.wait()


class Plan:
    def __init__(self, samples, slabs, chan, width, width_b):
        self.samples, self.slabs, self.width = samples, slabs, width
        self.share = width_b // samples
        self.pieces = 128 // self.share
        self.tall = 9 * width // self.pieces
        self.rows_b = -(-3 * self.tall // (8 * slabs)) * 8
        self.rows_a = -(-27 * chan // (8 * samples * slabs)) * 8
        self.block = -(-(self.rows_b + self.rows_a) // 16) * 16
        self.low = -(-self.block * 4 // 112) * 16
        self.far = slabs // 2


def hidden_kernel(side, weight, grad, before, after, hidden, matrix, grad_hidden, products):
    half = side // 2
    width = hidden.shape[1]
    block = 9 * width
    taps = jnp.concatenate([weight[a * block : (a + 1) * block] for a in range(3)], 1)
    planes = jnp.concatenate([after[...], grad[...], before[...]], 0)
    products[...] = jnp.dot(taps, planes, preferred_element_type=f32)

    def part(b, c):
        tap = 3 * b + c
        return products[tap * width : (tap + 1) * width]

    back = gathered(part, half)
    high = back.astype(bf16)
    low = (back - high.astype(f32)).astype(bf16)
    pool = matrix[...]
    spread = lax.dot_general(high, pool, transposed, preferred_element_type=f32)
    spread += lax.dot_general(low, pool, transposed, preferred_element_type=f32)
    for plane in range(2):
        slope = jnp.where(hidden[plane].astype(f32) > 0, 1.0, negative_slope)
        grad_hidden[plane * width : (plane + 1) * width] = (spread * slope).astype(bf16)


def taps_kernel(side, source, moved):
    chan = source.shape[1]
    for plane in range(2):
        cells = source[plane].astype(f32)
        for tap in range(9):
            moved[plane, tap * chan : (tap + 1) * chan] = shifted(
                cells, tap // 3 - 1, tap % 3 - 1, side
            ).astype(bf16)


def sums_a_kernel(side, plan, grad_hidden, inner, even_pairs, odd_pairs, *refs):
    half = plan.samples // 2
    keep, send, (moved, sums) = refs[:half], refs[half:-2], refs[-2:]
    width = plan.width
    chan = even_pairs.shape[0]
    before, after = sides(even_pairs[...], odd_pairs[...])
    for index, plane in enumerate((before, after)):
        cells = plane.astype(f32)
        for tap in range(9):
            moved[index, tap * chan : (tap + 1) * chan] = shifted(
                cells, tap // 3 - 1, tap % 3 - 1, side
            ).astype(bf16)
    both = grad_hidden[...]
    outer0 = lax.dot_general(moved[0], both[:width], transposed, preferred_element_type=f32)
    inner0 = lax.dot_general(inner[0], both, transposed, preferred_element_type=f32)
    inner1 = lax.dot_general(inner[1], both, transposed, preferred_element_type=f32)
    outer1 = lax.dot_general(moved[1], both[width:], transposed, preferred_element_type=f32)
    tall = 9 * chan
    sums[:tall] = outer0 + inner0[:, width:]
    sums[tall : 2 * tall] = inner0[:, :width] + inner1[:, width:]
    sums[2 * tall : 3 * tall] = inner1[:, :width] + outer1
    sums[3 * tall :] = jnp.zeros((sums.shape[0] - 3 * tall, width), f32)
    me = lax.axis_index("dp")
    rows = keep[0].shape[0]
    for k in range(plan.samples):
        part = sums[pl.ds(pl.multiple_of((me ^ k) * rows, rows), rows)]
        if k % 2:
            send[k // 2][...] = part.astype(bf16)
        else:
            keep[k // 2][...] = part


def halve_kernel(*refs):
    count = len(refs) // 3
    mine, got, out = refs[:count], refs[count : 2 * count], refs[2 * count :]
    for k in range(count):
        total = mine[k][...] + got[k][...].astype(f32)
        out[k // 2 + k % 2 * (count // 2)][...] = total.astype(out[k // 2 + k % 2 * (count // 2)].dtype)


def tap_parts(products):
    chan = products.shape[0] // 9

    def part(b, c):
        tap = 3 * b + c
        return products[tap * chan : (tap + 1) * chan]

    return part


def edges_kernel(side, weight, grad_hidden, even_pairs, odd_pairs, products):
    width = weight.shape[1]
    tall = weight.shape[0] // 3
    both = grad_hidden[...]
    products[...] = jnp.dot(weight[:tall], both[:width], preferred_element_type=f32)
    to_before = gathered(tap_parts(products), side).astype(bf16)
    products[...] = jnp.dot(weight[2 * tall :], both[width:], preferred_element_type=f32)
    to_after = gathered(tap_parts(products), side).astype(bf16)
    even_pairs[...], odd_pairs[...] = for_sides(to_before, to_after)


def own_kernel(side, weight, grad_hidden, own, products):
    tall = weight.shape[0] // 3
    both = grad_hidden[...]
    for plane in range(2):
        mixed = jnp.concatenate(
            [weight[(plane + 1) * tall : (plane + 2) * tall], weight[plane * tall : (plane + 1) * tall]], 1
        )
        products[...] = jnp.dot(mixed, both, preferred_element_type=f32)
        own[plane] = gathered(tap_parts(products), side)


def swapped(part, axis, distance):
    return lax.ppermute(part, axis, [(i, i ^ distance) for i in range(lax.axis_size(axis))])


def per_device(layer_input, hidden_pre, output_pre, output_grad, weight_a, weight_b):
    side = math.isqrt(layer_input.shape[3])
    half = side // 2
    size, small = side * side, half * half
    depth_a = layer_input.shape[2]
    samples, slabs = lax.axis_size("dp"), lax.axis_size("space")
    even = [(i, i ^ 1) for i in range(slabs)]
    odd = [(i, ((i + 1 ^ 1) - 1) % slabs) for i in range(slabs)]
    odd_inside = [(i, k) if abs(i - k) == 1 else (i, i) for i, k in odd]
    shape = jax.ShapeDtypeStruct
    outer = output_pre[0, :, 0].astype(f32)
    grad = (output_grad[0, :, 0].astype(f32) * jnp.where(outer > 0, 1.0, negative_slope)).astype(bf16)
    grad, layer_input, hidden_pre = lax.optimization_barrier((grad, layer_input, hidden_pre))
    grad_sides = [lax.ppermute(grad, "space", pairs) for pairs in (even, odd)]
    source = layer_input[0].transpose(1, 0, 2)
    hidden = hidden_pre[0].transpose(1, 0, 2)
    chan = source.shape[1]
    width_a = hidden.shape[1]
    width_b = grad.shape[0]
    plan = Plan(samples, slabs, chan, width_a, width_b)
    pooled, matrix = call(
        lambda *refs: pool_kernel(side, *refs),
        [shape((width_a, small), bf16), shape((size, small), bf16)],
        [],
        1 << 28,
        hidden,
    )
    source, pooled = lax.optimization_barrier((source, pooled))
    edge_planes, source = lax.optimization_barrier((for_sides(source[0], source[1]), source))
    source_sides = [lax.ppermute(part, "space", pairs) for part, pairs in zip(edge_planes, (even, odd))]
    inner = call(
        lambda *refs: taps_kernel(side, *refs), shape((2, 9 * chan, size), bf16), [], 1 << 20, source
    )
    grad_sides, inner = lax.optimization_barrier((grad_sides, inner))
    channels = 3 * plan.share
    heights = [channels + (plan.width if k == 1 or k % 2 == 0 else 0) for k in range(samples)]
    packed = call(
        lambda *refs: pack_kernel(plan, *refs),
        [shape((height, small), bf16) for height in heights] + [shape(grad.shape, bf16)] * 2,
        [],
        1 << 20,
        pooled,
        grad,
        *grad_sides,
    )
    packed, (before, after) = packed[:-2], packed[-2:]
    crossed = [swapped(packed[k], "dp", k // 2 * 2) for k in range(2, samples)]
    core_b = swapped(packed[1], "dp", 1)
    grad_hidden = call(
        lambda *refs: hidden_kernel(side, *refs),
        shape((2 * width_a, size), bf16),
        [pltpu.VMEM((9 * width_a, small), f32)],
        1 << 30,
        weight_b.reshape(27 * width_a, width_b),
        grad,
        before,
        after,
        hidden,
        matrix,
    )
    halves = call(
        lambda *refs: sums_a_kernel(side, plan, *refs),
        [shape((plan.rows_a * slabs, width_a), kind) for kind in (f32, bf16) for _ in range(samples // 2)],
        [
            pltpu.VMEM((2, 9 * chan, size), bf16),
            pltpu.VMEM((plan.rows_a * samples * slabs, width_a), f32),
        ],
        1 << 30,
        grad_hidden,
        inner,
        *source_sides,
    )
    keep, send = halves[: samples // 2], halves[samples // 2 :]
    edges = call(
        lambda *refs: edges_kernel(side, *refs),
        [shape((chan, size), bf16)] * 2,
        [pltpu.VMEM((9 * chan, size), f32)],
        1 << 28,
        weight_a.reshape(27 * chan, width_a),
        grad_hidden,
    )
    got_a, edges = lax.optimization_barrier(([swapped(part, "dp", 1) for part in send], edges))
    for stride in [1 << k for k in range(1, samples.bit_length() - 1)]:
        count = len(keep) // 2
        halves = call(
            halve_kernel,
            [shape(keep[0].shape, kind) for kind in (f32, bf16) for _ in range(count)],
            [],
            1 << 20,
            *keep,
            *got_a,
        )
        keep, send = halves[:count], halves[count:]
        got_a = [swapped(part, "dp", stride) for part in send]
    crossed, keep = lax.optimization_barrier((crossed, keep))
    pooled_parts, channel_parts = [packed[0], core_b], [packed[0], core_b]
    for first, second in zip(crossed[::2], crossed[1::2]):
        pooled_parts += [first, swapped(first[: plan.width], "dp", 1)]
        channel_parts += [first, swapped(second, "dp", 1)]
    totals = call(
        lambda *refs: share_kernel(plan, *refs),
        shape((slabs, plan.rows_b, 128), f32),
        [
            pltpu.VMEM((9 * width_a, samples * small), bf16),
            pltpu.VMEM((slabs * plan.rows_b, 128), f32),
        ],
        1 << 30,
        *pooled_parts,
        *channel_parts,
    )
    from_odd = lax.ppermute(edges[1], "space", odd_inside)
    far = plan.far
    blocks = call(
        lambda *refs: blocks_kernel(plan, *refs),
        [shape((2, plan.block, 128), bf16)] * far,
        [pltpu.VMEM((plan.rows_a * slabs, 128), f32)],
        1 << 20,
        totals,
        keep[0],
        got_a[0],
    )
    parts = blocks[:1] + [swapped(blocks[k], "space", k) for k in range(1, far)]
    own = call(
        lambda *refs: own_kernel(side, *refs),
        shape((2, chan, size), f32),
        [pltpu.VMEM((9 * chan, size), f32)],
        1 << 28,
        weight_a.reshape(27 * chan, width_a),
        grad_hidden,
    )
    parts, from_odd, own = lax.optimization_barrier((parts, from_odd, own))
    both = call(near_kernel, shape((2, plan.block, 128), bf16), [], 1 << 20, *parts)
    there = swapped(both, "space", far)
    both, even_edge = lax.optimization_barrier((both, edges[0]))
    from_even = lax.ppermute(even_edge, "space", even)
    there, from_even = lax.optimization_barrier((there, from_even))
    input_grad = own + jnp.stack(sides(from_even, from_odd)).astype(f32)
    input_grad = input_grad.astype(bf16).transpose(1, 0, 2)[None]
    pair, low = call(
        lambda *refs: far_kernel(plan, *refs),
        [shape((2, rows, 128), bf16) for rows in (plan.block, plan.low)],
        [],
        1 << 20,
        both,
        there,
    )
    strides = [samples >> k for k in range(1, samples.bit_length())]

    def stacked(parts):
        rows = sum(part.shape[0] for part in parts)
        return call(stack_kernel, shape((rows, *parts[0].shape[1:]), bf16), [], 1 << 20, *parts)

    hop = swapped(pair, "dp", strides[0])
    near = [swapped(low, "space", k) for k in range(1, far)]
    pair, hop, near = lax.optimization_barrier((pair, hop, near))
    lows = stacked(near)
    rows = 4 * plan.block + (slabs - 2) * plan.low
    flat = call(flat_kernel, shape((rows, 128), bf16), [], 1 << 20, pair, hop, *near)
    first = [swapped(flat, "dp", stride) for stride in strides[1:]]
    high = call(
        lambda *refs: high_kernel(plan, *refs),
        shape((4, plan.block - plan.low, 128), bf16),
        [],
        1 << 20,
        pair,
        hop,
    )
    lows_hop = swapped(lows, "dp", strides[0])
    highs = [swapped(high, "space", k) for k in range(1, far)]
    lows_hop, highs, first, input_grad = lax.optimization_barrier((lows_hop, highs, first, input_grad))
    known = {0: [flat, lows_hop, *highs]}
    for stride, part in zip(strides[1:], first):
        for k in list(known):
            done = [] if k else [part]
            known[k ^ stride] = done + [swapped(part, "dp", stride) for part in known[k][len(done) :]]
    shares = [known[k] for k in sorted(known)]
    planes_a = depth_a * slabs
    total_a, total_b = call(
        lambda *refs: last_kernel(
            plan,
            1.0 / math.sqrt(samples * planes_a * size),
            1.0 / math.sqrt(samples * (planes_a // 2) * small),
            *refs,
        ),
        [shape((27 * chan, width_a), f32), shape((27 * width_a, width_b), f32)],
        [
            pltpu.VMEM((samples, slabs, plan.block, 128), bf16),
            pltpu.VMEM((27 * chan, width_a), f32),
            pltpu.VMEM((27 * width_a, width_b), f32),
            pltpu.SemaphoreType.DMA((4,)),
        ],
        1 << 20,
        *[part for parts in shares for part in parts],
        out_specs=[pl.BlockSpec(memory_space=pl.ANY)] * 2,
    )
    return (input_grad, total_a.reshape(weight_a.shape), total_b.reshape(weight_b.shape))


def solution(mesh):
    in_specs = (
        P("dp", None, "space", None),
        P("dp", None, "space", None),
        P("dp", None, "space", None),
        P("dp", None, "space", None),
        P(),
        P(),
    )
    out_specs = (P("dp", None, "space", None), P(), P())
    return jax.shard_map(
        per_device, mesh=mesh, in_specs=in_specs, out_specs=out_specs, check_vma=False
    )
```

```python
import math

import jax
import jax.numpy as jnp
from jax import lax
from jax.experimental import pallas as pl
from jax.experimental.pallas import tpu as pltpu
from jax.sharding import PartitionSpec as P

negative_slope = 0.3
f32 = jnp.float32
bf16 = jnp.bfloat16
vmem = pl.BlockSpec(memory_space=pltpu.VMEM)
transposed = (((1,), (1,)), ((), ()))


def shifted(cells, rows, columns, side):
    size = side * side
    offset = rows * side + columns
    if offset:
        cells = pltpu.roll(cells, (-offset) % size, 1)
    place = lax.broadcasted_iota(jnp.int32, cells.shape, 1)
    if rows:
        y = place // side + rows
        cells = jnp.where((y >= 0) & (y < side), cells, 0.0)
    if columns:
        x = place % side + columns
        cells = jnp.where((x >= 0) & (x < side), cells, 0.0)
    return cells


def gathered(parts, side):
    total = None
    for c in range(3):
        line = parts(1, c) + shifted(parts(0, c), 1, 0, side) + shifted(parts(2, c), -1, 0, side)
        line = shifted(line, 0, 1 - c, side)
        total = line if total is None else total + line
    return total


def pool_matrix(side):
    half = side // 2
    fine = lax.broadcasted_iota(jnp.int32, (side * side, half * half), 0)
    coarse = lax.broadcasted_iota(jnp.int32, (side * side, half * half), 1)
    parent = (fine // (2 * side)) * half + (fine % side) // 2
    return jnp.where(parent == coarse, 0.125, 0.0).astype(bf16)


def sides(even_pairs, odd_pairs):
    here = lax.axis_index("space")
    even = here % 2 == 0
    nothing = jnp.zeros(even_pairs.shape, bf16)
    before = jnp.where(here == 0, nothing, jnp.where(even, odd_pairs, even_pairs))
    after = jnp.where(here == lax.axis_size("space") - 1, nothing, jnp.where(even, even_pairs, odd_pairs))
    return before, after


def for_sides(before, after):
    even = lax.axis_index("space") % 2 == 0
    return jnp.where(even, after, before), jnp.where(even, before, after)


def call(kernel, out_shape, scratch, flops, *args, out_specs=None):
    result = pl.pallas_call(
        kernel,
        out_shape=out_shape,
        in_specs=[vmem] * len(args),
        out_specs=out_specs or jax.tree.map(lambda _: vmem, out_shape),
        scratch_shapes=scratch,
        compiler_params=pltpu.CompilerParams(vmem_limit_bytes=48 * 1024 * 1024),
        cost_estimate=pl.CostEstimate(flops=flops >> 12, bytes_accessed=1 << 10, transcendentals=0),
    )(*args)
    return list(result) if isinstance(out_shape, list) else result


def pool_kernel(side, hidden, pooled, matrix):
    width = hidden.shape[1]
    pool = pool_matrix(side)
    matrix[...] = pool
    total = None
    for plane in range(2):
        cells = hidden[plane].astype(f32)
        stacked = jnp.concatenate([jnp.maximum(cells, 0.0), jnp.minimum(cells, 0.0)], 0).astype(bf16)
        part = jnp.dot(stacked, pool, preferred_element_type=f32)
        total = part if total is None else total + part
    pooled[...] = (total[:width] + negative_slope * total[width:]).astype(bf16)


def pack_kernel(plan, pooled, grad, even_pairs, odd_pairs, *refs):
    me = lax.axis_index("dp")
    messages, (before, after) = refs[:-2], refs[-2:]
    before[...], after[...] = sides(even_pairs[...], odd_pairs[...])
    for distance, message in enumerate(messages):
        row = message.shape[0] - 3 * plan.share
        if row:
            message[:row] = pooled[...]
        start = pl.multiple_of((me ^ distance) * plan.share, plan.share)
        for a, plane in enumerate((after, grad, before)):
            message[row + a * plan.share : row + (a + 1) * plan.share] = plane[pl.ds(start, plan.share)]


def share_kernel(plan, *refs):
    pooled, channels, (out, moved, totals) = refs[: plan.samples], refs[plan.samples : -3], refs[-3:]
    size = pooled[0].shape[1]
    half = math.isqrt(size)
    width, share = plan.width, plan.share
    for k, message in enumerate(pooled):
        cells = message[:width]
        cells = cells.astype(f32)
        for tap in range(9):
            moved[tap * width : (tap + 1) * width, k * size : (k + 1) * size] = shifted(
                cells, tap // 3 - 1, tap % 3 - 1, half
            ).astype(bf16)
    right = jnp.concatenate([message[message.shape[0] - 3 * share :] for message in channels], 1)
    result = lax.dot_general(moved[...], right, transposed, preferred_element_type=f32)
    for a in range(3):
        pieces = [
            result[k * plan.tall : (k + 1) * plan.tall, a * share : (a + 1) * share] for k in range(plan.pieces)
        ]
        totals[a * plan.tall : (a + 1) * plan.tall] = jnp.concatenate(pieces, 1)
    spare = totals.shape[0] - 3 * plan.tall
    if spare:
        totals[3 * plan.tall :] = jnp.zeros((spare, 128), f32)
    for slab in range(plan.slabs):
        out[slab] = totals[slab * plan.rows_b : (slab + 1) * plan.rows_b]


def blocks_kernel(plan, totals, *refs):
    mine, got, *blocks, first = refs
    first[...] = mine[...] + got[...].astype(f32)
    me = lax.axis_index("space")
    for distance, block in enumerate(blocks):
        for k in range(2):
            slab = me ^ distance ^ (k * plan.far)
            row = pl.multiple_of(slab * plan.rows_a, plan.rows_a)
            parts = [totals[slab], first[pl.ds(row, plan.rows_a)]]
            spare = plan.block - plan.rows_b - plan.rows_a
            if spare:
                parts.append(jnp.zeros((spare, 128), f32))
            block[k] = jnp.concatenate(parts, 0).astype(bf16)


def near_kernel(*refs):
    total = refs[0][...].astype(f32)
    for part in refs[1:-1]:
        total += part[...].astype(f32)
    refs[-1][...] = total.astype(bf16)


def far_kernel(plan, here, there, pair, low):
    for k in range(2):
        pair[k] = (here[k].astype(f32) + there[1 - k].astype(f32)).astype(bf16)
        low[k] = pair[k, : plan.low]


def flat_kernel(*refs):
    row = 0
    for part in refs[:-1]:
        for k in range(part.shape[0]):
            refs[-1][row : row + part.shape[1]] = part[k]
            row += part.shape[1]


def high_kernel(plan, pair, hop, high):
    for k in range(2):
        high[k], high[2 + k] = pair[k, plan.low :], hop[k, plan.low :]


def stack_kernel(*refs):
    count = refs[0].shape[0]
    for k, part in enumerate(refs[:-1]):
        refs[-1][count * k : count * (k + 1)] = part[...]


def last_kernel(plan, scale_a, scale_b, *refs):
    got, (out_a, out_b, shares, rows_a, rows, sems) = refs[:-6], refs[-6:]
    me, here = lax.axis_index("dp"), lax.axis_index("space")
    far, groups = plan.far, plan.samples // 2
    each = len(got) // groups
    for group in range(groups):
        flat, lows_hop, *highs = got[group * each : (group + 1) * each]
        for hop in range(2):
            sample = me ^ group ^ (hop * groups)
            for k in range(plan.slabs):
                slab = here ^ (k // 2) ^ (k % 2 * far)
                if k < 2:
                    row = (2 * hop + k) * plan.block
                    shares[sample, slab] = flat[row : row + plan.block]
                else:
                    row = 4 * plan.block + (k - 2) * plan.low
                    shares[sample, slab, : plan.low] = lows_hop[k - 2] if hop else flat[row : row + plan.low]
                    shares[sample, slab, plan.low :] = highs[k // 2 - 1][2 * hop + k % 2]
    for sample in range(plan.samples):
        for slab in range(plan.slabs):
            row = (sample * plan.slabs + slab) * plan.rows_a
            height = min(plan.rows_a, out_a.shape[0] - row)
            if height > 0:
                base = plan.rows_b // 16 * 16
                block = shares[sample, slab, base:].astype(f32)[plan.rows_b - base :]
                rows_a[row : row + height] = block[:height] * scale_a
    copy_a = pltpu.make_async_copy(rows_a, out_a, sems.at[3])
    copy_a.start()
    copies = []
    for slab in range(plan.slabs):
        blocks = [shares[sample, slab].astype(f32) for sample in range(plan.samples)]
        for k in range(plan.pieces):
            lanes = slice(k * plan.share, (k + 1) * plan.share)
            wide = jnp.concatenate([block[: plan.rows_b, lanes] for block in blocks], 1) * scale_b
            start, stop = slab * plan.rows_b, min((slab + 1) * plan.rows_b, 3 * plan.tall)
            while start < stop:
                a = start // plan.tall
                end = min(stop, (a + 1) * plan.tall)
                row = (a * (plan.pieces - 1) + k) * plan.tall + start
                rows[row : row + end - start] = wide[start - slab * plan.rows_b : end - slab * plan.rows_b]
                start = end
        height = plan.pieces * plan.tall
        while len(copies) < 3 and (slab + 1) * plan.rows_b >= (len(copies) + 1) * plan.tall:
            place = pl.ds(len(copies) * height, height)
            copies.append(pltpu.make_async_copy(rows.at[place], out_b.at[place], sems.at[len(copies)]))
            copies[-1].start()
    for copy in (copy_a, *copies):
        copy.wait()


class Plan:
    def __init__(self, samples, slabs, chan, width, width_b):
        self.samples, self.slabs, self.width = samples, slabs, width
        self.share = width_b // samples
        self.pieces = 128 // self.share
        self.tall = 9 * width // self.pieces
        self.rows_b = -(-3 * self.tall // (8 * slabs)) * 8
        self.rows_a = -(-27 * chan // (8 * samples * slabs)) * 8
        self.block = -(-(self.rows_b + self.rows_a) // 16) * 16
        self.low = -(-self.block * 4 // 112) * 16
        self.far = slabs // 2


def hidden_kernel(side, weight, grad, before, after, hidden, matrix, grad_hidden, products):
    half = side // 2
    width = hidden.shape[1]
    block = 9 * width
    taps = jnp.concatenate([weight[a * block : (a + 1) * block] for a in range(3)], 1)
    planes = jnp.concatenate([after[...], grad[...], before[...]], 0)
    products[...] = jnp.dot(taps, planes, preferred_element_type=f32)

    def part(b, c):
        tap = 3 * b + c
        return products[tap * width : (tap + 1) * width]

    back = gathered(part, half)
    high = back.astype(bf16)
    low = (back - high.astype(f32)).astype(bf16)
    pool = matrix[...]
    spread = lax.dot_general(high, pool, transposed, preferred_element_type=f32)
    spread += lax.dot_general(low, pool, transposed, preferred_element_type=f32)
    for plane in range(2):
        slope = jnp.where(hidden[plane].astype(f32) > 0, 1.0, negative_slope)
        grad_hidden[plane * width : (plane + 1) * width] = (spread * slope).astype(bf16)


def taps_kernel(side, source, moved):
    chan = source.shape[1]
    for plane in range(2):
        cells = source[plane].astype(f32)
        for tap in range(9):
            moved[plane, tap * chan : (tap + 1) * chan] = shifted(
                cells, tap // 3 - 1, tap % 3 - 1, side
            ).astype(bf16)


def sums_a_kernel(side, plan, grad_hidden, inner, even_pairs, odd_pairs, *refs):
    half = plan.samples // 2
    keep, send, (moved, sums) = refs[:half], refs[half:-2], refs[-2:]
    width = plan.width
    chan = even_pairs.shape[0]
    before, after = sides(even_pairs[...], odd_pairs[...])
    for index, plane in enumerate((before, after)):
        cells = plane.astype(f32)
        for tap in range(9):
            moved[index, tap * chan : (tap + 1) * chan] = shifted(
                cells, tap // 3 - 1, tap % 3 - 1, side
            ).astype(bf16)
    both = grad_hidden[...]
    outer0 = lax.dot_general(moved[0], both[:width], transposed, preferred_element_type=f32)
    inner0 = lax.dot_general(inner[0], both, transposed, preferred_element_type=f32)
    inner1 = lax.dot_general(inner[1], both, transposed, preferred_element_type=f32)
    outer1 = lax.dot_general(moved[1], both[width:], transposed, preferred_element_type=f32)
    tall = 9 * chan
    sums[:tall] = outer0 + inner0[:, width:]
    sums[tall : 2 * tall] = inner0[:, :width] + inner1[:, width:]
    sums[2 * tall : 3 * tall] = inner1[:, :width] + outer1
    sums[3 * tall :] = jnp.zeros((sums.shape[0] - 3 * tall, width), f32)
    me = lax.axis_index("dp")
    rows = keep[0].shape[0]
    for k in range(plan.samples):
        part = sums[pl.ds(pl.multiple_of((me ^ k) * rows, rows), rows)]
        if k % 2:
            send[k // 2][...] = part.astype(bf16)
        else:
            keep[k // 2][...] = part


def halve_kernel(*refs):
    count = len(refs) // 3
    mine, got, out = refs[:count], refs[count : 2 * count], refs[2 * count :]
    for k in range(count):
        total = mine[k][...] + got[k][...].astype(f32)
        out[k // 2 + k % 2 * (count // 2)][...] = total.astype(out[k // 2 + k % 2 * (count // 2)].dtype)


def tap_parts(products):
    chan = products.shape[0] // 9

    def part(b, c):
        tap = 3 * b + c
        return products[tap * chan : (tap + 1) * chan]

    return part


def edges_kernel(side, weight, grad_hidden, even_pairs, odd_pairs, products):
    width = weight.shape[1]
    tall = weight.shape[0] // 3
    both = grad_hidden[...]
    products[...] = jnp.dot(weight[:tall], both[:width], preferred_element_type=f32)
    to_before = gathered(tap_parts(products), side).astype(bf16)
    products[...] = jnp.dot(weight[2 * tall :], both[width:], preferred_element_type=f32)
    to_after = gathered(tap_parts(products), side).astype(bf16)
    even_pairs[...], odd_pairs[...] = for_sides(to_before, to_after)


def own_kernel(side, weight, grad_hidden, own, products):
    tall = weight.shape[0] // 3
    both = grad_hidden[...]
    for plane in range(2):
        mixed = jnp.concatenate(
            [weight[(plane + 1) * tall : (plane + 2) * tall], weight[plane * tall : (plane + 1) * tall]], 1
        )
        products[...] = jnp.dot(mixed, both, preferred_element_type=f32)
        own[plane] = gathered(tap_parts(products), side)


def swapped(part, axis, distance):
    return lax.ppermute(part, axis, [(i, i ^ distance) for i in range(lax.axis_size(axis))])


def per_device(layer_input, hidden_pre, output_pre, output_grad, weight_a, weight_b):
    side = math.isqrt(layer_input.shape[3])
    half = side // 2
    size, small = side * side, half * half
    depth_a = layer_input.shape[2]
    samples, slabs = lax.axis_size("dp"), lax.axis_size("space")
    even = [(i, i ^ 1) for i in range(slabs)]
    odd = [(i, ((i + 1 ^ 1) - 1) % slabs) for i in range(slabs)]
    shape = jax.ShapeDtypeStruct
    outer = output_pre[0, :, 0].astype(f32)
    grad = (output_grad[0, :, 0].astype(f32) * jnp.where(outer > 0, 1.0, negative_slope)).astype(bf16)
    grad, layer_input, hidden_pre = lax.optimization_barrier((grad, layer_input, hidden_pre))
    grad_sides = [lax.ppermute(grad, "space", pairs) for pairs in (even, odd)]
    source = layer_input[0].transpose(1, 0, 2)
    hidden = hidden_pre[0].transpose(1, 0, 2)
    chan = source.shape[1]
    width_a = hidden.shape[1]
    width_b = grad.shape[0]
    plan = Plan(samples, slabs, chan, width_a, width_b)
    pooled, matrix = call(
        lambda *refs: pool_kernel(side, *refs),
        [shape((width_a, small), bf16), shape((size, small), bf16)],
        [],
        1 << 28,
        hidden,
    )
    source, pooled = lax.optimization_barrier((source, pooled))
    edge_planes, source = lax.optimization_barrier((for_sides(source[0], source[1]), source))
    source_sides = [lax.ppermute(part, "space", pairs) for part, pairs in zip(edge_planes, (even, odd))]
    inner = call(
        lambda *refs: taps_kernel(side, *refs), shape((2, 9 * chan, size), bf16), [], 1 << 20, source
    )
    grad_sides, inner = lax.optimization_barrier((grad_sides, inner))
    channels = 3 * plan.share
    heights = [channels + (plan.width if k == 1 or k % 2 == 0 else 0) for k in range(samples)]
    packed = call(
        lambda *refs: pack_kernel(plan, *refs),
        [shape((height, small), bf16) for height in heights] + [shape(grad.shape, bf16)] * 2,
        [],
        1 << 20,
        pooled,
        grad,
        *grad_sides,
    )
    packed, (before, after) = packed[:-2], packed[-2:]
    crossed = [swapped(packed[k], "dp", k // 2 * 2) for k in range(2, samples)]
    core_b = swapped(packed[1], "dp", 1)
    grad_hidden = call(
        lambda *refs: hidden_kernel(side, *refs),
        shape((2 * width_a, size), bf16),
        [pltpu.VMEM((9 * width_a, small), f32)],
        1 << 30,
        weight_b.reshape(27 * width_a, width_b),
        grad,
        before,
        after,
        hidden,
        matrix,
    )
    edges = call(
        lambda *refs: edges_kernel(side, *refs),
        [shape((chan, size), bf16)] * 2,
        [pltpu.VMEM((9 * chan, size), f32)],
        1 << 28,
        weight_a.reshape(27 * chan, width_a),
        grad_hidden,
    )
    edges, source_sides = lax.optimization_barrier((edges, source_sides))
    halves = call(
        lambda *refs: sums_a_kernel(side, plan, *refs),
        [shape((plan.rows_a * slabs, width_a), kind) for kind in (f32, bf16) for _ in range(samples // 2)],
        [
            pltpu.VMEM((2, 9 * chan, size), bf16),
            pltpu.VMEM((plan.rows_a * samples * slabs, width_a), f32),
        ],
        1 << 30,
        grad_hidden,
        inner,
        *source_sides,
    )
    keep, send = halves[: samples // 2], halves[samples // 2 :]
    got_a = [swapped(part, "dp", 1) for part in send]
    for stride in [1 << k for k in range(1, samples.bit_length() - 1)]:
        count = len(keep) // 2
        halves = call(
            halve_kernel,
            [shape(keep[0].shape, kind) for kind in (f32, bf16) for _ in range(count)],
            [],
            1 << 20,
            *keep,
            *got_a,
        )
        keep, send = halves[:count], halves[count:]
        got_a = [swapped(part, "dp", stride) for part in send]
    crossed, keep = lax.optimization_barrier((crossed, keep))
    pooled_parts, channel_parts = [packed[0], core_b], [packed[0], core_b]
    for first, second in zip(crossed[::2], crossed[1::2]):
        pooled_parts += [first, swapped(first[: plan.width], "dp", 1)]
        channel_parts += [first, swapped(second, "dp", 1)]
    totals = call(
        lambda *refs: share_kernel(plan, *refs),
        shape((slabs, plan.rows_b, 128), f32),
        [
            pltpu.VMEM((9 * width_a, samples * small), bf16),
            pltpu.VMEM((slabs * plan.rows_b, 128), f32),
        ],
        1 << 30,
        *pooled_parts,
        *channel_parts,
    )
    from_odd = lax.ppermute(edges[1], "space", odd)
    far = plan.far
    totals, from_odd = lax.optimization_barrier((totals, from_odd))
    blocks = call(
        lambda *refs: blocks_kernel(plan, *refs),
        [shape((2, plan.block, 128), bf16)] * far,
        [pltpu.VMEM((plan.rows_a * slabs, 128), f32)],
        1 << 20,
        totals,
        keep[0],
        got_a[0],
    )
    parts = blocks[:1] + [swapped(blocks[k], "space", k) for k in range(1, far)]
    own = call(
        lambda *refs: own_kernel(side, *refs),
        shape((2, chan, size), f32),
        [pltpu.VMEM((9 * chan, size), f32)],
        1 << 28,
        weight_a.reshape(27 * chan, width_a),
        grad_hidden,
    )
    parts, own = lax.optimization_barrier((parts, own))
    both = call(near_kernel, shape((2, plan.block, 128), bf16), [], 1 << 20, *parts)
    there = swapped(both, "space", far)
    both, even_edge = lax.optimization_barrier((both, edges[0]))
    from_even = lax.ppermute(even_edge, "space", even)
    there, from_even = lax.optimization_barrier((there, from_even))
    input_grad = own + jnp.stack(sides(from_even, from_odd)).astype(f32)
    input_grad = input_grad.astype(bf16).transpose(1, 0, 2)[None]
    pair, low = call(
        lambda *refs: far_kernel(plan, *refs),
        [shape((2, rows, 128), bf16) for rows in (plan.block, plan.low)],
        [],
        1 << 20,
        both,
        there,
    )
    strides = [samples >> k for k in range(1, samples.bit_length())]

    def stacked(parts):
        rows = sum(part.shape[0] for part in parts)
        return call(stack_kernel, shape((rows, *parts[0].shape[1:]), bf16), [], 1 << 20, *parts)

    hop = swapped(pair, "dp", strides[0])
    near = [swapped(low, "space", k) for k in range(1, far)]
    pair, hop, near = lax.optimization_barrier((pair, hop, near))
    lows = stacked(near)
    rows = 4 * plan.block + (slabs - 2) * plan.low
    flat = call(flat_kernel, shape((rows, 128), bf16), [], 1 << 20, pair, hop, *near)
    first = [swapped(flat, "dp", stride) for stride in strides[1:]]
    high = call(
        lambda *refs: high_kernel(plan, *refs),
        shape((4, plan.block - plan.low, 128), bf16),
        [],
        1 << 20,
        pair,
        hop,
    )
    lows_hop = swapped(lows, "dp", strides[0])
    highs = [swapped(high, "space", k) for k in range(1, far)]
    lows_hop, highs, first, input_grad = lax.optimization_barrier((lows_hop, highs, first, input_grad))
    known = {0: [flat, lows_hop, *highs]}
    for stride, part in zip(strides[1:], first):
        for k in list(known):
            done = [] if k else [part]
            known[k ^ stride] = done + [swapped(part, "dp", stride) for part in known[k][len(done) :]]
    shares = [known[k] for k in sorted(known)]
    planes_a = depth_a * slabs
    total_a, total_b = call(
        lambda *refs: last_kernel(
            plan,
            1.0 / math.sqrt(samples * planes_a * size),
            1.0 / math.sqrt(samples * (planes_a // 2) * small),
            *refs,
        ),
        [shape((27 * chan, width_a), f32), shape((27 * width_a, width_b), f32)],
        [
            pltpu.VMEM((samples, slabs, plan.block, 128), bf16),
            pltpu.VMEM((27 * chan, width_a), f32),
            pltpu.VMEM((27 * width_a, width_b), f32),
            pltpu.SemaphoreType.DMA((4,)),
        ],
        1 << 20,
        *[part for parts in shares for part in parts],
        out_specs=[pl.BlockSpec(memory_space=pl.ANY)] * 2,
    )
    return (input_grad, total_a.reshape(weight_a.shape), total_b.reshape(weight_b.shape))


def solution(mesh):
    in_specs = (
        P("dp", None, "space", None),
        P("dp", None, "space", None),
        P("dp", None, "space", None),
        P("dp", None, "space", None),
        P(),
        P(),
    )
    out_specs = (P("dp", None, "space", None), P(), P())
    return jax.shard_map(
        per_device, mesh=mesh, in_specs=in_specs, out_specs=out_specs, check_vma=False
    )
```

```python
import math

import jax
import jax.numpy as jnp
from jax import lax
from jax.experimental import pallas as pl
from jax.experimental.pallas import tpu as pltpu
from jax.sharding import PartitionSpec as P

negative_slope = 0.3
f32 = jnp.float32
bf16 = jnp.bfloat16
vmem = pl.BlockSpec(memory_space=pltpu.VMEM)
transposed = (((1,), (1,)), ((), ()))


def shifted(cells, rows, columns, side):
    size = side * side
    offset = rows * side + columns
    if offset:
        cells = pltpu.roll(cells, (-offset) % size, 1)
    place = lax.broadcasted_iota(jnp.int32, cells.shape, 1)
    if rows:
        y = place // side + rows
        cells = jnp.where((y >= 0) & (y < side), cells, 0.0)
    if columns:
        x = place % side + columns
        cells = jnp.where((x >= 0) & (x < side), cells, 0.0)
    return cells


def gathered(parts, side):
    total = None
    for c in range(3):
        line = parts(1, c) + shifted(parts(0, c), 1, 0, side) + shifted(parts(2, c), -1, 0, side)
        line = shifted(line, 0, 1 - c, side)
        total = line if total is None else total + line
    return total


def pool_matrix(side):
    half = side // 2
    fine = lax.broadcasted_iota(jnp.int32, (side * side, half * half), 0)
    coarse = lax.broadcasted_iota(jnp.int32, (side * side, half * half), 1)
    parent = (fine // (2 * side)) * half + (fine % side) // 2
    return jnp.where(parent == coarse, 0.125, 0.0).astype(bf16)


def sides(even_pairs, odd_pairs):
    here = lax.axis_index("space")
    even = here % 2 == 0
    nothing = jnp.zeros(even_pairs.shape, bf16)
    before = jnp.where(here == 0, nothing, jnp.where(even, odd_pairs, even_pairs))
    after = jnp.where(here == lax.axis_size("space") - 1, nothing, jnp.where(even, even_pairs, odd_pairs))
    return before, after


def for_sides(before, after):
    even = lax.axis_index("space") % 2 == 0
    return jnp.where(even, after, before), jnp.where(even, before, after)


def call(kernel, out_shape, scratch, flops, *args, out_specs=None):
    result = pl.pallas_call(
        kernel,
        out_shape=out_shape,
        in_specs=[vmem] * len(args),
        out_specs=out_specs or jax.tree.map(lambda _: vmem, out_shape),
        scratch_shapes=scratch,
        compiler_params=pltpu.CompilerParams(vmem_limit_bytes=48 * 1024 * 1024),
        cost_estimate=pl.CostEstimate(flops=flops >> 12, bytes_accessed=1 << 10, transcendentals=0),
    )(*args)
    return list(result) if isinstance(out_shape, list) else result


def pool_kernel(side, hidden, pooled, matrix):
    width = hidden.shape[1]
    pool = pool_matrix(side)
    matrix[...] = pool
    total = None
    for plane in range(2):
        cells = hidden[plane].astype(f32)
        stacked = jnp.concatenate([jnp.maximum(cells, 0.0), jnp.minimum(cells, 0.0)], 0).astype(bf16)
        part = jnp.dot(stacked, pool, preferred_element_type=f32)
        total = part if total is None else total + part
    pooled[...] = (total[:width] + negative_slope * total[width:]).astype(bf16)


def pack_kernel(plan, pooled, grad, even_pairs, odd_pairs, *refs):
    me = lax.axis_index("dp")
    messages, (before, after) = refs[:-2], refs[-2:]
    before[...], after[...] = sides(even_pairs[...], odd_pairs[...])
    for distance, message in enumerate(messages):
        row = message.shape[0] - 3 * plan.share
        if row:
            message[:row] = pooled[...]
        start = pl.multiple_of((me ^ distance) * plan.share, plan.share)
        for a, plane in enumerate((after, grad, before)):
            message[row + a * plan.share : row + (a + 1) * plan.share] = plane[pl.ds(start, plan.share)]


def share_kernel(plan, *refs):
    pooled, channels, (out, moved, totals) = refs[: plan.samples], refs[plan.samples : -3], refs[-3:]
    size = pooled[0].shape[1]
    half = math.isqrt(size)
    width, share = plan.width, plan.share
    for k, message in enumerate(pooled):
        cells = message[:width]
        cells = cells.astype(f32)
        for tap in range(9):
            moved[tap * width : (tap + 1) * width, k * size : (k + 1) * size] = shifted(
                cells, tap // 3 - 1, tap % 3 - 1, half
            ).astype(bf16)
    right = jnp.concatenate([message[message.shape[0] - 3 * share :] for message in channels], 1)
    result = lax.dot_general(moved[...], right, transposed, preferred_element_type=f32)
    for a in range(3):
        pieces = [
            result[k * plan.tall : (k + 1) * plan.tall, a * share : (a + 1) * share] for k in range(plan.pieces)
        ]
        totals[a * plan.tall : (a + 1) * plan.tall] = jnp.concatenate(pieces, 1)
    spare = totals.shape[0] - 3 * plan.tall
    if spare:
        totals[3 * plan.tall :] = jnp.zeros((spare, 128), f32)
    for slab in range(plan.slabs):
        out[slab] = totals[slab * plan.rows_b : (slab + 1) * plan.rows_b]


def blocks_kernel(plan, totals, *refs):
    mine, got, *blocks, first = refs
    first[...] = mine[...] + got[...].astype(f32)
    me = lax.axis_index("space")
    for distance, block in enumerate(blocks):
        for k in range(2):
            slab = me ^ distance ^ (k * plan.far)
            row = pl.multiple_of(slab * plan.rows_a, plan.rows_a)
            parts = [totals[slab], first[pl.ds(row, plan.rows_a)]]
            spare = plan.block - plan.rows_b - plan.rows_a
            if spare:
                parts.append(jnp.zeros((spare, 128), f32))
            block[k] = jnp.concatenate(parts, 0).astype(bf16)


def near_kernel(*refs):
    total = refs[0][...].astype(f32)
    for part in refs[1:-1]:
        total += part[...].astype(f32)
    refs[-1][...] = total.astype(bf16)


def far_kernel(plan, here, there, pair, low):
    for k in range(2):
        pair[k] = (here[k].astype(f32) + there[1 - k].astype(f32)).astype(bf16)
        low[k] = pair[k, : plan.low]


def flat_kernel(*refs):
    row = 0
    for part in refs[:-1]:
        for k in range(part.shape[0]):
            refs[-1][row : row + part.shape[1]] = part[k]
            row += part.shape[1]


def high_kernel(plan, pair, hop, high):
    for k in range(2):
        high[k], high[2 + k] = pair[k, plan.low :], hop[k, plan.low :]


def stack_kernel(*refs):
    count = refs[0].shape[0]
    for k, part in enumerate(refs[:-1]):
        refs[-1][count * k : count * (k + 1)] = part[...]


def last_kernel(plan, scale_a, scale_b, *refs):
    got, (out_a, out_b, shares, rows_a, rows, sems) = refs[:-6], refs[-6:]
    me, here = lax.axis_index("dp"), lax.axis_index("space")
    far, groups = plan.far, plan.samples // 2
    each = len(got) // groups
    for group in range(groups):
        flat, lows_hop, *highs = got[group * each : (group + 1) * each]
        for hop in range(2):
            sample = me ^ group ^ (hop * groups)
            for k in range(plan.slabs):
                slab = here ^ (k // 2) ^ (k % 2 * far)
                if k < 2:
                    row = (2 * hop + k) * plan.block
                    shares[sample, slab] = flat[row : row + plan.block]
                else:
                    row = 4 * plan.block + (k - 2) * plan.low
                    shares[sample, slab, : plan.low] = lows_hop[k - 2] if hop else flat[row : row + plan.low]
                    shares[sample, slab, plan.low :] = highs[k // 2 - 1][2 * hop + k % 2]
    for sample in range(plan.samples):
        for slab in range(plan.slabs):
            row = (sample * plan.slabs + slab) * plan.rows_a
            height = min(plan.rows_a, out_a.shape[0] - row)
            if height > 0:
                base = plan.rows_b // 16 * 16
                block = shares[sample, slab, base:].astype(f32)[plan.rows_b - base :]
                rows_a[row : row + height] = block[:height] * scale_a
    copy_a = pltpu.make_async_copy(rows_a, out_a, sems.at[3])
    copy_a.start()
    copies = []
    for slab in range(plan.slabs):
        blocks = [shares[sample, slab].astype(f32) for sample in range(plan.samples)]
        for k in range(plan.pieces):
            lanes = slice(k * plan.share, (k + 1) * plan.share)
            wide = jnp.concatenate([block[: plan.rows_b, lanes] for block in blocks], 1) * scale_b
            start, stop = slab * plan.rows_b, min((slab + 1) * plan.rows_b, 3 * plan.tall)
            while start < stop:
                a = start // plan.tall
                end = min(stop, (a + 1) * plan.tall)
                row = (a * (plan.pieces - 1) + k) * plan.tall + start
                rows[row : row + end - start] = wide[start - slab * plan.rows_b : end - slab * plan.rows_b]
                start = end
        height = plan.pieces * plan.tall
        while len(copies) < 3 and (slab + 1) * plan.rows_b >= (len(copies) + 1) * plan.tall:
            place = pl.ds(len(copies) * height, height)
            copies.append(pltpu.make_async_copy(rows.at[place], out_b.at[place], sems.at[len(copies)]))
            copies[-1].start()
    for copy in (copy_a, *copies):
        copy.wait()


class Plan:
    def __init__(self, samples, slabs, chan, width, width_b):
        self.samples, self.slabs, self.width = samples, slabs, width
        self.share = width_b // samples
        self.pieces = 128 // self.share
        self.tall = 9 * width // self.pieces
        self.rows_b = -(-3 * self.tall // (8 * slabs)) * 8
        self.rows_a = -(-27 * chan // (8 * samples * slabs)) * 8
        self.block = -(-(self.rows_b + self.rows_a) // 16) * 16
        self.low = -(-self.block * 5 // 128) * 16
        self.far = slabs // 2


def hidden_kernel(side, weight, grad, before, after, hidden, matrix, grad_hidden, products):
    half = side // 2
    width = hidden.shape[1]
    block = 9 * width
    taps = jnp.concatenate([weight[a * block : (a + 1) * block] for a in range(3)], 1)
    planes = jnp.concatenate([after[...], grad[...], before[...]], 0)
    products[...] = jnp.dot(taps, planes, preferred_element_type=f32)

    def part(b, c):
        tap = 3 * b + c
        return products[tap * width : (tap + 1) * width]

    back = gathered(part, half)
    high = back.astype(bf16)
    low = (back - high.astype(f32)).astype(bf16)
    pool = matrix[...]
    spread = lax.dot_general(high, pool, transposed, preferred_element_type=f32)
    spread += lax.dot_general(low, pool, transposed, preferred_element_type=f32)
    for plane in range(2):
        slope = jnp.where(hidden[plane].astype(f32) > 0, 1.0, negative_slope)
        grad_hidden[plane * width : (plane + 1) * width] = (spread * slope).astype(bf16)


def taps_kernel(side, source, moved):
    chan = source.shape[1]
    for plane in range(2):
        cells = source[plane].astype(f32)
        for tap in range(9):
            moved[plane, tap * chan : (tap + 1) * chan] = shifted(
                cells, tap // 3 - 1, tap % 3 - 1, side
            ).astype(bf16)


def sums_a_kernel(side, plan, grad_hidden, inner, even_pairs, odd_pairs, *refs):
    half = plan.samples // 2
    keep, send, (moved, sums) = refs[:half], refs[half:-2], refs[-2:]
    width = plan.width
    chan = even_pairs.shape[0]
    before, after = sides(even_pairs[...], odd_pairs[...])
    for index, plane in enumerate((before, after)):
        cells = plane.astype(f32)
        for tap in range(9):
            moved[index, tap * chan : (tap + 1) * chan] = shifted(
                cells, tap // 3 - 1, tap % 3 - 1, side
            ).astype(bf16)
    both = grad_hidden[...]
    outer0 = lax.dot_general(moved[0], both[:width], transposed, preferred_element_type=f32)
    inner0 = lax.dot_general(inner[0], both, transposed, preferred_element_type=f32)
    inner1 = lax.dot_general(inner[1], both, transposed, preferred_element_type=f32)
    outer1 = lax.dot_general(moved[1], both[width:], transposed, preferred_element_type=f32)
    tall = 9 * chan
    sums[:tall] = outer0 + inner0[:, width:]
    sums[tall : 2 * tall] = inner0[:, :width] + inner1[:, width:]
    sums[2 * tall : 3 * tall] = inner1[:, :width] + outer1
    sums[3 * tall :] = jnp.zeros((sums.shape[0] - 3 * tall, width), f32)
    me = lax.axis_index("dp")
    rows = keep[0].shape[0]
    for k in range(plan.samples):
        part = sums[pl.ds(pl.multiple_of((me ^ k) * rows, rows), rows)]
        if k % 2:
            send[k // 2][...] = part.astype(bf16)
        else:
            keep[k // 2][...] = part


def halve_kernel(*refs):
    count = len(refs) // 3
    mine, got, out = refs[:count], refs[count : 2 * count], refs[2 * count :]
    for k in range(count):
        total = mine[k][...] + got[k][...].astype(f32)
        out[k // 2 + k % 2 * (count // 2)][...] = total.astype(out[k // 2 + k % 2 * (count // 2)].dtype)


def tap_parts(products):
    chan = products.shape[0] // 9

    def part(b, c):
        tap = 3 * b + c
        return products[tap * chan : (tap + 1) * chan]

    return part


def edges_kernel(side, weight, grad_hidden, even_pairs, odd_pairs, products):
    width = weight.shape[1]
    tall = weight.shape[0] // 3
    both = grad_hidden[...]
    products[...] = jnp.dot(weight[:tall], both[:width], preferred_element_type=f32)
    to_before = gathered(tap_parts(products), side).astype(bf16)
    products[...] = jnp.dot(weight[2 * tall :], both[width:], preferred_element_type=f32)
    to_after = gathered(tap_parts(products), side).astype(bf16)
    even_pairs[...], odd_pairs[...] = for_sides(to_before, to_after)


def own_kernel(side, weight, grad_hidden, own, products):
    tall = weight.shape[0] // 3
    both = grad_hidden[...]
    for plane in range(2):
        mixed = jnp.concatenate(
            [weight[(plane + 1) * tall : (plane + 2) * tall], weight[plane * tall : (plane + 1) * tall]], 1
        )
        products[...] = jnp.dot(mixed, both, preferred_element_type=f32)
        own[plane] = gathered(tap_parts(products), side)


def swapped(part, axis, distance):
    return lax.ppermute(part, axis, [(i, i ^ distance) for i in range(lax.axis_size(axis))])


def per_device(layer_input, hidden_pre, output_pre, output_grad, weight_a, weight_b):
    side = math.isqrt(layer_input.shape[3])
    half = side // 2
    size, small = side * side, half * half
    depth_a = layer_input.shape[2]
    samples, slabs = lax.axis_size("dp"), lax.axis_size("space")
    even = [(i, i ^ 1) for i in range(slabs)]
    odd = [(i, ((i + 1 ^ 1) - 1) % slabs) for i in range(slabs)]
    shape = jax.ShapeDtypeStruct
    outer = output_pre[0, :, 0].astype(f32)
    grad = (output_grad[0, :, 0].astype(f32) * jnp.where(outer > 0, 1.0, negative_slope)).astype(bf16)
    grad, layer_input, hidden_pre = lax.optimization_barrier((grad, layer_input, hidden_pre))
    grad_sides = [lax.ppermute(grad, "space", pairs) for pairs in (even, odd)]
    source = layer_input[0].transpose(1, 0, 2)
    hidden = hidden_pre[0].transpose(1, 0, 2)
    chan = source.shape[1]
    width_a = hidden.shape[1]
    width_b = grad.shape[0]
    plan = Plan(samples, slabs, chan, width_a, width_b)
    pooled, matrix = call(
        lambda *refs: pool_kernel(side, *refs),
        [shape((width_a, small), bf16), shape((size, small), bf16)],
        [],
        1 << 28,
        hidden,
    )
    source, pooled = lax.optimization_barrier((source, pooled))
    edge_planes, source = lax.optimization_barrier((for_sides(source[0], source[1]), source))
    source_sides = [lax.ppermute(part, "space", pairs) for part, pairs in zip(edge_planes, (even, odd))]
    inner = call(
        lambda *refs: taps_kernel(side, *refs), shape((2, 9 * chan, size), bf16), [], 1 << 20, source
    )
    grad_sides, inner = lax.optimization_barrier((grad_sides, inner))
    channels = 3 * plan.share
    heights = [channels + (plan.width if k == 1 or k % 2 == 0 else 0) for k in range(samples)]
    packed = call(
        lambda *refs: pack_kernel(plan, *refs),
        [shape((height, small), bf16) for height in heights] + [shape(grad.shape, bf16)] * 2,
        [],
        1 << 20,
        pooled,
        grad,
        *grad_sides,
    )
    packed, (before, after) = packed[:-2], packed[-2:]
    crossed = [swapped(packed[k], "dp", k // 2 * 2) for k in range(2, samples)]
    core_b = swapped(packed[1], "dp", 1)
    grad_hidden = call(
        lambda *refs: hidden_kernel(side, *refs),
        shape((2 * width_a, size), bf16),
        [pltpu.VMEM((9 * width_a, small), f32)],
        1 << 30,
        weight_b.reshape(27 * width_a, width_b),
        grad,
        before,
        after,
        hidden,
        matrix,
    )
    edges = call(
        lambda *refs: edges_kernel(side, *refs),
        [shape((chan, size), bf16)] * 2,
        [pltpu.VMEM((9 * chan, size), f32)],
        1 << 28,
        weight_a.reshape(27 * chan, width_a),
        grad_hidden,
    )
    edges, source_sides = lax.optimization_barrier((edges, source_sides))
    halves = call(
        lambda *refs: sums_a_kernel(side, plan, *refs),
        [shape((plan.rows_a * slabs, width_a), kind) for kind in (f32, bf16) for _ in range(samples // 2)],
        [
            pltpu.VMEM((2, 9 * chan, size), bf16),
            pltpu.VMEM((plan.rows_a * samples * slabs, width_a), f32),
        ],
        1 << 30,
        grad_hidden,
        inner,
        *source_sides,
    )
    keep, send = halves[: samples // 2], halves[samples // 2 :]
    got_a = [swapped(part, "dp", 1) for part in send]
    for stride in [1 << k for k in range(1, samples.bit_length() - 1)]:
        count = len(keep) // 2
        halves = call(
            halve_kernel,
            [shape(keep[0].shape, kind) for kind in (f32, bf16) for _ in range(count)],
            [],
            1 << 20,
            *keep,
            *got_a,
        )
        keep, send = halves[:count], halves[count:]
        got_a = [swapped(part, "dp", stride) for part in send]
    crossed, keep = lax.optimization_barrier((crossed, keep))
    pooled_parts, channel_parts = [packed[0], core_b], [packed[0], core_b]
    for first, second in zip(crossed[::2], crossed[1::2]):
        pooled_parts += [first, swapped(first[: plan.width], "dp", 1)]
        channel_parts += [first, swapped(second, "dp", 1)]
    totals = call(
        lambda *refs: share_kernel(plan, *refs),
        shape((slabs, plan.rows_b, 128), f32),
        [
            pltpu.VMEM((9 * width_a, samples * small), bf16),
            pltpu.VMEM((slabs * plan.rows_b, 128), f32),
        ],
        1 << 30,
        *pooled_parts,
        *channel_parts,
    )
    from_odd = lax.ppermute(edges[1], "space", odd)
    far = plan.far
    totals, from_odd = lax.optimization_barrier((totals, from_odd))
    blocks = call(
        lambda *refs: blocks_kernel(plan, *refs),
        [shape((2, plan.block, 128), bf16)] * far,
        [pltpu.VMEM((plan.rows_a * slabs, 128), f32)],
        1 << 20,
        totals,
        keep[0],
        got_a[0],
    )
    parts = blocks[:1] + [swapped(blocks[k], "space", k) for k in range(1, far)]
    own = call(
        lambda *refs: own_kernel(side, *refs),
        shape((2, chan, size), f32),
        [pltpu.VMEM((9 * chan, size), f32)],
        1 << 28,
        weight_a.reshape(27 * chan, width_a),
        grad_hidden,
    )
    parts, own = lax.optimization_barrier((parts, own))
    both = call(near_kernel, shape((2, plan.block, 128), bf16), [], 1 << 20, *parts)
    there = swapped(both, "space", far)
    both, even_edge = lax.optimization_barrier((both, edges[0]))
    from_even = lax.ppermute(even_edge, "space", even)
    there, from_even = lax.optimization_barrier((there, from_even))
    input_grad = own + jnp.stack(sides(from_even, from_odd)).astype(f32)
    input_grad = input_grad.astype(bf16).transpose(1, 0, 2)[None]
    pair, low = call(
        lambda *refs: far_kernel(plan, *refs),
        [shape((2, rows, 128), bf16) for rows in (plan.block, plan.low)],
        [],
        1 << 20,
        both,
        there,
    )
    strides = [samples >> k for k in range(1, samples.bit_length())]

    def stacked(parts):
        rows = sum(part.shape[0] for part in parts)
        return call(stack_kernel, shape((rows, *parts[0].shape[1:]), bf16), [], 1 << 20, *parts)

    hop = swapped(pair, "dp", strides[0])
    near = [swapped(low, "space", k) for k in range(1, far)]
    pair, hop, near = lax.optimization_barrier((pair, hop, near))
    lows = stacked(near)
    rows = 4 * plan.block + (slabs - 2) * plan.low
    flat = call(flat_kernel, shape((rows, 128), bf16), [], 1 << 20, pair, hop, *near)
    first = [swapped(flat, "dp", stride) for stride in strides[1:]]
    high = call(
        lambda *refs: high_kernel(plan, *refs),
        shape((4, plan.block - plan.low, 128), bf16),
        [],
        1 << 20,
        pair,
        hop,
    )
    lows_hop = swapped(lows, "dp", strides[0])
    highs = [swapped(high, "space", k) for k in range(1, far)]
    lows_hop, highs, first, input_grad = lax.optimization_barrier((lows_hop, highs, first, input_grad))
    known = {0: [flat, lows_hop, *highs]}
    for stride, part in zip(strides[1:], first):
        for k in list(known):
            done = [] if k else [part]
            known[k ^ stride] = done + [swapped(part, "dp", stride) for part in known[k][len(done) :]]
    shares = [known[k] for k in sorted(known)]
    planes_a = depth_a * slabs
    total_a, total_b = call(
        lambda *refs: last_kernel(
            plan,
            1.0 / math.sqrt(samples * planes_a * size),
            1.0 / math.sqrt(samples * (planes_a // 2) * small),
            *refs,
        ),
        [shape((27 * chan, width_a), f32), shape((27 * width_a, width_b), f32)],
        [
            pltpu.VMEM((samples, slabs, plan.block, 128), bf16),
            pltpu.VMEM((27 * chan, width_a), f32),
            pltpu.VMEM((27 * width_a, width_b), f32),
            pltpu.SemaphoreType.DMA((4,)),
        ],
        1 << 20,
        *[part for parts in shares for part in parts],
        out_specs=[pl.BlockSpec(memory_space=pl.ANY)] * 2,
    )
    return (input_grad, total_a.reshape(weight_a.shape), total_b.reshape(weight_b.shape))


def solution(mesh):
    in_specs = (
        P("dp", None, "space", None),
        P("dp", None, "space", None),
        P("dp", None, "space", None),
        P("dp", None, "space", None),
        P(),
        P(),
    )
    out_specs = (P("dp", None, "space", None), P(), P())
    return jax.shard_map(
        per_device, mesh=mesh, in_specs=in_specs, out_specs=out_specs, check_vma=False
    )
```

```python
import math

import jax
import jax.numpy as jnp
from jax import lax
from jax.experimental import pallas as pl
from jax.experimental.pallas import tpu as pltpu
from jax.sharding import PartitionSpec as P

negative_slope = 0.3
f32 = jnp.float32
bf16 = jnp.bfloat16
vmem = pl.BlockSpec(memory_space=pltpu.VMEM)
transposed = (((1,), (1,)), ((), ()))


def shifted(cells, rows, columns, side):
    size = side * side
    offset = rows * side + columns
    if offset:
        cells = pltpu.roll(cells, (-offset) % size, 1)
    place = lax.broadcasted_iota(jnp.int32, cells.shape, 1)
    if rows:
        y = place // side + rows
        cells = jnp.where((y >= 0) & (y < side), cells, 0.0)
    if columns:
        x = place % side + columns
        cells = jnp.where((x >= 0) & (x < side), cells, 0.0)
    return cells


def gathered(parts, side):
    total = None
    for c in range(3):
        line = parts(1, c) + shifted(parts(0, c), 1, 0, side) + shifted(parts(2, c), -1, 0, side)
        line = shifted(line, 0, 1 - c, side)
        total = line if total is None else total + line
    return total


def pool_matrix(side):
    half = side // 2
    fine = lax.broadcasted_iota(jnp.int32, (side * side, half * half), 0)
    coarse = lax.broadcasted_iota(jnp.int32, (side * side, half * half), 1)
    parent = (fine // (2 * side)) * half + (fine % side) // 2
    return jnp.where(parent == coarse, 0.125, 0.0).astype(bf16)


def sides(even_pairs, odd_pairs):
    here = lax.axis_index("space")
    even = here % 2 == 0
    nothing = jnp.zeros(even_pairs.shape, bf16)
    before = jnp.where(here == 0, nothing, jnp.where(even, odd_pairs, even_pairs))
    after = jnp.where(here == lax.axis_size("space") - 1, nothing, jnp.where(even, even_pairs, odd_pairs))
    return before, after


def for_sides(before, after):
    even = lax.axis_index("space") % 2 == 0
    return jnp.where(even, after, before), jnp.where(even, before, after)


def call(kernel, out_shape, scratch, flops, *args, out_specs=None):
    result = pl.pallas_call(
        kernel,
        out_shape=out_shape,
        in_specs=[vmem] * len(args),
        out_specs=out_specs or jax.tree.map(lambda _: vmem, out_shape),
        scratch_shapes=scratch,
        compiler_params=pltpu.CompilerParams(vmem_limit_bytes=48 * 1024 * 1024),
        cost_estimate=pl.CostEstimate(flops=flops >> 12, bytes_accessed=1 << 10, transcendentals=0),
    )(*args)
    return list(result) if isinstance(out_shape, list) else result


def pool_kernel(side, hidden, pooled, matrix):
    width = hidden.shape[1]
    pool = pool_matrix(side)
    matrix[...] = pool
    total = None
    for plane in range(2):
        cells = hidden[plane].astype(f32)
        stacked = jnp.concatenate([jnp.maximum(cells, 0.0), jnp.minimum(cells, 0.0)], 0).astype(bf16)
        part = jnp.dot(stacked, pool, preferred_element_type=f32)
        total = part if total is None else total + part
    pooled[...] = (total[:width] + negative_slope * total[width:]).astype(bf16)


def pack_kernel(plan, pooled, grad, even_pairs, odd_pairs, *refs):
    me = lax.axis_index("dp")
    messages, (before, after) = refs[:-2], refs[-2:]
    before[...], after[...] = sides(even_pairs[...], odd_pairs[...])
    for distance, message in enumerate(messages):
        row = message.shape[0] - 3 * plan.share
        if row:
            message[:row] = pooled[...]
        start = pl.multiple_of((me ^ distance) * plan.share, plan.share)
        for a, plane in enumerate((after, grad, before)):
            message[row + a * plan.share : row + (a + 1) * plan.share] = plane[pl.ds(start, plan.share)]


def share_kernel(plan, *refs):
    pooled, channels, (out, moved, totals) = refs[: plan.samples], refs[plan.samples : -3], refs[-3:]
    size = pooled[0].shape[1]
    half = math.isqrt(size)
    width, share = plan.width, plan.share
    for k, message in enumerate(pooled):
        cells = message[:width]
        cells = cells.astype(f32)
        for tap in range(9):
            moved[tap * width : (tap + 1) * width, k * size : (k + 1) * size] = shifted(
                cells, tap // 3 - 1, tap % 3 - 1, half
            ).astype(bf16)
    right = jnp.concatenate([message[message.shape[0] - 3 * share :] for message in channels], 1)
    result = lax.dot_general(moved[...], right, transposed, preferred_element_type=f32)
    for a in range(3):
        pieces = [
            result[k * plan.tall : (k + 1) * plan.tall, a * share : (a + 1) * share] for k in range(plan.pieces)
        ]
        totals[a * plan.tall : (a + 1) * plan.tall] = jnp.concatenate(pieces, 1)
    spare = totals.shape[0] - 3 * plan.tall
    if spare:
        totals[3 * plan.tall :] = jnp.zeros((spare, 128), f32)
    for slab in range(plan.slabs):
        out[slab] = totals[slab * plan.rows_b : (slab + 1) * plan.rows_b]


def blocks_kernel(plan, totals, *refs):
    mine, got, *blocks, first = refs
    first[...] = mine[...] + got[...].astype(f32)
    me = lax.axis_index("space")
    for distance, block in enumerate(blocks):
        for k in range(2):
            slab = me ^ distance ^ (k * plan.far)
            row = pl.multiple_of(slab * plan.rows_a, plan.rows_a)
            parts = [totals[slab], first[pl.ds(row, plan.rows_a)]]
            spare = plan.block - plan.rows_b - plan.rows_a
            if spare:
                parts.append(jnp.zeros((spare, 128), f32))
            block[k] = jnp.concatenate(parts, 0).astype(bf16)


def near_kernel(*refs):
    total = refs[0][...].astype(f32)
    for part in refs[1:-1]:
        total += part[...].astype(f32)
    refs[-1][...] = total.astype(bf16)


def far_kernel(plan, here, there, pair, low):
    for k in range(2):
        pair[k] = (here[k].astype(f32) + there[1 - k].astype(f32)).astype(bf16)
        low[k] = pair[k, : plan.low]


def flat_kernel(*refs):
    row = 0
    for part in refs[:-1]:
        for k in range(part.shape[0]):
            refs[-1][row : row + part.shape[1]] = part[k]
            row += part.shape[1]


def high_kernel(plan, pair, hop, high):
    for k in range(2):
        high[k], high[2 + k] = pair[k, plan.low :], hop[k, plan.low :]


def stack_kernel(*refs):
    count = refs[0].shape[0]
    for k, part in enumerate(refs[:-1]):
        refs[-1][count * k : count * (k + 1)] = part[...]


def last_kernel(plan, scale_a, scale_b, *refs):
    got, (out_a, out_b, shares, rows_a, rows, sems) = refs[:-6], refs[-6:]
    me, here = lax.axis_index("dp"), lax.axis_index("space")
    far, groups = plan.far, plan.samples // 2
    each = len(got) // groups
    for group in range(groups):
        flat, lows_hop, *highs = got[group * each : (group + 1) * each]
        for hop in range(2):
            sample = me ^ group ^ (hop * groups)
            for k in range(plan.slabs):
                slab = here ^ (k // 2) ^ (k % 2 * far)
                if k < 2:
                    row = (2 * hop + k) * plan.block
                    shares[sample, slab] = flat[row : row + plan.block]
                else:
                    row = 4 * plan.block + (k - 2) * plan.low
                    shares[sample, slab, : plan.low] = lows_hop[k - 2] if hop else flat[row : row + plan.low]
                    shares[sample, slab, plan.low :] = highs[k // 2 - 1][2 * hop + k % 2]
    for sample in range(plan.samples):
        for slab in range(plan.slabs):
            row = (sample * plan.slabs + slab) * plan.rows_a
            height = min(plan.rows_a, out_a.shape[0] - row)
            if height > 0:
                base = plan.rows_b // 16 * 16
                block = shares[sample, slab, base:].astype(f32)[plan.rows_b - base :]
                rows_a[row : row + height] = block[:height] * scale_a
    copy_a = pltpu.make_async_copy(rows_a, out_a, sems.at[3])
    copy_a.start()
    copies = []
    for slab in range(plan.slabs):
        blocks = [shares[sample, slab].astype(f32) for sample in range(plan.samples)]
        for k in range(plan.pieces):
            lanes = slice(k * plan.share, (k + 1) * plan.share)
            wide = jnp.concatenate([block[: plan.rows_b, lanes] for block in blocks], 1) * scale_b
            start, stop = slab * plan.rows_b, min((slab + 1) * plan.rows_b, 3 * plan.tall)
            while start < stop:
                a = start // plan.tall
                end = min(stop, (a + 1) * plan.tall)
                row = (a * (plan.pieces - 1) + k) * plan.tall + start
                rows[row : row + end - start] = wide[start - slab * plan.rows_b : end - slab * plan.rows_b]
                start = end
        height = plan.pieces * plan.tall
        while len(copies) < 3 and (slab + 1) * plan.rows_b >= (len(copies) + 1) * plan.tall:
            place = pl.ds(len(copies) * height, height)
            copies.append(pltpu.make_async_copy(rows.at[place], out_b.at[place], sems.at[len(copies)]))
            copies[-1].start()
    for copy in (copy_a, *copies):
        copy.wait()


class Plan:
    def __init__(self, samples, slabs, chan, width, width_b):
        self.samples, self.slabs, self.width = samples, slabs, width
        self.share = width_b // samples
        self.pieces = 128 // self.share
        self.tall = 9 * width // self.pieces
        self.rows_b = -(-3 * self.tall // (8 * slabs)) * 8
        self.rows_a = -(-27 * chan // (8 * samples * slabs)) * 8
        self.block = -(-(self.rows_b + self.rows_a) // 16) * 16
        self.low = -(-self.block * 11 // 256) * 16
        self.far = slabs // 2


def hidden_kernel(side, weight, grad, before, after, hidden, matrix, grad_hidden, products):
    half = side // 2
    width = hidden.shape[1]
    block = 9 * width
    taps = jnp.concatenate([weight[a * block : (a + 1) * block] for a in range(3)], 1)
    planes = jnp.concatenate([after[...], grad[...], before[...]], 0)
    products[...] = jnp.dot(taps, planes, preferred_element_type=f32)

    def part(b, c):
        tap = 3 * b + c
        return products[tap * width : (tap + 1) * width]

    back = gathered(part, half)
    high = back.astype(bf16)
    low = (back - high.astype(f32)).astype(bf16)
    pool = matrix[...]
    spread = lax.dot_general(high, pool, transposed, preferred_element_type=f32)
    spread += lax.dot_general(low, pool, transposed, preferred_element_type=f32)
    for plane in range(2):
        slope = jnp.where(hidden[plane].astype(f32) > 0, 1.0, negative_slope)
        grad_hidden[plane * width : (plane + 1) * width] = (spread * slope).astype(bf16)


def taps_kernel(side, source, moved):
    chan = source.shape[1]
    for plane in range(2):
        cells = source[plane].astype(f32)
        for tap in range(9):
            moved[plane, tap * chan : (tap + 1) * chan] = shifted(
                cells, tap // 3 - 1, tap % 3 - 1, side
            ).astype(bf16)


def sums_a_kernel(side, plan, grad_hidden, inner, even_pairs, odd_pairs, *refs):
    half = plan.samples // 2
    keep, send, (moved, sums) = refs[:half], refs[half:-2], refs[-2:]
    width = plan.width
    chan = even_pairs.shape[0]
    before, after = sides(even_pairs[...], odd_pairs[...])
    for index, plane in enumerate((before, after)):
        cells = plane.astype(f32)
        for tap in range(9):
            moved[index, tap * chan : (tap + 1) * chan] = shifted(
                cells, tap // 3 - 1, tap % 3 - 1, side
            ).astype(bf16)
    both = grad_hidden[...]
    outer0 = lax.dot_general(moved[0], both[:width], transposed, preferred_element_type=f32)
    inner0 = lax.dot_general(inner[0], both, transposed, preferred_element_type=f32)
    inner1 = lax.dot_general(inner[1], both, transposed, preferred_element_type=f32)
    outer1 = lax.dot_general(moved[1], both[width:], transposed, preferred_element_type=f32)
    tall = 9 * chan
    sums[:tall] = outer0 + inner0[:, width:]
    sums[tall : 2 * tall] = inner0[:, :width] + inner1[:, width:]
    sums[2 * tall : 3 * tall] = inner1[:, :width] + outer1
    sums[3 * tall :] = jnp.zeros((sums.shape[0] - 3 * tall, width), f32)
    me = lax.axis_index("dp")
    rows = keep[0].shape[0]
    for k in range(plan.samples):
        part = sums[pl.ds(pl.multiple_of((me ^ k) * rows, rows), rows)]
        if k % 2:
            send[k // 2][...] = part.astype(bf16)
        else:
            keep[k // 2][...] = part


def halve_kernel(*refs):
    count = len(refs) // 3
    mine, got, out = refs[:count], refs[count : 2 * count], refs[2 * count :]
    for k in range(count):
        total = mine[k][...] + got[k][...].astype(f32)
        out[k // 2 + k % 2 * (count // 2)][...] = total.astype(out[k // 2 + k % 2 * (count // 2)].dtype)


def tap_parts(products):
    chan = products.shape[0] // 9

    def part(b, c):
        tap = 3 * b + c
        return products[tap * chan : (tap + 1) * chan]

    return part


def edges_kernel(side, weight, grad_hidden, even_pairs, odd_pairs, products):
    width = weight.shape[1]
    tall = weight.shape[0] // 3
    both = grad_hidden[...]
    products[...] = jnp.dot(weight[:tall], both[:width], preferred_element_type=f32)
    to_before = gathered(tap_parts(products), side).astype(bf16)
    products[...] = jnp.dot(weight[2 * tall :], both[width:], preferred_element_type=f32)
    to_after = gathered(tap_parts(products), side).astype(bf16)
    even_pairs[...], odd_pairs[...] = for_sides(to_before, to_after)


def own_kernel(side, weight, grad_hidden, own, products):
    tall = weight.shape[0] // 3
    both = grad_hidden[...]
    for plane in range(2):
        mixed = jnp.concatenate(
            [weight[(plane + 1) * tall : (plane + 2) * tall], weight[plane * tall : (plane + 1) * tall]], 1
        )
        products[...] = jnp.dot(mixed, both, preferred_element_type=f32)
        own[plane] = gathered(tap_parts(products), side)


def swapped(part, axis, distance):
    return lax.ppermute(part, axis, [(i, i ^ distance) for i in range(lax.axis_size(axis))])


def per_device(layer_input, hidden_pre, output_pre, output_grad, weight_a, weight_b):
    side = math.isqrt(layer_input.shape[3])
    half = side // 2
    size, small = side * side, half * half
    depth_a = layer_input.shape[2]
    samples, slabs = lax.axis_size("dp"), lax.axis_size("space")
    even = [(i, i ^ 1) for i in range(slabs)]
    odd = [(i, ((i + 1 ^ 1) - 1) % slabs) for i in range(slabs)]
    shape = jax.ShapeDtypeStruct
    outer = output_pre[0, :, 0].astype(f32)
    grad = (output_grad[0, :, 0].astype(f32) * jnp.where(outer > 0, 1.0, negative_slope)).astype(bf16)
    grad, layer_input, hidden_pre = lax.optimization_barrier((grad, layer_input, hidden_pre))
    grad_sides = [lax.ppermute(grad, "space", pairs) for pairs in (even, odd)]
    source = layer_input[0].transpose(1, 0, 2)
    hidden = hidden_pre[0].transpose(1, 0, 2)
    chan = source.shape[1]
    width_a = hidden.shape[1]
    width_b = grad.shape[0]
    plan = Plan(samples, slabs, chan, width_a, width_b)
    pooled, matrix = call(
        lambda *refs: pool_kernel(side, *refs),
        [shape((width_a, small), bf16), shape((size, small), bf16)],
        [],
        1 << 28,
        hidden,
    )
    source, pooled = lax.optimization_barrier((source, pooled))
    edge_planes, source = lax.optimization_barrier((for_sides(source[0], source[1]), source))
    source_sides = [lax.ppermute(part, "space", pairs) for part, pairs in zip(edge_planes, (even, odd))]
    inner = call(
        lambda *refs: taps_kernel(side, *refs), shape((2, 9 * chan, size), bf16), [], 1 << 20, source
    )
    grad_sides, inner = lax.optimization_barrier((grad_sides, inner))
    channels = 3 * plan.share
    heights = [channels + (plan.width if k == 1 or k % 2 == 0 else 0) for k in range(samples)]
    packed = call(
        lambda *refs: pack_kernel(plan, *refs),
        [shape((height, small), bf16) for height in heights] + [shape(grad.shape, bf16)] * 2,
        [],
        1 << 20,
        pooled,
        grad,
        *grad_sides,
    )
    packed, (before, after) = packed[:-2], packed[-2:]
    crossed = [swapped(packed[k], "dp", k // 2 * 2) for k in range(2, samples)]
    core_b = swapped(packed[1], "dp", 1)
    grad_hidden = call(
        lambda *refs: hidden_kernel(side, *refs),
        shape((2 * width_a, size), bf16),
        [pltpu.VMEM((9 * width_a, small), f32)],
        1 << 30,
        weight_b.reshape(27 * width_a, width_b),
        grad,
        before,
        after,
        hidden,
        matrix,
    )
    edges = call(
        lambda *refs: edges_kernel(side, *refs),
        [shape((chan, size), bf16)] * 2,
        [pltpu.VMEM((9 * chan, size), f32)],
        1 << 28,
        weight_a.reshape(27 * chan, width_a),
        grad_hidden,
    )
    edges, source_sides = lax.optimization_barrier((edges, source_sides))
    halves = call(
        lambda *refs: sums_a_kernel(side, plan, *refs),
        [shape((plan.rows_a * slabs, width_a), kind) for kind in (f32, bf16) for _ in range(samples // 2)],
        [
            pltpu.VMEM((2, 9 * chan, size), bf16),
            pltpu.VMEM((plan.rows_a * samples * slabs, width_a), f32),
        ],
        1 << 30,
        grad_hidden,
        inner,
        *source_sides,
    )
    keep, send = halves[: samples // 2], halves[samples // 2 :]
    got_a = [swapped(part, "dp", 1) for part in send]
    for stride in [1 << k for k in range(1, samples.bit_length() - 1)]:
        count = len(keep) // 2
        halves = call(
            halve_kernel,
            [shape(keep[0].shape, kind) for kind in (f32, bf16) for _ in range(count)],
            [],
            1 << 20,
            *keep,
            *got_a,
        )
        keep, send = halves[:count], halves[count:]
        got_a = [swapped(part, "dp", stride) for part in send]
    crossed, keep = lax.optimization_barrier((crossed, keep))
    pooled_parts, channel_parts = [packed[0], core_b], [packed[0], core_b]
    for first, second in zip(crossed[::2], crossed[1::2]):
        pooled_parts += [first, swapped(first[: plan.width], "dp", 1)]
        channel_parts += [first, swapped(second, "dp", 1)]
    totals = call(
        lambda *refs: share_kernel(plan, *refs),
        shape((slabs, plan.rows_b, 128), f32),
        [
            pltpu.VMEM((9 * width_a, samples * small), bf16),
            pltpu.VMEM((slabs * plan.rows_b, 128), f32),
        ],
        1 << 30,
        *pooled_parts,
        *channel_parts,
    )
    from_odd = lax.ppermute(edges[1], "space", odd)
    far = plan.far
    totals, from_odd = lax.optimization_barrier((totals, from_odd))
    blocks = call(
        lambda *refs: blocks_kernel(plan, *refs),
        [shape((2, plan.block, 128), bf16)] * far,
        [pltpu.VMEM((plan.rows_a * slabs, 128), f32)],
        1 << 20,
        totals,
        keep[0],
        got_a[0],
    )
    parts = blocks[:1] + [swapped(blocks[k], "space", k) for k in range(1, far)]
    own = call(
        lambda *refs: own_kernel(side, *refs),
        shape((2, chan, size), f32),
        [pltpu.VMEM((9 * chan, size), f32)],
        1 << 28,
        weight_a.reshape(27 * chan, width_a),
        grad_hidden,
    )
    parts, own = lax.optimization_barrier((parts, own))
    both = call(near_kernel, shape((2, plan.block, 128), bf16), [], 1 << 20, *parts)
    there = swapped(both, "space", far)
    both, even_edge = lax.optimization_barrier((both, edges[0]))
    from_even = lax.ppermute(even_edge, "space", even)
    there, from_even = lax.optimization_barrier((there, from_even))
    input_grad = own + jnp.stack(sides(from_even, from_odd)).astype(f32)
    input_grad = input_grad.astype(bf16).transpose(1, 0, 2)[None]
    pair, low = call(
        lambda *refs: far_kernel(plan, *refs),
        [shape((2, rows, 128), bf16) for rows in (plan.block, plan.low)],
        [],
        1 << 20,
        both,
        there,
    )
    strides = [samples >> k for k in range(1, samples.bit_length())]

    def stacked(parts):
        rows = sum(part.shape[0] for part in parts)
        return call(stack_kernel, shape((rows, *parts[0].shape[1:]), bf16), [], 1 << 20, *parts)

    hop = swapped(pair, "dp", strides[0])
    near = [swapped(low, "space", k) for k in range(1, far)]
    pair, hop, near = lax.optimization_barrier((pair, hop, near))
    lows = stacked(near)
    rows = 4 * plan.block + (slabs - 2) * plan.low
    flat = call(flat_kernel, shape((rows, 128), bf16), [], 1 << 20, pair, hop, *near)
    first = [swapped(flat, "dp", stride) for stride in strides[1:]]
    high = call(
        lambda *refs: high_kernel(plan, *refs),
        shape((4, plan.block - plan.low, 128), bf16),
        [],
        1 << 20,
        pair,
        hop,
    )
    lows_hop = swapped(lows, "dp", strides[0])
    highs = [swapped(high, "space", k) for k in range(1, far)]
    lows_hop, highs, first, input_grad = lax.optimization_barrier((lows_hop, highs, first, input_grad))
    known = {0: [flat, lows_hop, *highs]}
    for stride, part in zip(strides[1:], first):
        for k in list(known):
            done = [] if k else [part]
            known[k ^ stride] = done + [swapped(part, "dp", stride) for part in known[k][len(done) :]]
    shares = [known[k] for k in sorted(known)]
    planes_a = depth_a * slabs
    total_a, total_b = call(
        lambda *refs: last_kernel(
            plan,
            1.0 / math.sqrt(samples * planes_a * size),
            1.0 / math.sqrt(samples * (planes_a // 2) * small),
            *refs,
        ),
        [shape((27 * chan, width_a), f32), shape((27 * width_a, width_b), f32)],
        [
            pltpu.VMEM((samples, slabs, plan.block, 128), bf16),
            pltpu.VMEM((27 * chan, width_a), f32),
            pltpu.VMEM((27 * width_a, width_b), f32),
            pltpu.SemaphoreType.DMA((4,)),
        ],
        1 << 20,
        *[part for parts in shares for part in parts],
        out_specs=[pl.BlockSpec(memory_space=pl.ANY)] * 2,
    )
    return (input_grad, total_a.reshape(weight_a.shape), total_b.reshape(weight_b.shape))


def solution(mesh):
    in_specs = (
        P("dp", None, "space", None),
        P("dp", None, "space", None),
        P("dp", None, "space", None),
        P("dp", None, "space", None),
        P(),
        P(),
    )
    out_specs = (P("dp", None, "space", None), P(), P())
    return jax.shard_map(
        per_device, mesh=mesh, in_specs=in_specs, out_specs=out_specs, check_vma=False
    )
```

```python
import math

import jax
import jax.numpy as jnp
from jax import lax
from jax.experimental import pallas as pl
from jax.experimental.pallas import tpu as pltpu
from jax.sharding import PartitionSpec as P

negative_slope = 0.3
f32 = jnp.float32
bf16 = jnp.bfloat16
vmem = pl.BlockSpec(memory_space=pltpu.VMEM)
transposed = (((1,), (1,)), ((), ()))


def shifted(cells, rows, columns, side):
    size = side * side
    offset = rows * side + columns
    if offset:
        cells = pltpu.roll(cells, (-offset) % size, 1)
    place = lax.broadcasted_iota(jnp.int32, cells.shape, 1)
    if rows:
        y = place // side + rows
        cells = jnp.where((y >= 0) & (y < side), cells, 0.0)
    if columns:
        x = place % side + columns
        cells = jnp.where((x >= 0) & (x < side), cells, 0.0)
    return cells


def gathered(parts, side):
    total = None
    for c in range(3):
        line = parts(1, c) + shifted(parts(0, c), 1, 0, side) + shifted(parts(2, c), -1, 0, side)
        line = shifted(line, 0, 1 - c, side)
        total = line if total is None else total + line
    return total


def pool_matrix(side):
    half = side // 2
    fine = lax.broadcasted_iota(jnp.int32, (side * side, half * half), 0)
    coarse = lax.broadcasted_iota(jnp.int32, (side * side, half * half), 1)
    parent = (fine // (2 * side)) * half + (fine % side) // 2
    return jnp.where(parent == coarse, 0.125, 0.0).astype(bf16)


def sides(even_pairs, odd_pairs):
    here = lax.axis_index("space")
    even = here % 2 == 0
    nothing = jnp.zeros(even_pairs.shape, bf16)
    before = jnp.where(here == 0, nothing, jnp.where(even, odd_pairs, even_pairs))
    after = jnp.where(here == lax.axis_size("space") - 1, nothing, jnp.where(even, even_pairs, odd_pairs))
    return before, after


def for_sides(before, after):
    even = lax.axis_index("space") % 2 == 0
    return jnp.where(even, after, before), jnp.where(even, before, after)


def call(kernel, out_shape, scratch, flops, *args, out_specs=None):
    result = pl.pallas_call(
        kernel,
        out_shape=out_shape,
        in_specs=[vmem] * len(args),
        out_specs=out_specs or jax.tree.map(lambda _: vmem, out_shape),
        scratch_shapes=scratch,
        compiler_params=pltpu.CompilerParams(vmem_limit_bytes=48 * 1024 * 1024),
        cost_estimate=pl.CostEstimate(flops=flops >> 12, bytes_accessed=1 << 10, transcendentals=0),
    )(*args)
    return list(result) if isinstance(out_shape, list) else result


def pool_kernel(side, hidden, pooled, matrix):
    width = hidden.shape[1]
    pool = pool_matrix(side)
    matrix[...] = pool
    total = None
    for plane in range(2):
        cells = hidden[plane].astype(f32)
        stacked = jnp.concatenate([jnp.maximum(cells, 0.0), jnp.minimum(cells, 0.0)], 0).astype(bf16)
        part = jnp.dot(stacked, pool, preferred_element_type=f32)
        total = part if total is None else total + part
    pooled[...] = (total[:width] + negative_slope * total[width:]).astype(bf16)


def pack_kernel(plan, pooled, grad, even_pairs, odd_pairs, *refs):
    me = lax.axis_index("dp")
    messages, (before, after) = refs[:-2], refs[-2:]
    before[...], after[...] = sides(even_pairs[...], odd_pairs[...])
    for distance, message in enumerate(messages):
        row = message.shape[0] - 3 * plan.share
        if row:
            message[:row] = pooled[...]
        start = pl.multiple_of((me ^ distance) * plan.share, plan.share)
        for a, plane in enumerate((after, grad, before)):
            message[row + a * plan.share : row + (a + 1) * plan.share] = plane[pl.ds(start, plan.share)]


def share_kernel(plan, *refs):
    pooled, channels, (out, moved, totals) = refs[: plan.samples], refs[plan.samples : -3], refs[-3:]
    size = pooled[0].shape[1]
    half = math.isqrt(size)
    width, share = plan.width, plan.share
    for k, message in enumerate(pooled):
        cells = message[:width]
        cells = cells.astype(f32)
        for tap in range(9):
            moved[tap * width : (tap + 1) * width, k * size : (k + 1) * size] = shifted(
                cells, tap // 3 - 1, tap % 3 - 1, half
            ).astype(bf16)
    right = jnp.concatenate([message[message.shape[0] - 3 * share :] for message in channels], 1)
    result = lax.dot_general(moved[...], right, transposed, preferred_element_type=f32)
    for a in range(3):
        pieces = [
            result[k * plan.tall : (k + 1) * plan.tall, a * share : (a + 1) * share] for k in range(plan.pieces)
        ]
        totals[a * plan.tall : (a + 1) * plan.tall] = jnp.concatenate(pieces, 1)
    spare = totals.shape[0] - 3 * plan.tall
    if spare:
        totals[3 * plan.tall :] = jnp.zeros((spare, 128), f32)
    for slab in range(plan.slabs):
        out[slab] = totals[slab * plan.rows_b : (slab + 1) * plan.rows_b]


def blocks_kernel(plan, totals, *refs):
    mine, got, *blocks, first = refs
    first[...] = mine[...] + got[...].astype(f32)
    me = lax.axis_index("space")
    for distance, block in enumerate(blocks):
        for k in range(2):
            slab = me ^ distance ^ (k * plan.far)
            row = pl.multiple_of(slab * plan.rows_a, plan.rows_a)
            parts = [totals[slab], first[pl.ds(row, plan.rows_a)]]
            spare = plan.block - plan.rows_b - plan.rows_a
            if spare:
                parts.append(jnp.zeros((spare, 128), f32))
            block[k] = jnp.concatenate(parts, 0).astype(bf16)


def near_kernel(*refs):
    total = refs[0][...].astype(f32)
    for part in refs[1:-1]:
        total += part[...].astype(f32)
    refs[-1][...] = total.astype(bf16)


def far_kernel(plan, here, there, pair, low):
    for k in range(2):
        pair[k] = (here[k].astype(f32) + there[1 - k].astype(f32)).astype(bf16)
        low[k] = pair[k, : plan.low]


def flat_kernel(*refs):
    row = 0
    for part in refs[:-1]:
        for k in range(part.shape[0]):
            refs[-1][row : row + part.shape[1]] = part[k]
            row += part.shape[1]


def high_kernel(plan, pair, hop, high):
    for k in range(2):
        high[k], high[2 + k] = pair[k, plan.low :], hop[k, plan.low :]


def stack_kernel(*refs):
    count = refs[0].shape[0]
    for k, part in enumerate(refs[:-1]):
        refs[-1][count * k : count * (k + 1)] = part[...]


def last_kernel(plan, scale_a, scale_b, *refs):
    got, (out_a, out_b, shares, rows_a, rows, sems) = refs[:-6], refs[-6:]
    me, here = lax.axis_index("dp"), lax.axis_index("space")
    far, groups = plan.far, plan.samples // 2
    each = len(got) // groups
    for group in range(groups):
        flat, lows_hop, *highs = got[group * each : (group + 1) * each]
        for hop in range(2):
            sample = me ^ group ^ (hop * groups)
            for k in range(plan.slabs):
                slab = here ^ (k // 2) ^ (k % 2 * far)
                if k < 2:
                    row = (2 * hop + k) * plan.block
                    shares[sample, slab] = flat[row : row + plan.block]
                else:
                    row = 4 * plan.block + (k - 2) * plan.low
                    shares[sample, slab, : plan.low] = lows_hop[k - 2] if hop else flat[row : row + plan.low]
                    shares[sample, slab, plan.low :] = highs[k // 2 - 1][2 * hop + k % 2]
    for sample in range(plan.samples):
        for slab in range(plan.slabs):
            row = (sample * plan.slabs + slab) * plan.rows_a
            height = min(plan.rows_a, out_a.shape[0] - row)
            if height > 0:
                base = plan.rows_b // 16 * 16
                block = shares[sample, slab, base:].astype(f32)[plan.rows_b - base :]
                rows_a[row : row + height] = block[:height] * scale_a
    copy_a = pltpu.make_async_copy(rows_a, out_a, sems.at[3])
    copy_a.start()
    copies = []
    for slab in range(plan.slabs):
        blocks = [shares[sample, slab].astype(f32) for sample in range(plan.samples)]
        for k in range(plan.pieces):
            lanes = slice(k * plan.share, (k + 1) * plan.share)
            wide = jnp.concatenate([block[: plan.rows_b, lanes] for block in blocks], 1) * scale_b
            start, stop = slab * plan.rows_b, min((slab + 1) * plan.rows_b, 3 * plan.tall)
            while start < stop:
                a = start // plan.tall
                end = min(stop, (a + 1) * plan.tall)
                row = (a * (plan.pieces - 1) + k) * plan.tall + start
                rows[row : row + end - start] = wide[start - slab * plan.rows_b : end - slab * plan.rows_b]
                start = end
        height = plan.pieces * plan.tall
        while len(copies) < 3 and (slab + 1) * plan.rows_b >= (len(copies) + 1) * plan.tall:
            place = pl.ds(len(copies) * height, height)
            copies.append(pltpu.make_async_copy(rows.at[place], out_b.at[place], sems.at[len(copies)]))
            copies[-1].start()
    for copy in (copy_a, *copies):
        copy.wait()


class Plan:
    def __init__(self, samples, slabs, chan, width, width_b):
        self.samples, self.slabs, self.width = samples, slabs, width
        self.share = width_b // samples
        self.pieces = 128 // self.share
        self.tall = 9 * width // self.pieces
        self.rows_b = -(-3 * self.tall // (8 * slabs)) * 8
        self.rows_a = -(-27 * chan // (8 * samples * slabs)) * 8
        self.block = -(-(self.rows_b + self.rows_a) // 16) * 16
        self.low = -(-self.block * 11 // 256) * 16
        self.far = slabs // 2


def hidden_kernel(side, weight, grad, before, after, hidden, matrix, grad_hidden, products):
    half = side // 2
    width = hidden.shape[1]
    block = 9 * width
    taps = jnp.concatenate([weight[a * block : (a + 1) * block] for a in range(3)], 1)
    planes = jnp.concatenate([after[...], grad[...], before[...]], 0)
    products[...] = jnp.dot(taps, planes, preferred_element_type=f32)

    def part(b, c):
        tap = 3 * b + c
        return products[tap * width : (tap + 1) * width]

    back = gathered(part, half)
    high = back.astype(bf16)
    low = (back - high.astype(f32)).astype(bf16)
    pool = matrix[...]
    spread = lax.dot_general(high, pool, transposed, preferred_element_type=f32)
    spread += lax.dot_general(low, pool, transposed, preferred_element_type=f32)
    for plane in range(2):
        slope = jnp.where(hidden[plane].astype(f32) > 0, 1.0, negative_slope)
        grad_hidden[plane * width : (plane + 1) * width] = (spread * slope).astype(bf16)


def taps_kernel(side, source, moved):
    chan = source.shape[1]
    for plane in range(2):
        cells = source[plane].astype(f32)
        for tap in range(9):
            moved[plane, tap * chan : (tap + 1) * chan] = shifted(
                cells, tap // 3 - 1, tap % 3 - 1, side
            ).astype(bf16)


def sums_a_kernel(side, plan, grad_hidden, inner, even_pairs, odd_pairs, *refs):
    half = plan.samples // 2
    keep, send, (moved, sums) = refs[:half], refs[half:-2], refs[-2:]
    width = plan.width
    chan = even_pairs.shape[0]
    before, after = sides(even_pairs[...], odd_pairs[...])
    for index, plane in enumerate((before, after)):
        cells = plane.astype(f32)
        for tap in range(9):
            moved[index, tap * chan : (tap + 1) * chan] = shifted(
                cells, tap // 3 - 1, tap % 3 - 1, side
            ).astype(bf16)
    both = grad_hidden[...]
    outer0 = lax.dot_general(moved[0], both[:width], transposed, preferred_element_type=f32)
    inner0 = lax.dot_general(inner[0], both, transposed, preferred_element_type=f32)
    inner1 = lax.dot_general(inner[1], both, transposed, preferred_element_type=f32)
    outer1 = lax.dot_general(moved[1], both[width:], transposed, preferred_element_type=f32)
    tall = 9 * chan
    sums[:tall] = outer0 + inner0[:, width:]
    sums[tall : 2 * tall] = inner0[:, :width] + inner1[:, width:]
    sums[2 * tall : 3 * tall] = inner1[:, :width] + outer1
    sums[3 * tall :] = jnp.zeros((sums.shape[0] - 3 * tall, width), f32)
    me = lax.axis_index("dp")
    rows = keep[0].shape[0]
    for k in range(plan.samples):
        part = sums[pl.ds(pl.multiple_of((me ^ k) * rows, rows), rows)]
        if k % 2:
            send[k // 2][...] = part.astype(bf16)
        else:
            keep[k // 2][...] = part


def halve_kernel(*refs):
    count = len(refs) // 3
    mine, got, out = refs[:count], refs[count : 2 * count], refs[2 * count :]
    for k in range(count):
        total = mine[k][...] + got[k][...].astype(f32)
        out[k // 2 + k % 2 * (count // 2)][...] = total.astype(out[k // 2 + k % 2 * (count // 2)].dtype)


def tap_parts(products):
    chan = products.shape[0] // 9

    def part(b, c):
        tap = 3 * b + c
        return products[tap * chan : (tap + 1) * chan]

    return part


def edges_kernel(side, weight, grad_hidden, even_pairs, odd_pairs, products):
    width = weight.shape[1]
    tall = weight.shape[0] // 3
    both = grad_hidden[...]
    products[...] = jnp.dot(weight[:tall], both[:width], preferred_element_type=f32)
    to_before = gathered(tap_parts(products), side).astype(bf16)
    products[...] = jnp.dot(weight[2 * tall :], both[width:], preferred_element_type=f32)
    to_after = gathered(tap_parts(products), side).astype(bf16)
    even_pairs[...], odd_pairs[...] = for_sides(to_before, to_after)


def own_kernel(side, weight, grad_hidden, own, products):
    tall = weight.shape[0] // 3
    both = grad_hidden[...]
    for plane in range(2):
        mixed = jnp.concatenate(
            [weight[(plane + 1) * tall : (plane + 2) * tall], weight[plane * tall : (plane + 1) * tall]], 1
        )
        products[...] = jnp.dot(mixed, both, preferred_element_type=f32)
        own[plane] = gathered(tap_parts(products), side)


def swapped(part, axis, distance):
    return lax.ppermute(part, axis, [(i, i ^ distance) for i in range(lax.axis_size(axis))])


def per_device(layer_input, hidden_pre, output_pre, output_grad, weight_a, weight_b):
    side = math.isqrt(layer_input.shape[3])
    half = side // 2
    size, small = side * side, half * half
    depth_a = layer_input.shape[2]
    samples, slabs = lax.axis_size("dp"), lax.axis_size("space")
    even = [(i, i ^ 1) for i in range(slabs)]
    odd = [(i, ((i + 1 ^ 1) - 1) % slabs) for i in range(slabs)]
    shape = jax.ShapeDtypeStruct
    outer = output_pre[0, :, 0].astype(f32)
    grad = (output_grad[0, :, 0].astype(f32) * jnp.where(outer > 0, 1.0, negative_slope)).astype(bf16)
    grad, layer_input, hidden_pre = lax.optimization_barrier((grad, layer_input, hidden_pre))
    grad_sides = [lax.ppermute(grad, "space", pairs) for pairs in (even, odd)]
    source = layer_input[0].transpose(1, 0, 2)
    hidden = hidden_pre[0].transpose(1, 0, 2)
    chan = source.shape[1]
    width_a = hidden.shape[1]
    width_b = grad.shape[0]
    plan = Plan(samples, slabs, chan, width_a, width_b)
    pooled, matrix = call(
        lambda *refs: pool_kernel(side, *refs),
        [shape((width_a, small), bf16), shape((size, small), bf16)],
        [],
        1 << 28,
        hidden,
    )
    source, pooled = lax.optimization_barrier((source, pooled))
    edge_planes, source = lax.optimization_barrier((for_sides(source[0], source[1]), source))
    source_sides = [lax.ppermute(part, "space", pairs) for part, pairs in zip(edge_planes, (even, odd))]
    inner = call(
        lambda *refs: taps_kernel(side, *refs), shape((2, 9 * chan, size), bf16), [], 1 << 20, source
    )
    grad_sides, inner = lax.optimization_barrier((grad_sides, inner))
    channels = 3 * plan.share
    heights = [channels + (plan.width if k == 1 or k % 2 == 0 else 0) for k in range(samples)]
    packed = call(
        lambda *refs: pack_kernel(plan, *refs),
        [shape((height, small), bf16) for height in heights] + [shape(grad.shape, bf16)] * 2,
        [],
        1 << 20,
        pooled,
        grad,
        *grad_sides,
    )
    packed, (before, after) = packed[:-2], packed[-2:]
    crossed = [swapped(packed[k], "dp", k // 2 * 2) for k in range(2, samples)]
    core_b = swapped(packed[1], "dp", 1)
    grad_hidden = call(
        lambda *refs: hidden_kernel(side, *refs),
        shape((2 * width_a, size), bf16),
        [pltpu.VMEM((9 * width_a, small), f32)],
        1 << 30,
        weight_b.reshape(27 * width_a, width_b),
        grad,
        before,
        after,
        hidden,
        matrix,
    )
    edges = call(
        lambda *refs: edges_kernel(side, *refs),
        [shape((chan, size), bf16)] * 2,
        [pltpu.VMEM((9 * chan, size), f32)],
        1 << 28,
        weight_a.reshape(27 * chan, width_a),
        grad_hidden,
    )
    edges, source_sides = lax.optimization_barrier((edges, source_sides))
    halves = call(
        lambda *refs: sums_a_kernel(side, plan, *refs),
        [shape((plan.rows_a * slabs, width_a), kind) for kind in (f32, bf16) for _ in range(samples // 2)],
        [
            pltpu.VMEM((2, 9 * chan, size), bf16),
            pltpu.VMEM((plan.rows_a * samples * slabs, width_a), f32),
        ],
        1 << 30,
        grad_hidden,
        inner,
        *source_sides,
    )
    keep, send = halves[: samples // 2], halves[samples // 2 :]
    got_a = [swapped(part, "dp", 1) for part in send]
    for stride in [1 << k for k in range(1, samples.bit_length() - 1)]:
        count = len(keep) // 2
        halves = call(
            halve_kernel,
            [shape(keep[0].shape, kind) for kind in (f32, bf16) for _ in range(count)],
            [],
            1 << 20,
            *keep,
            *got_a,
        )
        keep, send = halves[:count], halves[count:]
        got_a = [swapped(part, "dp", stride) for part in send]
    crossed, keep = lax.optimization_barrier((crossed, keep))
    pooled_parts, channel_parts = [packed[0], core_b], [packed[0], core_b]
    for first, second in zip(crossed[::2], crossed[1::2]):
        pooled_parts += [first, swapped(first[: plan.width], "dp", 1)]
        channel_parts += [first, swapped(second, "dp", 1)]
    totals = call(
        lambda *refs: share_kernel(plan, *refs),
        shape((slabs, plan.rows_b, 128), f32),
        [
            pltpu.VMEM((9 * width_a, samples * small), bf16),
            pltpu.VMEM((slabs * plan.rows_b, 128), f32),
        ],
        1 << 30,
        *pooled_parts,
        *channel_parts,
    )
    inside = [(i, k) if abs(i - k) == 1 else (i, i) for i, k in odd]
    from_odd = lax.ppermute(edges[1], "space", inside)
    far = plan.far
    totals, from_odd = lax.optimization_barrier((totals, from_odd))
    blocks = call(
        lambda *refs: blocks_kernel(plan, *refs),
        [shape((2, plan.block, 128), bf16)] * far,
        [pltpu.VMEM((plan.rows_a * slabs, 128), f32)],
        1 << 20,
        totals,
        keep[0],
        got_a[0],
    )
    parts = blocks[:1] + [swapped(blocks[k], "space", k) for k in range(1, far)]
    own = call(
        lambda *refs: own_kernel(side, *refs),
        shape((2, chan, size), f32),
        [pltpu.VMEM((9 * chan, size), f32)],
        1 << 28,
        weight_a.reshape(27 * chan, width_a),
        grad_hidden,
    )
    parts, own = lax.optimization_barrier((parts, own))
    both = call(near_kernel, shape((2, plan.block, 128), bf16), [], 1 << 20, *parts)
    there = swapped(both, "space", far)
    both, even_edge = lax.optimization_barrier((both, edges[0]))
    from_even = lax.ppermute(even_edge, "space", even)
    there, from_even = lax.optimization_barrier((there, from_even))
    input_grad = own + jnp.stack(sides(from_even, from_odd)).astype(f32)
    input_grad = input_grad.astype(bf16).transpose(1, 0, 2)[None]
    pair, low = call(
        lambda *refs: far_kernel(plan, *refs),
        [shape((2, rows, 128), bf16) for rows in (plan.block, plan.low)],
        [],
        1 << 20,
        both,
        there,
    )
    strides = [samples >> k for k in range(1, samples.bit_length())]

    def stacked(parts):
        rows = sum(part.shape[0] for part in parts)
        return call(stack_kernel, shape((rows, *parts[0].shape[1:]), bf16), [], 1 << 20, *parts)

    hop = swapped(pair, "dp", strides[0])
    near = [swapped(low, "space", k) for k in range(1, far)]
    pair, hop, near = lax.optimization_barrier((pair, hop, near))
    lows = stacked(near)
    rows = 4 * plan.block + (slabs - 2) * plan.low
    flat = call(flat_kernel, shape((rows, 128), bf16), [], 1 << 20, pair, hop, *near)
    first = [swapped(flat, "dp", stride) for stride in strides[1:]]
    high = call(
        lambda *refs: high_kernel(plan, *refs),
        shape((4, plan.block - plan.low, 128), bf16),
        [],
        1 << 20,
        pair,
        hop,
    )
    lows_hop = swapped(lows, "dp", strides[0])
    highs = [swapped(high, "space", k) for k in range(1, far)]
    lows_hop, highs, first, input_grad = lax.optimization_barrier((lows_hop, highs, first, input_grad))
    known = {0: [flat, lows_hop, *highs]}
    for stride, part in zip(strides[1:], first):
        for k in list(known):
            done = [] if k else [part]
            known[k ^ stride] = done + [swapped(part, "dp", stride) for part in known[k][len(done) :]]
    shares = [known[k] for k in sorted(known)]
    planes_a = depth_a * slabs
    total_a, total_b = call(
        lambda *refs: last_kernel(
            plan,
            1.0 / math.sqrt(samples * planes_a * size),
            1.0 / math.sqrt(samples * (planes_a // 2) * small),
            *refs,
        ),
        [shape((27 * chan, width_a), f32), shape((27 * width_a, width_b), f32)],
        [
            pltpu.VMEM((samples, slabs, plan.block, 128), bf16),
            pltpu.VMEM((27 * chan, width_a), f32),
            pltpu.VMEM((27 * width_a, width_b), f32),
            pltpu.SemaphoreType.DMA((4,)),
        ],
        1 << 20,
        *[part for parts in shares for part in parts],
        out_specs=[pl.BlockSpec(memory_space=pl.ANY)] * 2,
    )
    return (input_grad, total_a.reshape(weight_a.shape), total_b.reshape(weight_b.shape))


def solution(mesh):
    in_specs = (
        P("dp", None, "space", None),
        P("dp", None, "space", None),
        P("dp", None, "space", None),
        P("dp", None, "space", None),
        P(),
        P(),
    )
    out_specs = (P("dp", None, "space", None), P(), P())
    return jax.shard_map(
        per_device, mesh=mesh, in_specs=in_specs, out_specs=out_specs, check_vma=False
    )
```
